128 devices in a mesh: rows: 16 (over y_lo, x, core), cols: 8 (over z, y_hi).
Axes of the slice: x: 4, y: 4 (y_hi: 2, y_lo: 2; y = y_hi * 2 + y_lo), z: 4, core: 2. Of those that a mesh axis runs over, the one named last changes fastest.
Arguments:
- image: bfloat16 [256, 512, 384], P('rows', 'cols'), may hold values from -14 to 14
- mb_expand: bfloat16 [384, 1536], replicated, may hold values from -0.3125 to 0.3125
- mb_taps: bfloat16 [9, 1536], replicated, may hold values from -3.5 to 3.5
- mb_reduce: bfloat16 [1536, 96], replicated, may hold values from -2.5 to 2.5
- mb_restore: bfloat16 [96, 1536], replicated, may hold values from -3.5 to 3.5
- mb_project: bfloat16 [1536, 384], replicated, may hold values from -0.15625 to 0.15625
- block_qkv: bfloat16 [384, 1152], replicated, may hold values from -2 to 2
- block_out: bfloat16 [384, 384], replicated, may hold values from -0.3125 to 0.3125
- first_up: bfloat16 [384, 1536], replicated, may hold values from -0.3125 to 0.3125
- first_down: bfloat16 [1536, 384], replicated, may hold values from -0.15625 to 0.15625
- grid_qkv: bfloat16 [384, 1152], replicated, may hold values from -2 to 2
- grid_out: bfloat16 [384, 384], replicated, may hold values from -0.3125 to 0.3125
- second_up: bfloat16 [384, 1536], replicated, may hold values from -0.3125 to 0.3125
- second_down: bfloat16 [1536, 384], replicated, may hold values from -0.15625 to 0.15625
- down_expand: bfloat16 [384, 1536], replicated, may hold values from -0.3125 to 0.3125
- down_taps: bfloat16 [9, 1536], replicated, may hold values from -3.5 to 3.5
- down_reduce: bfloat16 [1536, 96], replicated, may hold values from -2.5 to 2.5
- down_restore: bfloat16 [96, 1536], replicated, may hold values from -3.5 to 3.5
- down_project: bfloat16 [1536, 768], replicated, may hold values from -0.15625 to 0.15625
- down_shortcut: bfloat16 [384, 768], replicated, may hold values from -0.15625 to 0.15625
Outputs:
- section_out: bfloat16 [256, 512, 384], P('rows', 'cols')
- downsampled: bfloat16 [128, 256, 768], P('rows', 'cols')
The draws below stay inside these ranges and needn't reach their ends.
All inputs are finite; a program needn't handle non-finite values.
Results may differ from the reference program's by a relative error of at most 0.014.
Values may be sent and summed in bfloat16 or wider, within the bound.
No kernel may reach another device: no remote copies, remote signals or barrier semaphores. Data moves between devices by JAX's collectives and lax.ppermute only.
A program may use at most 128 MiB of HBM per device.

```python
import math
import jax
import jax.numpy as jnp
from jax import lax

D = 384
HEADS = 12
FF = 1536
SE_D = 96
OUT_D = 768
WIN = 8
HEIGHT = 256
WIDTH = 512


def draw_image(key, part):
    key = jax.random.fold_in(key, 11)
    key_rough, key_pattern, key_scaling = jax.random.split(key, 3)
    row_pos = jnp.arange(HEIGHT, dtype=jnp.float32)[:, None, None] / HEIGHT
    pattern = jax.random.uniform(key_pattern, (1, 1, D), jnp.float32, -2.0, 2.0)
    rough = jnp.clip(jax.random.normal(key_rough, (HEIGHT, WIDTH, D), jnp.float32), -5.0, 5.0)
    scaling = jax.random.uniform(key_scaling, (HEIGHT, WIDTH, 1), jnp.float32, 0.5, 1.5)
    slope_part = 2.5 * row_pos
    return (rough * scaling + slope_part * pattern).astype(jnp.bfloat16)


def draw_block_qkv(key, part):
    key = jax.random.fold_in(key, 23)
    key_shared = jax.random.fold_in(key, 0)
    spread = 1.0 / math.sqrt(D)
    return (jnp.clip(jax.random.normal(key_shared, (D, 3 * D), jnp.float32), -6.0, 6.0) * spread).astype(jnp.bfloat16)


def draw_grid_qkv(key, part):
    key = jax.random.fold_in(key, 37)
    key_shared = jax.random.fold_in(key, 0)
    spread = 1.0 / math.sqrt(D)
    return (jnp.clip(jax.random.normal(key_shared, (D, 3 * D), jnp.float32), -6.0, 6.0) * spread).astype(jnp.bfloat16)


def noise(rng, shape, deviation, most, kind=jnp.bfloat16):
    values = jax.random.normal(rng, shape, jnp.float32) * deviation
    return jnp.minimum(jnp.maximum(values, -most), most).astype(kind)


def setup_inputs(seed: int = 0) -> dict:
    arg_keys = jax.random.split(jax.random.key(seed), 21)
    image = draw_image(jax.random.fold_in(arg_keys[20], 71), 0)
    mb_expand = noise(arg_keys[1], (D, FF), D ** -0.5, 0.3125)
    mb_taps = noise(arg_keys[2], (9, FF), 3 ** -0.5, 3.5)
    mb_reduce = noise(arg_keys[3], (FF, SE_D), (max(FF // 256, 1)) ** -0.5, 2.5)
    mb_restore = noise(arg_keys[4], (SE_D, FF), (max(SE_D // 32, 1)) ** -0.5, 3.5)
    mb_project = noise(arg_keys[5], (FF, D), FF ** -0.5, 0.15625)
    block_qkv = draw_block_qkv(jax.random.fold_in(arg_keys[20], 71), 0)
    block_out = noise(arg_keys[7], (D, D), D ** -0.5, 0.3125)
    first_up = noise(arg_keys[8], (D, FF), D ** -0.5, 0.3125)
    first_down = noise(arg_keys[9], (FF, D), FF ** -0.5, 0.15625)
    grid_qkv = draw_grid_qkv(jax.random.fold_in(arg_keys[20], 71), 0)
    grid_out = noise(arg_keys[11], (D, D), D ** -0.5, 0.3125)
    second_up = noise(arg_keys[12], (D, FF), D ** -0.5, 0.3125)
    second_down = noise(arg_keys[13], (FF, D), FF ** -0.5, 0.15625)
    down_expand = noise(arg_keys[14], (D, FF), D ** -0.5, 0.3125)
    down_taps = noise(arg_keys[15], (9, FF), 3 ** -0.5, 3.5)
    down_reduce = noise(arg_keys[16], (FF, SE_D), (max(FF // 256, 1)) ** -0.5, 2.5)
    down_restore = noise(arg_keys[17], (SE_D, FF), (max(SE_D // 32, 1)) ** -0.5, 3.5)
    down_project = noise(arg_keys[18], (FF, OUT_D), FF ** -0.5, 0.15625)
    down_shortcut = noise(arg_keys[19], (D, OUT_D), (4 * D) ** -0.5, 0.15625)
    return dict(image=image, mb_expand=mb_expand, mb_taps=mb_taps, mb_reduce=mb_reduce, mb_restore=mb_restore, mb_project=mb_project, block_qkv=block_qkv, block_out=block_out, first_up=first_up, first_down=first_down, grid_qkv=grid_qkv, grid_out=grid_out, second_up=second_up, second_down=second_down, down_expand=down_expand, down_taps=down_taps, down_reduce=down_reduce, down_restore=down_restore, down_project=down_project, down_shortcut=down_shortcut)


epsilon = 1e-05

def layer_norm(values):
    values = values.astype(jnp.float32)
    average = lax.optimization_barrier(jnp.mean(values, axis=-1, keepdims=True))
    centred = values - average
    spread = lax.optimization_barrier(jnp.mean(centred * centred, axis=-1, keepdims=True))
    return centred * lax.rsqrt(spread + epsilon)

def expand_cells(cells_in, weight):
    channels = cells_in.shape[-1]
    normed = layer_norm(cells_in.reshape(-1, channels)).astype(jnp.bfloat16)
    hidden = jax.nn.gelu(jnp.dot(normed, weight, preferred_element_type=jnp.float32), approximate=True)
    return hidden.astype(jnp.bfloat16).reshape(cells_in.shape[:-1] + (weight.shape[1],))

def depthwise(padded, kernel, out_rows, out_cols, stride):
    summed = jnp.zeros((out_rows, out_cols, padded.shape[-1]), jnp.float32)
    for row_tap in range(3):
        for col_tap in range(3):
            window = padded[row_tap:row_tap + stride * (out_rows - 1) + 1:stride, col_tap:col_tap + stride * (out_cols - 1) + 1:stride]
            summed = summed + window.astype(jnp.float32) * kernel[3 * row_tap + col_tap].astype(jnp.float32)
    return jax.nn.gelu(summed, approximate=True)

def excite(channel_sums, cell_count, shrink_weight, expand_weight):
    average = (channel_sums / cell_count)[None, :]
    squeezed = jax.nn.silu(jnp.dot(average, shrink_weight.astype(jnp.float32), precision=lax.Precision.HIGHEST))
    return jax.nn.sigmoid(jnp.dot(squeezed, expand_weight.astype(jnp.float32), precision=lax.Precision.HIGHEST))[0]

def attend_some(groups, qkv_weight, out_weight, head_count):
    group_count, group_size, channels = groups.shape
    head_width = channels // head_count
    normed = layer_norm(groups.reshape(-1, channels)).astype(jnp.bfloat16)
    projected = jnp.dot(normed, qkv_weight, preferred_element_type=jnp.float32).astype(jnp.bfloat16)
    projected = projected.reshape(group_count, group_size, 3, head_count, head_width).astype(jnp.float32)
    queries = projected[:, :, 0]
    key_rows = projected[:, :, 1]
    value_rows = projected[:, :, 2]
    scores = jnp.einsum('gqhd,gkhd->ghqk', queries, key_rows) / math.sqrt(head_width)
    row_max = lax.optimization_barrier(jnp.max(scores, axis=-1, keepdims=True))
    weights = jnp.exp(scores - row_max)
    shares = (weights / lax.optimization_barrier(jnp.sum(weights, axis=-1, keepdims=True))).astype(jnp.bfloat16)
    blended = jnp.einsum('ghqk,gkhd->gqhd', shares.astype(jnp.float32), value_rows).astype(jnp.bfloat16)
    blended = blended.reshape(-1, channels)
    result = groups.reshape(-1, channels).astype(jnp.float32) + jnp.dot(blended, out_weight, preferred_element_type=jnp.float32)
    return result.astype(jnp.bfloat16).reshape(groups.shape)

def attend(groups, qkv_weight, out_weight, head_count):
    group_count, group_size, channels = groups.shape
    per_block = math.gcd(group_count, 64)
    stacked = groups.reshape(group_count // per_block, per_block, group_size, channels)
    done = lax.map(lambda piece: attend_some(piece, qkv_weight, out_weight, head_count), stacked)
    return done.reshape(groups.shape)

def feed_cells(cells_in, up_weight, down_weight):
    channels = cells_in.shape[-1]
    rows_flat = cells_in.reshape(-1, channels)
    normed = layer_norm(rows_flat).astype(jnp.bfloat16)
    hidden = jax.nn.gelu(jnp.dot(normed, up_weight, preferred_element_type=jnp.float32), approximate=True).astype(jnp.bfloat16)
    result = rows_flat.astype(jnp.float32) + jnp.dot(hidden, down_weight, preferred_element_type=jnp.float32)
    return result.astype(jnp.bfloat16).reshape(cells_in.shape)

def reference(image, mb_expand, mb_taps, mb_reduce, mb_restore, mb_project, block_qkv, block_out, first_up, first_down, grid_qkv, grid_out, second_up, second_down, down_expand, down_taps, down_reduce, down_restore, down_project, down_shortcut):
    height, width, channels = image.shape
    hidden = expand_cells(image, mb_expand)
    padded = jnp.pad(hidden, ((1, 1), (1, 1), (0, 0)))
    activated = depthwise(padded, mb_taps, height, width, 1)
    gate_vec = excite(lax.optimization_barrier(jnp.sum(activated, axis=(0, 1))), height * width, mb_reduce, mb_restore)
    excited = (activated * gate_vec).astype(jnp.bfloat16).reshape(-1, activated.shape[-1])
    after_conv = image.reshape(-1, channels).astype(jnp.float32) + jnp.dot(excited, mb_project, preferred_element_type=jnp.float32)
    after_conv = after_conv.astype(jnp.bfloat16).reshape(height, width, channels)
    blocks = after_conv.reshape(height // WIN, WIN, width // WIN, WIN, channels).transpose(0, 2, 1, 3, 4)
    blocks = attend(blocks.reshape(-1, WIN * WIN, channels), block_qkv, block_out, HEADS)
    block_mixed = blocks.reshape(height // WIN, width // WIN, WIN, WIN, channels).transpose(0, 2, 1, 3, 4)
    first_mixed = feed_cells(block_mixed.reshape(height, width, channels), first_up, first_down)
    grid_sets = first_mixed.reshape(WIN, height // WIN, WIN, width // WIN, channels).transpose(1, 3, 0, 2, 4)
    grid_sets = attend(grid_sets.reshape(-1, WIN * WIN, channels), grid_qkv, grid_out, HEADS)
    grid_mixed = grid_sets.reshape(height // WIN, width // WIN, WIN, WIN, channels).transpose(2, 0, 3, 1, 4)
    section_out = feed_cells(grid_mixed.reshape(height, width, channels), second_up, second_down)
    down_hidden = expand_cells(jnp.pad(section_out, ((1, 0), (1, 0), (0, 0))), down_expand)
    down_act = depthwise(down_hidden, down_taps, height // 2, width // 2, 2)
    down_gate = excite(lax.optimization_barrier(jnp.sum(down_act, axis=(0, 1))), height // 2 * (width // 2), down_reduce, down_restore)
    down_scaled = (down_act * down_gate).astype(jnp.bfloat16).reshape(-1, down_act.shape[-1])
    pooled = lax.optimization_barrier(jnp.mean(section_out.astype(jnp.float32).reshape(height // 2, 2, width // 2, 2, channels), axis=(1, 3)))
    pooled = pooled.astype(jnp.bfloat16).reshape(-1, channels)
    branch = jnp.dot(down_scaled, down_project, preferred_element_type=jnp.float32)
    shortcut = jnp.dot(pooled, down_shortcut, preferred_element_type=jnp.float32)
    downsampled = (branch + shortcut).astype(jnp.bfloat16).reshape(height // 2, width // 2, down_project.shape[1])
    return (section_out, downsampled)
```

```python
import math

import jax
import jax.numpy as jnp
import numpy as np
from jax import lax
from jax.experimental import pallas as pl
from jax.experimental.pallas import tpu as pltpu
from jax.sharding import Mesh
from jax.sharding import PartitionSpec as P

HEADS = 12
WIN = 8
CELLS = WIN * WIN
QUAD = 4

epsilon = 1e-05
F32 = jnp.float32
BF16 = jnp.bfloat16
ROWS = ("row_pair", "core")
ALL = ("row_pair", "core", "cols")
CLASS = ("row_pair", "cols")


def params(megabytes=48):
    return pltpu.CompilerParams(vmem_limit_bytes=megabytes << 20)


def cost(flops, moved):
    return pl.CostEstimate(flops=int(flops), bytes_accessed=int(moved), transcendentals=0)


def gelu(x):
    half = 0.5 * x
    inner = x * (0.7978845608028654 + 0.035677408136300125 * (x * x))
    return half + half * jnp.tanh(inner)


def layer_norm(x):
    average = jnp.mean(x, axis=-1, keepdims=True)
    centred = x - average
    spread = jnp.mean(centred * centred, axis=-1, keepdims=True)
    return centred * lax.rsqrt(spread + epsilon)


def dot(a, b):
    return jnp.dot(a, b, preferred_element_type=F32)


def panels(rows, channels):
    return pltpu.VMEM((channels // 128, rows, 128), F32)


def put(ref, x):
    for c in range(ref.shape[0]):
        ref[c] = x[:, c * 128 : (c + 1) * 128]


def put_strided(ref, x, start, count, stride):
    for c in range(ref.shape[0]):
        ref[c, pl.ds(start, count, stride=stride), :] = x[:, c * 128 : (c + 1) * 128]


def take(ref):
    return jnp.concatenate([ref[c] for c in range(ref.shape[0])], 1)


def take_strided(ref, start, count, stride):
    return jnp.concatenate(
        [ref[c, pl.ds(start, count, stride=stride), :] for c in range(ref.shape[0])], 1
    )


def expand_kernel(x_ref, w_ref, out_ref):
    normed = layer_norm(x_ref[...].astype(F32)).astype(BF16)
    for c in range(0, w_ref.shape[1], 512):
        out_ref[:, c : c + 512] = gelu(dot(normed, w_ref[:, c : c + 512])).astype(BF16)


def expand(x, weight, block=256):
    cells, channels = x.shape
    hidden = weight.shape[1]
    return pl.pallas_call(
        expand_kernel,
        grid=(cells // block,),
        in_specs=[
            pl.BlockSpec((block, channels), lambda i: (i, 0)),
            pl.BlockSpec((channels, hidden), lambda i: (0, 0)),
        ],
        out_specs=pl.BlockSpec((block, hidden), lambda i: (i, 0)),
        out_shape=jax.ShapeDtypeStruct((cells, hidden), BF16),
        compiler_params=params(),
        cost_estimate=cost(2 * cells * channels * hidden, 2 * cells * (channels + hidden)),
        name="expand",
    )(x, weight)


def conv_kernel(
    hid_ref, top_ref, bot_ref, left_ref, right_ref, w_ref, taps_ref, red_ref,
    act_ref, part_ref, normed, left, right, part,
):
    step = pl.program_id(0)
    rows, cols, chunk = hid_ref.shape

    @pl.when(step == 0)
    def _():
        for ref, start in ((top_ref, 0), (bot_ref, 80), (left_ref, 160), (right_ref, 176)):
            size = ref.shape[0]
            normed[start : start + size, :] = layer_norm(ref[...].astype(F32)).astype(BF16)
        part[...] = jnp.zeros_like(part)

    rim = gelu(dot(normed[...], w_ref[...])).astype(BF16).astype(F32)
    left[0:1, :] = rim[64:65]
    left[1:17, :] = rim[160:176]
    left[17:18, :] = rim[144:145]
    right[0:1, :] = rim[65:66]
    right[1:17, :] = rim[176:192]
    right[17:18, :] = rim[145:146]
    place = lax.broadcasted_iota(jnp.int32, (8, 128), 0)
    sums = []
    for lane in range(0, chunk, 128):
        lanes = slice(lane, lane + 128)
        taps = [taps_ref[t : t + 1, lanes].astype(F32) for t in range(9)]
        before = sum(taps[3 * a] * left[a : a + rows, lanes] for a in range(3))
        after = sum(taps[3 * a + 2] * right[a : a + rows, lanes] for a in range(3))
        total = jnp.zeros((8, 128), F32)

        def line(r):
            if r < 0:
                return rim[0:64, lanes]
            if r == rows:
                return rim[80:144, lanes]
            return hid_ref[r, :, lanes].astype(F32)

        window = [line(-1), line(0), None]
        for r in range(rows):
            window[2] = line(r + 1)
            one = [
                taps[b] * window[0] + taps[3 + b] * window[1] + taps[6 + b] * window[2]
                for b in range(3)
            ]
            down = pltpu.roll(one[0], 1, 0)
            up = pltpu.roll(one[2], cols - 1, 0)
            first = jnp.where(place == 0, before[r : r + 1], down[0:8])
            last = jnp.where(place == 7, after[r : r + 1], up[cols - 8 :])
            whole = (
                one[1]
                + jnp.concatenate([first, down[8:]], 0)
                + jnp.concatenate([up[: cols - 8], last], 0)
            )
            act = gelu(whole)
            act_ref[r, :, lanes] = act.astype(BF16)
            for s in range(0, cols, 8):
                total = total + act[s : s + 8]
            window = [window[1], window[2], None]
        sums.append(total)
    part[...] += jnp.dot(
        jnp.concatenate(sums, 1),
        red_ref[...].astype(F32),
        precision=lax.Precision.HIGHEST,
        preferred_element_type=F32,
    )

    @pl.when(step == pl.num_programs(0) - 1)
    def _():
        whole = jnp.sum(part[...], axis=0, keepdims=True)
        part_ref[...] = jnp.broadcast_to(whole, part_ref.shape)


def conv(hidden, top, bottom, left, right, weight, taps, reduce, copies, chunk=256):
    rows, cols, width = hidden.shape
    channels = weight.shape[0]
    squeezed = reduce.shape[1]
    whole = lambda a: pl.BlockSpec(a.shape, lambda c: (0, 0))
    return pl.pallas_call(
        conv_kernel,
        grid=(width // chunk,),
        in_specs=[
            pl.BlockSpec((rows, cols, chunk), lambda c: (0, 0, c)),
            whole(top),
            whole(bottom),
            whole(left),
            whole(right),
            pl.BlockSpec((channels, chunk), lambda c: (0, c)),
            pl.BlockSpec((9, chunk), lambda c: (0, c)),
            pl.BlockSpec((chunk, squeezed), lambda c: (c, 0)),
        ],
        out_specs=[
            pl.BlockSpec((rows, cols, chunk), lambda c: (0, 0, c)),
            pl.BlockSpec((copies, squeezed), lambda c: (0, 0)),
        ],
        out_shape=[
            jax.ShapeDtypeStruct((rows, cols, width), BF16),
            jax.ShapeDtypeStruct((copies, squeezed), F32),
        ],
        scratch_shapes=[
            pltpu.VMEM((192, channels), BF16),
            pltpu.VMEM((24, chunk), F32),
            pltpu.VMEM((24, chunk), F32),
            pltpu.VMEM((8, squeezed), F32),
        ],
        compiler_params=params(),
        name="conv",
    )(hidden, top, bottom, left, right, weight, taps, reduce)


def gate_of(parts_ref, restore_ref, cell_count):
    average = jnp.sum(parts_ref[...], axis=0, keepdims=True) / cell_count
    squeezed = average * jax.nn.sigmoid(average)
    squeezed = jnp.broadcast_to(squeezed, (8, squeezed.shape[1]))
    wide = jnp.dot(
        squeezed,
        restore_ref[...].astype(F32),
        precision=lax.Precision.HIGHEST,
        preferred_element_type=F32,
    )
    return jax.nn.sigmoid(wide)


def mix(x, qkv_ref, out_ref, up_ref, down_ref):
    cells, channels = x.shape
    width = channels // HEADS
    normed = layer_norm(x).astype(BF16)
    projected = dot(normed, qkv_ref[...])
    queries = (projected[:, :channels] * (1.0 / math.sqrt(width))).astype(BF16)
    keys = projected[:, channels : 2 * channels].astype(BF16)
    values = projected[:, 2 * channels :].astype(BF16)
    lane = lax.broadcasted_iota(jnp.int32, (1, 128), 1)
    masks = [((lane >= h * width) & (lane < (h + 1) * width)).astype(BF16) for h in range(QUAD)]
    groups = []
    for g in range(0, cells, CELLS):
        mine = slice(g, g + CELLS)
        quads = []
        for c in range(0, channels, 128):
            lanes = slice(c, c + 128)
            q, k, v = queries[mine, lanes], keys[mine, lanes], values[mine, lanes]
            stacked = jnp.concatenate([q * m for m in masks], 0)
            scores = lax.dot_general(
                k, stacked, (((1,), (1,)), ((), ())), preferred_element_type=F32
            )
            weights = jnp.exp(scores - jnp.max(scores, axis=0, keepdims=True))
            shares = weights * (1.0 / jnp.sum(weights, axis=0, keepdims=True))
            blended = lax.dot_general(
                shares.astype(BF16), v, (((0,), (0,)), ((), ())), preferred_element_type=F32
            )
            picked = blended[3 * CELLS :]
            for h in (2, 1, 0):
                picked = jnp.where(
                    lane < (h + 1) * width, blended[h * CELLS : (h + 1) * CELLS], picked
                )
            quads.append(picked)
        groups.append(jnp.concatenate(quads, 1).astype(BF16))
    x = x + dot(jnp.concatenate(groups, 0), out_ref[...])
    normed = layer_norm(x).astype(BF16)
    for c in range(0, up_ref.shape[1], 512):
        hidden = gelu(dot(normed, up_ref[:, c : c + 512])).astype(BF16)
        x = x + dot(hidden, down_ref[c : c + 512, :])
    return x


def block_kernel(
    img_ref, act_ref, parts_ref, restore_ref, project_ref, qkv_ref, out_ref, up_ref, down_ref,
    res_ref, gate, *, cell_count,
):
    @pl.when(pl.program_id(0) == 0)
    def _():
        gate[...] = gate_of(parts_ref, restore_ref, cell_count)

    rows, cols, channels = img_ref.shape
    scaled = act_ref[...].reshape(rows * cols, act_ref.shape[2]).astype(F32) * gate[0:1, :]
    x = img_ref[...].reshape(rows * cols, channels).astype(F32)
    x = x + dot(scaled.astype(BF16), project_ref[...])
    wide = cols // WIN
    pieces = [
        x[r * cols + g * WIN : r * cols + (g + 1) * WIN] for g in range(wide) for r in range(rows)
    ]
    y = mix(jnp.concatenate(pieces, 0), qkv_ref, out_ref, up_ref, down_ref)
    pieces = [
        y[g * CELLS + r * WIN : g * CELLS + (r + 1) * WIN] for r in range(rows) for g in range(wide)
    ]
    res_ref[...] = jnp.concatenate(pieces, 0).astype(BF16).reshape(rows, cols, channels)


def block_part(image, act, parts, restore, project, qkv, out, up, down, cell_count, wide=32):
    rows, cols, channels = image.shape
    hidden = act.shape[2]
    across = cols // wide
    place = lambda i: (i // across, i % across, 0)
    whole = lambda a: pl.BlockSpec(a.shape, lambda i: (0, 0))
    weights = (restore, project, qkv, out, up, down)

    def kernel(*refs):
        block_kernel(*refs, cell_count=cell_count)

    return pl.pallas_call(
        kernel,
        grid=((rows // WIN) * across,),
        in_specs=[
            pl.BlockSpec((WIN, wide, channels), place),
            pl.BlockSpec((WIN, wide, hidden), place),
            whole(parts),
            *[whole(w) for w in weights],
        ],
        out_specs=pl.BlockSpec((WIN, wide, channels), place),
        out_shape=jax.ShapeDtypeStruct(image.shape, BF16),
        scratch_shapes=[pltpu.VMEM((8, hidden), F32)],
        compiler_params=params(),
        name="block_part",
    )(image, act, parts, *weights)


def grid_kernel(x_ref, qkv_ref, out_ref, up_ref, down_ref, res_ref, before, after, *, groups):
    step = pl.program_id(0)
    members, held, channels = x_ref.shape

    @pl.when(step == 0)
    def _():
        put(before, x_ref[...].reshape(members * held, channels).astype(F32))

    x = jnp.concatenate(
        [take_strided(before, step * groups + g, members, held) for g in range(groups)], 0
    )
    y = mix(x, qkv_ref, out_ref, up_ref, down_ref)
    for g in range(groups):
        mine = y[g * CELLS : (g + 1) * CELLS]
        put_strided(after, mine, step * groups + g, members, held)

    @pl.when(step == pl.num_programs(0) - 1)
    def _():
        res_ref[...] = take(after).astype(BF16).reshape(members, held, channels)


def grid_part(x, qkv, out, up, down, groups=4):
    members, held, channels = x.shape
    weights = (qkv, out, up, down)

    def kernel(*refs):
        grid_kernel(*refs, groups=groups)

    return pl.pallas_call(
        kernel,
        grid=(held // groups,),
        in_specs=[
            pl.BlockSpec(x.shape, lambda i: (0, 0, 0)),
            *[pl.BlockSpec(w.shape, lambda i: (0, 0)) for w in weights],
        ],
        out_specs=pl.BlockSpec(x.shape, lambda i: (0, 0, 0)),
        out_shape=jax.ShapeDtypeStruct(x.shape, BF16),
        scratch_shapes=[
            panels(members * held, channels),
            panels(members * held, channels),
        ],
        compiler_params=params(),
        name="grid_part",
    )(x, *weights)


def down_expand_kernel(x_ref, w_ref, out_ref, cells):
    rows, cols, channels = x_ref.shape
    put(cells, x_ref[...].reshape(rows * cols, channels).astype(F32))
    half = rows * cols // 2
    x = jnp.concatenate([take_strided(cells, parity, half, 2) for parity in range(2)], 0)
    normed = layer_norm(x).astype(BF16)
    for c in range(0, w_ref.shape[1], 512):
        hidden = gelu(dot(normed, w_ref[:, c : c + 512])).astype(BF16)
        for parity in range(2):
            out_ref[:, parity, :, c : c + 512] = hidden[parity * half : (parity + 1) * half].reshape(
                rows, cols // 2, 512
            )


def down_expand_part(x, weight, block=4):
    rows, cols, channels = x.shape
    hidden = weight.shape[1]
    return pl.pallas_call(
        down_expand_kernel,
        grid=(rows // block,),
        in_specs=[
            pl.BlockSpec((block, cols, channels), lambda i: (i, 0, 0)),
            pl.BlockSpec((channels, hidden), lambda i: (0, 0)),
        ],
        out_specs=pl.BlockSpec((block, 2, cols // 2, hidden), lambda i: (i, 0, 0, 0)),
        out_shape=jax.ShapeDtypeStruct((rows, 2, cols // 2, hidden), BF16),
        scratch_shapes=[panels(block * cols, channels)],
        compiler_params=params(),
        cost_estimate=cost(2 * rows * cols * channels * hidden, 2 * rows * cols * hidden),
        name="down_expand",
    )(x, weight)


def down_conv_kernel(
    hid_ref, upper_ref, left_ref, corner_ref, w_ref, taps_ref, red_ref,
    act_ref, part_ref, cells, normed, left, part,
):
    step = pl.program_id(0)
    rows, _, cols, chunk = hid_ref.shape

    @pl.when(step == 0)
    def _():
        put(cells, layer_norm(upper_ref[...].astype(F32)))
        normed[0:32, :] = take_strided(cells, 0, 32, 2).astype(BF16)
        normed[32:64, :] = take_strided(cells, 1, 32, 2).astype(BF16)
        normed[64:80, :] = layer_norm(left_ref[...].astype(F32)).astype(BF16)
        corner = layer_norm(corner_ref[...].astype(F32))
        normed[80:96, :] = jnp.broadcast_to(corner, (16, corner.shape[1])).astype(BF16)
        part[...] = jnp.zeros_like(part)

    rim = gelu(dot(normed[...], w_ref[...])).astype(BF16).astype(F32)
    left[0:1, :] = rim[80:81]
    left[1:17, :] = rim[64:80]
    place = lax.broadcasted_iota(jnp.int32, (8, 128), 0)
    sums = []
    for lane in range(0, chunk, 128):
        lanes = slice(lane, lane + 128)
        taps = [taps_ref[t : t + 1, lanes].astype(F32) for t in range(9)]
        before = sum(taps[3 * a] * left[a : a + rows, lanes] for a in range(3))
        total = jnp.zeros((8, 128), F32)

        def line(r, parity):
            if r < 0:
                return rim[32 * parity : 32 * parity + 32, lanes]
            return hid_ref[r, parity, :, lanes].astype(F32)

        for p in range(rows // 2):
            even = [line(2 * p + a - 1, 0) for a in range(3)]
            odd = [line(2 * p + a - 1, 1) for a in range(3)]
            shifted = sum(taps[3 * a] * odd[a] for a in range(3))
            whole = sum(taps[3 * a + 1] * even[a] + taps[3 * a + 2] * odd[a] for a in range(3))
            shifted = pltpu.roll(shifted, 1, 0)
            first = jnp.where(place == 0, before[2 * p : 2 * p + 1], shifted[0:8])
            act = gelu(whole + jnp.concatenate([first, shifted[8:]], 0))
            act_ref[p, :, lanes] = act.astype(BF16)
            for s in range(0, cols, 8):
                total = total + act[s : s + 8]
        sums.append(total)
    part[...] += jnp.dot(
        jnp.concatenate(sums, 1),
        red_ref[...].astype(F32),
        precision=lax.Precision.HIGHEST,
        preferred_element_type=F32,
    )

    @pl.when(step == pl.num_programs(0) - 1)
    def _():
        whole = jnp.sum(part[...], axis=0, keepdims=True)
        part_ref[...] = jnp.broadcast_to(whole, part_ref.shape)


def down_conv(hidden, upper, left, corner, weight, taps, reduce, copies, chunk=256):
    rows, _, cols, width = hidden.shape
    channels = weight.shape[0]
    squeezed = reduce.shape[1]
    whole = lambda a: pl.BlockSpec(a.shape, lambda c: (0, 0))
    return pl.pallas_call(
        down_conv_kernel,
        grid=(width // chunk,),
        in_specs=[
            pl.BlockSpec((rows, 2, cols, chunk), lambda c: (0, 0, 0, c)),
            whole(upper),
            whole(left),
            whole(corner),
            pl.BlockSpec((channels, chunk), lambda c: (0, c)),
            pl.BlockSpec((9, chunk), lambda c: (0, c)),
            pl.BlockSpec((chunk, squeezed), lambda c: (c, 0)),
        ],
        out_specs=[
            pl.BlockSpec((rows // 2, cols, chunk), lambda c: (0, 0, c)),
            pl.BlockSpec((copies, squeezed), lambda c: (0, 0)),
        ],
        out_shape=[
            jax.ShapeDtypeStruct((rows // 2, cols, width), BF16),
            jax.ShapeDtypeStruct((copies, squeezed), F32),
        ],
        scratch_shapes=[
            panels(64, channels),
            pltpu.VMEM((96, channels), BF16),
            pltpu.VMEM((24, chunk), F32),
            pltpu.VMEM((8, squeezed), F32),
        ],
        compiler_params=params(),
        name="down_conv",
    )(hidden, upper, left, corner, weight, taps, reduce)


def down_out_kernel(
    act_ref, x_ref, parts_ref, restore_ref, project_ref, short_ref, res_ref, cells, *, cell_count
):
    gate = gate_of(parts_ref, restore_ref, cell_count)
    rows, cols, channels = x_ref.shape
    half = cols // 2
    x = x_ref[...].astype(F32).reshape(rows // 2, 2, cols, channels)
    put(cells, (x[:, 0] + x[:, 1]).reshape(rows // 2 * cols, channels))
    count = rows // 2 * half
    pooled = (take_strided(cells, 0, count, 2) + take_strided(cells, 1, count, 2)) * 0.25
    scaled = act_ref[...].reshape(count, act_ref.shape[2]).astype(F32) * gate[0:1, :]
    y = dot(scaled.astype(BF16), project_ref[...]) + dot(pooled.astype(BF16), short_ref[...])
    res_ref[...] = y.astype(BF16).reshape(rows // 2, half, y.shape[1])


def down_out(act, x, parts, restore, project, short, cell_count):
    rows, cols, channels = x.shape
    outs = project.shape[1]

    def kernel(*refs):
        down_out_kernel(*refs, cell_count=cell_count)

    return pl.pallas_call(
        kernel,
        out_shape=jax.ShapeDtypeStruct((rows // 2, cols // 2, outs), BF16),
        scratch_shapes=[panels(rows // 2 * cols, channels)],
        compiler_params=params(),
        name="down_out",
    )(act, x, parts, restore, project, short)


def shift(x, axes, by):
    size = lax.axis_size(axes)
    pairs = [(i, i + by) for i in range(size) if 0 <= i + by < size]
    return lax.ppermute(x, axes, pairs)


def shift_both(x, by_rows, by_cols):
    rows, cols = lax.axis_size(ROWS), lax.axis_size("cols")
    pairs = [
        (r * cols + c, (r + by_rows) * cols + c + by_cols)
        for r in range(rows)
        for c in range(cols)
        if 0 <= r + by_rows < rows and 0 <= c + by_cols < cols
    ]
    return lax.ppermute(x, ALL, pairs)


def sum_parts(part):
    other = lax.ppermute(part, "core", [(0, 1), (1, 0)])
    count, squeezed = part.shape
    both = (part + other).reshape(count, 1, squeezed)
    arrived = lax.all_to_all(both, CLASS, split_axis=0, concat_axis=0, tiled=True)
    return arrived.reshape(count, squeezed)


def local(
    image,
    mb_expand,
    mb_taps,
    mb_reduce,
    mb_restore,
    mb_project,
    block_qkv,
    block_out,
    first_up,
    first_down,
    grid_qkv,
    grid_out,
    second_up,
    second_down,
    down_expand,
    down_taps,
    down_reduce,
    down_restore,
    down_project,
    down_shortcut,
):
    rows, cols, channels = image.shape
    sharers = lax.axis_size(CLASS)
    all_cells = rows * cols * lax.axis_size(ALL)

    left = shift(image[:, cols - 1], "cols", 1)
    right = shift(image[:, 0], "cols", -1)
    hidden = expand(image.reshape(rows * cols, channels), mb_expand)
    pad = jnp.zeros((14, channels), image.dtype)
    last = jnp.concatenate([image[rows - 1], left[rows - 1 :], right[rows - 1 :], pad], 0)
    first = jnp.concatenate([image[0], left[:1], right[:1], pad], 0)
    top = shift(last, ROWS, 1)
    bottom = shift(first, ROWS, -1)
    act, part = conv(
        hidden.reshape(rows, cols, -1), top, bottom, left, right, mb_expand, mb_taps, mb_reduce,
        sharers,
    )
    parts = sum_parts(part)
    mixed = block_part(
        image, act, parts, mb_restore, mb_project, block_qkv, block_out, first_up, first_down,
        all_cells,
    )
    held = rows * cols // sharers
    grouped = lax.all_to_all(
        mixed.reshape(sharers, held, channels), CLASS, split_axis=0, concat_axis=0, tiled=True
    )
    grouped = grid_part(grouped, grid_qkv, grid_out, second_up, second_down)
    section = lax.all_to_all(grouped, CLASS, split_axis=0, concat_axis=0, tiled=True)
    section = section.reshape(rows, cols, channels)

    upper = shift(section[rows - 1], ROWS, 1)
    left = shift(section[:, cols - 1], "cols", 1)
    corner = shift_both(section[rows - 1, cols - 1 :], 1, 1)
    hidden = down_expand_part(section, down_expand)
    act, part = down_conv(
        hidden, upper, left, corner, down_expand, down_taps, down_reduce, sharers
    )
    parts = sum_parts(part)
    downsampled = down_out(
        act, section, parts, down_restore, down_project, down_shortcut, all_cells // 4
    )
    return (section, downsampled)


def solution(mesh):
    rows, cols = mesh.devices.shape
    fine = Mesh(np.asarray(mesh.devices).reshape(rows // 2, 2, cols), ALL)
    tile = P(ROWS, "cols", None)
    in_specs = (tile,) + (P(),) * 19
    return jax.shard_map(
        local, mesh=fine, in_specs=in_specs, out_specs=(tile, tile), check_vma=False
    )
```

```python
import math

import jax
import jax.numpy as jnp
import numpy as np
from jax import lax
from jax.experimental import pallas as pl
from jax.experimental.pallas import tpu as pltpu
from jax.sharding import Mesh
from jax.sharding import PartitionSpec as P

HEADS = 12
WIN = 8
CELLS = WIN * WIN
QUAD = 4

epsilon = 1e-05
F32 = jnp.float32
BF16 = jnp.bfloat16
ROWS = ("row_pair", "core")
ALL = ("row_pair", "core", "cols")
CLASS = ("row_pair", "cols")


def params(megabytes):
    return pltpu.CompilerParams(vmem_limit_bytes=megabytes << 20)


def cost(flops, moved):
    return pl.CostEstimate(flops=int(flops), bytes_accessed=int(moved), transcendentals=0)


def gelu(x):
    half = 0.5 * x
    inner = x * (0.7978845608028654 + 0.035677408136300125 * (x * x))
    return half + half * jnp.tanh(inner)


def layer_norm(x):
    average = jnp.mean(x, axis=-1, keepdims=True)
    centred = x - average
    spread = jnp.mean(centred * centred, axis=-1, keepdims=True)
    return centred * lax.rsqrt(spread + epsilon)


def dot(a, b):
    return jnp.dot(a, b, preferred_element_type=F32)


def exact_dot(a, b, dims):
    total = None
    for _ in range(3):
        term = a.astype(BF16)
        a = a - term.astype(F32)
        product = lax.dot_general(term, b, (dims, ((), ())), preferred_element_type=F32)
        total = product if total is None else total + product
    return total


def panels(rows, channels):
    return pltpu.VMEM((channels // 128, rows, 128), F32)


def put(ref, x):
    for c in range(ref.shape[0]):
        ref[c] = x[:, c * 128 : (c + 1) * 128]


def put_strided(ref, x, start, count, stride):
    for c in range(ref.shape[0]):
        ref[c, pl.ds(start, count, stride=stride), :] = x[:, c * 128 : (c + 1) * 128]


def take(ref):
    return jnp.concatenate([ref[c] for c in range(ref.shape[0])], 1)


def take_strided(ref, start, count, stride):
    return jnp.concatenate(
        [ref[c, pl.ds(start, count, stride=stride), :] for c in range(ref.shape[0])], 1
    )


def expand_kernel(x_ref, w_ref, out_ref):
    normed = layer_norm(x_ref[...].astype(F32)).astype(BF16)
    for c in range(0, w_ref.shape[1], 512):
        out_ref[:, c : c + 512] = gelu(dot(normed, w_ref[:, c : c + 512])).astype(BF16)


def expand(x, weight, block=256):
    cells, channels = x.shape
    hidden = weight.shape[1]
    return pl.pallas_call(
        expand_kernel,
        grid=(cells // block,),
        in_specs=[
            pl.BlockSpec((block, channels), lambda i: (i, 0)),
            pl.BlockSpec((channels, hidden), lambda i: (0, 0)),
        ],
        out_specs=pl.BlockSpec((block, hidden), lambda i: (i, 0)),
        out_shape=jax.ShapeDtypeStruct((cells, hidden), BF16),
        compiler_params=params(16),
        cost_estimate=cost(2 * cells * channels * hidden, 2 * cells * (channels + hidden)),
        name="expand",
    )(x, weight)


def rim_of(normed, w_ref, rim, slot):
    rim[slot] = gelu(dot(normed[...], w_ref[...])).astype(BF16).astype(F32)


def squeeze_sums(sums, red_ref, part_ref):
    parts = exact_dot(sums[...], red_ref[...], ((1,), (1,)))
    part_ref[...] = jnp.broadcast_to(jnp.sum(parts, axis=0, keepdims=True), part_ref.shape)


def conv_kernel(
    hid_ref, over_ref, pair_ref, left_ref, right_ref, first_ref, w_ref, taps_ref, red_ref,
    act_ref, part_ref, normed, rim, left, right, sums,
):
    step = pl.program_id(0)
    core = lax.axis_index("core")
    rows, cols, chunk = hid_ref.shape
    slot = step % 2

    @pl.when(step == 0)
    def _():
        for ref, start in ((over_ref, 0), (pair_ref, 80), (left_ref, 160), (right_ref, 176)):
            size = ref.shape[0]
            normed[start : start + size, :] = layer_norm(ref[...].astype(F32)).astype(BF16)
        rim_of(normed, first_ref, rim, 0)

    top, bottom = core * 80, (1 - core) * 80
    for ref, start, corner in ((left, 160, 64), (right, 176, 65)):
        ref[0:1, :] = rim[slot, pl.ds(top + corner, 1), :]
        ref[1:17, :] = rim[slot, start : start + 16, :]
        ref[17:18, :] = rim[slot, pl.ds(bottom + corner, 1), :]
    place = lax.broadcasted_iota(jnp.int32, (8, 128), 0)
    for lane in range(0, chunk, 128):
        lanes = slice(lane, lane + 128)
        taps = [taps_ref[t : t + 1, lanes].astype(F32) for t in range(9)]
        before = sum(taps[3 * a] * left[a : a + rows, lanes] for a in range(3))
        after = sum(taps[3 * a + 2] * right[a : a + rows, lanes] for a in range(3))
        total = jnp.zeros((8, 128), F32)

        def line(r):
            if r < 0:
                return rim[slot, pl.ds(pl.multiple_of(top, 8), 64), lanes]
            if r == rows:
                return rim[slot, pl.ds(pl.multiple_of(bottom, 8), 64), lanes]
            return hid_ref[r, :, lanes].astype(F32)

        window = [line(-1), line(0), None]
        for r in range(rows):
            window[2] = line(r + 1)
            one = [
                taps[b] * window[0] + taps[3 + b] * window[1] + taps[6 + b] * window[2]
                for b in range(3)
            ]
            down = pltpu.roll(one[0], 1, 0)
            up = pltpu.roll(one[2], cols - 1, 0)
            first = jnp.where(place == 0, before[r : r + 1], down[0:8])
            last = jnp.where(place == 7, after[r : r + 1], up[cols - 8 :])
            whole = (
                one[1]
                + jnp.concatenate([first, down[8:]], 0)
                + jnp.concatenate([up[: cols - 8], last], 0)
            )
            act = gelu(whole)
            act_ref[r, :, lanes] = act.astype(BF16)
            for s in range(0, cols, 8):
                total = total + act[s : s + 8]
            window = [window[1], window[2], None]
        sums[:, pl.ds(pl.multiple_of(step * chunk + lane, 128), 128)] = total
    rim_of(normed, w_ref, rim, 1 - slot)

    @pl.when(step == pl.num_programs(0) - 1)
    def _():
        squeeze_sums(sums, red_ref, part_ref)


def conv(hidden, over, pair, left, right, weight, taps, reduce, copies, chunk=256):
    rows, cols, width = hidden.shape
    channels = weight.shape[0]
    squeezed = reduce.shape[0]
    steps = width // chunk
    whole = lambda a: pl.BlockSpec(a.shape, lambda c: (0, 0))
    return pl.pallas_call(
        conv_kernel,
        grid=(steps,),
        in_specs=[
            pl.BlockSpec((rows, cols, chunk), lambda c: (0, 0, c)),
            whole(over),
            whole(pair),
            whole(left),
            whole(right),
            pl.BlockSpec((channels, chunk), lambda c: (0, 0)),
            pl.BlockSpec((channels, chunk), lambda c: (0, jnp.minimum(c + 1, steps - 1))),
            pl.BlockSpec((9, chunk), lambda c: (0, c)),
            whole(reduce),
        ],
        out_specs=[
            pl.BlockSpec((rows, cols, chunk), lambda c: (0, 0, c)),
            pl.BlockSpec((copies, squeezed), lambda c: (0, 0)),
        ],
        out_shape=[
            jax.ShapeDtypeStruct((rows, cols, width), BF16),
            jax.ShapeDtypeStruct((copies, squeezed), F32),
        ],
        scratch_shapes=[
            pltpu.VMEM((192, channels), BF16),
            pltpu.VMEM((2, 192, chunk), F32),
            pltpu.VMEM((24, chunk), F32),
            pltpu.VMEM((24, chunk), F32),
            pltpu.VMEM((8, width), F32),
        ],
        compiler_params=params(20),
        name="conv",
    )(hidden, over, pair, left, right, weight, weight, taps, reduce)


def gate_of(parts_ref, restore_ref, cell_count):
    average = jnp.sum(parts_ref[...], axis=0, keepdims=True) / cell_count
    squeezed = average * jax.nn.sigmoid(average)
    squeezed = jnp.broadcast_to(squeezed, (8, squeezed.shape[1]))
    return jax.nn.sigmoid(exact_dot(squeezed, restore_ref[...], ((1,), (0,))))


def mix(x, qkv_ref, out_ref, up_ref, down_ref):
    cells, channels = x.shape
    width = channels // HEADS
    normed = layer_norm(x).astype(BF16)
    projected = dot(normed, qkv_ref[...])
    queries = (projected[:, :channels] * (1.0 / math.sqrt(width))).astype(BF16)
    keys = projected[:, channels : 2 * channels].astype(BF16)
    values = projected[:, 2 * channels :].astype(BF16)
    lane = lax.broadcasted_iota(jnp.int32, (1, 128), 1)
    masks = [((lane >= h * width) & (lane < (h + 1) * width)).astype(BF16) for h in range(QUAD)]
    groups = []
    for g in range(0, cells, CELLS):
        mine = slice(g, g + CELLS)
        quads = []
        for c in range(0, channels, 128):
            lanes = slice(c, c + 128)
            q, k, v = queries[mine, lanes], keys[mine, lanes], values[mine, lanes]
            stacked = jnp.concatenate([q * m for m in masks], 0)
            scores = lax.dot_general(
                k, stacked, (((1,), (1,)), ((), ())), preferred_element_type=F32
            )
            weights = jnp.exp(scores - jnp.max(scores, axis=0, keepdims=True))
            shares = weights * (1.0 / jnp.sum(weights, axis=0, keepdims=True))
            blended = lax.dot_general(
                shares.astype(BF16), v, (((0,), (0,)), ((), ())), preferred_element_type=F32
            )
            picked = blended[3 * CELLS :]
            for h in (2, 1, 0):
                picked = jnp.where(
                    lane < (h + 1) * width, blended[h * CELLS : (h + 1) * CELLS], picked
                )
            quads.append(picked)
        groups.append(jnp.concatenate(quads, 1).astype(BF16))
    x = x + dot(jnp.concatenate(groups, 0), out_ref[...])
    normed = layer_norm(x).astype(BF16)
    for c in range(0, up_ref.shape[1], 512):
        hidden = gelu(dot(normed, up_ref[:, c : c + 512])).astype(BF16)
        x = x + dot(hidden, down_ref[c : c + 512, :])
    return x


def block_kernel(
    img_ref, act_ref, parts_ref, restore_ref, project_ref, qkv_ref, out_ref, up_ref, down_ref,
    res_ref, gate, *, cell_count,
):
    @pl.when(pl.program_id(0) == 0)
    def _():
        gate[...] = gate_of(parts_ref, restore_ref, cell_count)

    rows, cols, channels = img_ref.shape
    scaled = act_ref[...].reshape(rows * cols, act_ref.shape[2]).astype(F32) * gate[0:1, :]
    x = img_ref[...].reshape(rows * cols, channels).astype(F32)
    x = x + dot(scaled.astype(BF16), project_ref[...])
    wide = cols // WIN
    pieces = [
        x[r * cols + g * WIN : r * cols + (g + 1) * WIN] for g in range(wide) for r in range(rows)
    ]
    y = mix(jnp.concatenate(pieces, 0), qkv_ref, out_ref, up_ref, down_ref)
    pieces = [
        y[g * CELLS + r * WIN : g * CELLS + (r + 1) * WIN] for r in range(rows) for g in range(wide)
    ]
    res_ref[...] = jnp.concatenate(pieces, 0).astype(BF16).reshape(rows, cols, channels)


def block_part(image, act, parts, restore, project, qkv, out, up, down, cell_count, wide=64):
    rows, cols, channels = image.shape
    hidden = act.shape[2]
    across = cols // wide
    place = lambda i: (i // across, i % across, 0)
    whole = lambda a: pl.BlockSpec(a.shape, lambda i: (0, 0))
    weights = (restore, project, qkv, out, up, down)

    def kernel(*refs):
        block_kernel(*refs, cell_count=cell_count)

    return pl.pallas_call(
        kernel,
        grid=((rows // WIN) * across,),
        in_specs=[
            pl.BlockSpec((WIN, wide, channels), place),
            pl.BlockSpec((WIN, wide, hidden), place),
            whole(parts),
            *[whole(w) for w in weights],
        ],
        out_specs=pl.BlockSpec((WIN, wide, channels), place),
        out_shape=jax.ShapeDtypeStruct(image.shape, BF16),
        scratch_shapes=[pltpu.VMEM((8, hidden), F32)],
        compiler_params=params(40),
        name="block_part",
    )(image, act, parts, *weights)


def grid_kernel(x_ref, qkv_ref, out_ref, up_ref, down_ref, res_ref, before, after, *, groups):
    step = pl.program_id(0)
    members, held, channels = x_ref.shape

    @pl.when(step == 0)
    def _():
        put(before, x_ref[...].reshape(members * held, channels).astype(F32))

    x = jnp.concatenate(
        [take_strided(before, step * groups + g, members, held) for g in range(groups)], 0
    )
    y = mix(x, qkv_ref, out_ref, up_ref, down_ref)
    for g in range(groups):
        mine = y[g * CELLS : (g + 1) * CELLS]
        put_strided(after, mine, step * groups + g, members, held)

    @pl.when(step == pl.num_programs(0) - 1)
    def _():
        res_ref[...] = take(after).astype(BF16).reshape(members, held, channels)


def grid_part(x, qkv, out, up, down, groups=8):
    members, held, channels = x.shape
    weights = (qkv, out, up, down)

    def kernel(*refs):
        grid_kernel(*refs, groups=groups)

    return pl.pallas_call(
        kernel,
        grid=(held // groups,),
        in_specs=[
            pl.BlockSpec(x.shape, lambda i: (0, 0, 0)),
            *[pl.BlockSpec(w.shape, lambda i: (0, 0)) for w in weights],
        ],
        out_specs=pl.BlockSpec(x.shape, lambda i: (0, 0, 0)),
        out_shape=jax.ShapeDtypeStruct(x.shape, BF16),
        scratch_shapes=[
            panels(members * held, channels),
            panels(members * held, channels),
        ],
        compiler_params=params(40),
        name="grid_part",
    )(x, *weights)


def down_expand_kernel(x_ref, w_ref, out_ref, cells):
    rows, cols, channels = x_ref.shape
    put(cells, x_ref[...].reshape(rows * cols, channels).astype(F32))
    half = rows * cols // 2
    x = jnp.concatenate([take_strided(cells, parity, half, 2) for parity in range(2)], 0)
    normed = layer_norm(x).astype(BF16)
    for c in range(0, w_ref.shape[1], 512):
        hidden = gelu(dot(normed, w_ref[:, c : c + 512])).astype(BF16)
        for parity in range(2):
            out_ref[:, parity, :, c : c + 512] = hidden[parity * half : (parity + 1) * half].reshape(
                rows, cols // 2, 512
            )


def down_expand_part(x, weight, block=4):
    rows, cols, channels = x.shape
    hidden = weight.shape[1]
    return pl.pallas_call(
        down_expand_kernel,
        grid=(rows // block,),
        in_specs=[
            pl.BlockSpec((block, cols, channels), lambda i: (i, 0, 0)),
            pl.BlockSpec((channels, hidden), lambda i: (0, 0)),
        ],
        out_specs=pl.BlockSpec((block, 2, cols // 2, hidden), lambda i: (i, 0, 0, 0)),
        out_shape=jax.ShapeDtypeStruct((rows, 2, cols // 2, hidden), BF16),
        scratch_shapes=[panels(block * cols, channels)],
        compiler_params=params(16),
        cost_estimate=cost(2 * rows * cols * channels * hidden, 2 * rows * cols * hidden),
        name="down_expand",
    )(x, weight)


def down_conv_kernel(
    hid_ref, upper_ref, left_ref, corner_ref, first_ref, w_ref, taps_ref, red_ref,
    act_ref, part_ref, cells, normed, rim, left, sums,
):
    step = pl.program_id(0)
    rows, _, cols, chunk = hid_ref.shape
    slot = step % 2

    @pl.when(step == 0)
    def _():
        put(cells, layer_norm(upper_ref[...].astype(F32)))
        normed[0:32, :] = take_strided(cells, 0, 32, 2).astype(BF16)
        normed[32:64, :] = take_strided(cells, 1, 32, 2).astype(BF16)
        normed[64:80, :] = layer_norm(left_ref[...].astype(F32)).astype(BF16)
        corner = layer_norm(corner_ref[...].astype(F32))
        normed[80:96, :] = jnp.broadcast_to(corner, (16, corner.shape[1])).astype(BF16)
        rim_of(normed, first_ref, rim, 0)

    left[0:1, :] = rim[slot, 80:81, :]
    left[1:17, :] = rim[slot, 64:80, :]
    place = lax.broadcasted_iota(jnp.int32, (8, 128), 0)
    for lane in range(0, chunk, 128):
        lanes = slice(lane, lane + 128)
        taps = [taps_ref[t : t + 1, lanes].astype(F32) for t in range(9)]
        before = sum(taps[3 * a] * left[a : a + rows, lanes] for a in range(3))
        total = jnp.zeros((8, 128), F32)

        def line(r, parity):
            if r < 0:
                return rim[slot, 32 * parity : 32 * parity + 32, lanes]
            return hid_ref[r, parity, :, lanes].astype(F32)

        for p in range(rows // 2):
            even = [line(2 * p + a - 1, 0) for a in range(3)]
            odd = [line(2 * p + a - 1, 1) for a in range(3)]
            shifted = sum(taps[3 * a] * odd[a] for a in range(3))
            whole = sum(taps[3 * a + 1] * even[a] + taps[3 * a + 2] * odd[a] for a in range(3))
            shifted = pltpu.roll(shifted, 1, 0)
            first = jnp.where(place == 0, before[2 * p : 2 * p + 1], shifted[0:8])
            act = gelu(whole + jnp.concatenate([first, shifted[8:]], 0))
            act_ref[p, :, lanes] = act.astype(BF16)
            for s in range(0, cols, 8):
                total = total + act[s : s + 8]
        sums[:, pl.ds(pl.multiple_of(step * chunk + lane, 128), 128)] = total
    rim_of(normed, w_ref, rim, 1 - slot)

    @pl.when(step == pl.num_programs(0) - 1)
    def _():
        squeeze_sums(sums, red_ref, part_ref)


def down_conv(hidden, upper, left, corner, weight, taps, reduce, copies, chunk=256):
    rows, _, cols, width = hidden.shape
    channels = weight.shape[0]
    squeezed = reduce.shape[0]
    steps = width // chunk
    whole = lambda a: pl.BlockSpec(a.shape, lambda c: (0, 0))
    return pl.pallas_call(
        down_conv_kernel,
        grid=(steps,),
        in_specs=[
            pl.BlockSpec((rows, 2, cols, chunk), lambda c: (0, 0, 0, c)),
            whole(upper),
            whole(left),
            whole(corner),
            pl.BlockSpec((channels, chunk), lambda c: (0, 0)),
            pl.BlockSpec((channels, chunk), lambda c: (0, jnp.minimum(c + 1, steps - 1))),
            pl.BlockSpec((9, chunk), lambda c: (0, c)),
            whole(reduce),
        ],
        out_specs=[
            pl.BlockSpec((rows // 2, cols, chunk), lambda c: (0, 0, c)),
            pl.BlockSpec((copies, squeezed), lambda c: (0, 0)),
        ],
        out_shape=[
            jax.ShapeDtypeStruct((rows // 2, cols, width), BF16),
            jax.ShapeDtypeStruct((copies, squeezed), F32),
        ],
        scratch_shapes=[
            panels(64, channels),
            pltpu.VMEM((96, channels), BF16),
            pltpu.VMEM((2, 96, chunk), F32),
            pltpu.VMEM((24, chunk), F32),
            pltpu.VMEM((8, width), F32),
        ],
        compiler_params=params(16),
        name="down_conv",
    )(hidden, upper, left, corner, weight, weight, taps, reduce)


def down_out_kernel(
    act_ref, x_ref, parts_ref, restore_ref, project_ref, short_ref, res_ref, cells, *, cell_count
):
    gate = gate_of(parts_ref, restore_ref, cell_count)
    rows, cols, channels = x_ref.shape
    half = cols // 2
    x = x_ref[...].astype(F32).reshape(rows // 2, 2, cols, channels)
    put(cells, (x[:, 0] + x[:, 1]).reshape(rows // 2 * cols, channels))
    count = rows // 2 * half
    pooled = (take_strided(cells, 0, count, 2) + take_strided(cells, 1, count, 2)) * 0.25
    scaled = act_ref[...].reshape(count, act_ref.shape[2]).astype(F32) * gate[0:1, :]
    y = dot(scaled.astype(BF16), project_ref[...]) + dot(pooled.astype(BF16), short_ref[...])
    res_ref[...] = y.astype(BF16).reshape(rows // 2, half, y.shape[1])


def down_out(act, x, parts, restore, project, short, cell_count):
    rows, cols, channels = x.shape
    outs = project.shape[1]

    def kernel(*refs):
        down_out_kernel(*refs, cell_count=cell_count)

    return pl.pallas_call(
        kernel,
        out_shape=jax.ShapeDtypeStruct((rows // 2, cols // 2, outs), BF16),
        scratch_shapes=[panels(rows // 2 * cols, channels)],
        compiler_params=params(24),
        name="down_out",
    )(act, x, parts, restore, project, short)


def shift(x, axes, by):
    size = lax.axis_size(axes)
    pairs = [(i, i + by) for i in range(size) if 0 <= i + by < size]
    return lax.ppermute(x, axes, pairs)


def shift_both(x, by_rows, by_cols):
    rows, cols = lax.axis_size(ROWS), lax.axis_size("cols")
    pairs = [
        (r * cols + c, (r + by_rows) * cols + c + by_cols)
        for r in range(rows)
        for c in range(cols)
        if 0 <= r + by_rows < rows and 0 <= c + by_cols < cols
    ]
    return lax.ppermute(x, ALL, pairs)


def sum_parts(part):
    count, squeezed = part.shape
    part = part.reshape(count, 1, squeezed)
    arrived = lax.all_to_all(part, ALL, split_axis=0, concat_axis=0, tiled=True)
    return arrived.reshape(count, squeezed)


def row_rims(image, left, right):
    rows, cols, channels = image.shape
    size = lax.axis_size(ROWS)
    pad = jnp.zeros((14, channels), image.dtype)
    first = jnp.concatenate([image[0], left[:1], right[:1], pad], 0)
    last = jnp.concatenate([image[rows - 1], left[rows - 1 :], right[rows - 1 :], pad], 0)
    even = lax.axis_index("core") == 0
    away = jnp.where(even, first, last)
    near = jnp.where(even, last, first)
    pairs = [(r, r - 1 if r % 2 == 0 else r + 1) for r in range(1, size - 1)]
    over = lax.ppermute(away, ROWS, pairs)
    pair = lax.ppermute(near, "core", [(0, 1), (1, 0)])
    return over, pair


def local(
    image,
    mb_expand,
    mb_taps,
    mb_reduce,
    mb_restore,
    mb_project,
    block_qkv,
    block_out,
    first_up,
    first_down,
    grid_qkv,
    grid_out,
    second_up,
    second_down,
    down_expand,
    down_taps,
    down_reduce,
    down_restore,
    down_project,
    down_shortcut,
):
    rows, cols, channels = image.shape
    sharers = lax.axis_size(CLASS)
    all_cells = rows * cols * lax.axis_size(ALL)

    left = shift(image[:, cols - 1], "cols", 1)
    right = shift(image[:, 0], "cols", -1)
    hidden = expand(image.reshape(rows * cols, channels), mb_expand)
    over, pair = row_rims(image, left, right)
    act, part = conv(
        hidden.reshape(rows, cols, -1), over, pair, left, right, mb_expand, mb_taps, mb_reduce.T,
        lax.axis_size(ALL),
    )
    parts = sum_parts(part)
    mixed = block_part(
        image, act, parts, mb_restore, mb_project, block_qkv, block_out, first_up, first_down,
        all_cells,
    )
    held = rows * cols // sharers
    grouped = lax.all_to_all(
        mixed.reshape(sharers, held, channels), CLASS, split_axis=0, concat_axis=0, tiled=True
    )
    grouped = grid_part(grouped, grid_qkv, grid_out, second_up, second_down)
    section = lax.all_to_all(grouped, CLASS, split_axis=0, concat_axis=0, tiled=True)
    section = section.reshape(rows, cols, channels)

    upper = shift(section[rows - 1], ROWS, 1)
    left = shift(section[:, cols - 1], "cols", 1)
    corner = shift_both(section[rows - 1, cols - 1 :], 1, 1)
    hidden = down_expand_part(section, down_expand)
    act, part = down_conv(
        hidden, upper, left, corner, down_expand, down_taps, down_reduce.T, lax.axis_size(ALL)
    )
    parts = sum_parts(part)
    downsampled = down_out(
        act, section, parts, down_restore, down_project, down_shortcut, all_cells // 4
    )
    return (section, downsampled)


def solution(mesh):
    rows, cols = mesh.devices.shape
    fine = Mesh(np.asarray(mesh.devices).reshape(rows // 2, 2, cols), ALL)
    tile = P(ROWS, "cols", None)
    in_specs = (tile,) + (P(),) * 19
    return jax.shard_map(
        local, mesh=fine, in_specs=in_specs, out_specs=(tile, tile), check_vma=False
    )
```

```python
import math

import jax
import jax.numpy as jnp
import numpy as np
from jax import lax
from jax.experimental import pallas as pl
from jax.experimental.pallas import tpu as pltpu
from jax.sharding import Mesh
from jax.sharding import PartitionSpec as P

HEADS = 12
WIN = 8
CELLS = WIN * WIN
QUAD = 4

epsilon = 1e-05
F32 = jnp.float32
BF16 = jnp.bfloat16
ROWS = ("row_pair", "core")
ALL = ("row_pair", "core", "cols")
CLASS = ("row_pair", "cols")


def params(megabytes):
    return pltpu.CompilerParams(vmem_limit_bytes=megabytes << 20)


def in_hbm(x):
    return pltpu.with_memory_space_constraint(x, pltpu.HBM)


def cost(flops, moved):
    return pl.CostEstimate(flops=int(flops), bytes_accessed=int(moved), transcendentals=0)


def gelu_twice(h):
    inner = h * (1.5957691216057308 + 0.285419265090401 * (h * h))
    return h + h * jnp.tanh(inner)


def layer_norm(x, scale=1.0):
    average = jnp.mean(x, axis=-1, keepdims=True)
    centred = x - average
    spread = jnp.mean(centred * centred, axis=-1, keepdims=True)
    return centred * (scale * lax.rsqrt(spread + epsilon))


def half_norm(x):
    return layer_norm(x, 0.5)


def dot(a, b):
    return jnp.dot(a, b, preferred_element_type=F32)


def exact_dot(a, b, dims):
    total = None
    for _ in range(3):
        term = a.astype(BF16)
        a = a - term.astype(F32)
        product = lax.dot_general(term, b, (dims, ((), ())), preferred_element_type=F32)
        total = product if total is None else total + product
    return total


def panels(rows, channels):
    return pltpu.VMEM((channels // 128, rows, 128), F32)


def put(ref, x):
    for c in range(ref.shape[0]):
        ref[c] = x[:, c * 128 : (c + 1) * 128]


def put_strided(ref, x, start, count, stride):
    for c in range(ref.shape[0]):
        ref[c, pl.ds(start, count, stride=stride), :] = x[:, c * 128 : (c + 1) * 128]


def take(ref):
    return jnp.concatenate([ref[c] for c in range(ref.shape[0])], 1)


def take_strided(ref, start, count, stride):
    return jnp.concatenate(
        [ref[c, pl.ds(start, count, stride=stride), :] for c in range(ref.shape[0])], 1
    )


def expand_kernel(x_ref, w_ref, out_ref):
    rows, cols, channels = x_ref.shape
    normed = half_norm(x_ref[...].reshape(rows * cols, channels).astype(F32)).astype(BF16)
    for c in range(0, w_ref.shape[1], 512):
        hidden = gelu_twice(dot(normed, w_ref[:, c : c + 512])).astype(BF16)
        out_ref[:, :, c : c + 512] = hidden.reshape(rows, cols, 512)


def expand(image, weight, first, count, block=4):
    _, cols, channels = image.shape
    hidden = weight.shape[1]
    return pl.pallas_call(
        expand_kernel,
        grid=(count // block,),
        in_specs=[
            pl.BlockSpec((block, cols, channels), lambda i: (first // block + i, 0, 0)),
            pl.BlockSpec((channels, hidden), lambda i: (0, 0)),
        ],
        out_specs=pl.BlockSpec((block, cols, hidden), lambda i: (i, 0, 0)),
        out_shape=jax.ShapeDtypeStruct((count, cols, hidden), BF16),
        compiler_params=params(16),
        cost_estimate=cost(2 * count * cols * channels * hidden, 2 * count * cols * hidden),
        name="expand",
    )(in_hbm(image), in_hbm(weight))


def flag(held):
    return jnp.where(held, 1.0, 0.0).astype(F32)


def rim_of(normed, w_ref, rim, slot):
    rim[slot] = gelu_twice(dot(normed[...], w_ref[...])).astype(BF16).astype(F32)


def squeeze_sums(sums, red_ref, part_ref):
    parts = exact_dot(sums[...], red_ref[...], ((1,), (1,)))
    part_ref[...] = jnp.broadcast_to(jnp.sum(parts, axis=0, keepdims=True), part_ref.shape)


def conv_kernel(
    upper_ref, lower_ref, over_ref, pair_ref, left_ref, right_ref, first_ref, w_ref, taps_ref,
    red_ref, act_ref, part_ref, normed, rim, left, right, sums,
):
    step = pl.program_id(0)
    core = lax.axis_index("core")
    rows, cols, chunk = act_ref.shape
    slot = step % 2

    @pl.when(step == 0)
    def _():
        row, col = lax.axis_index("row_pair"), lax.axis_index("cols")
        has_over = flag(row + core > 0) * flag(row - (1 - core) < lax.axis_size("row_pair") - 1)
        has_left, has_right = flag(col > 0), flag(col < lax.axis_size("cols") - 1)
        cell = lax.broadcasted_iota(jnp.int32, (80, 1), 0)
        corners = jnp.where(cell == cols, has_left, jnp.where(cell == cols + 1, has_right, 1.0))
        for ref, start, held in (
            (over_ref, 0, corners * has_over),
            (pair_ref, 80, corners),
            (left_ref, 160, has_left),
            (right_ref, 176, has_right),
        ):
            size = ref.shape[0]
            normed[start : start + size, :] = (half_norm(ref[...].astype(F32)) * held).astype(BF16)
        rim_of(normed, first_ref, rim, 0)

    top, bottom = core * 80, (1 - core) * 80
    for ref, start, corner in ((left, 160, 64), (right, 176, 65)):
        ref[0:1, :] = rim[slot, pl.ds(top + corner, 1), :]
        ref[1:17, :] = rim[slot, start : start + 16, :]
        ref[17:18, :] = rim[slot, pl.ds(bottom + corner, 1), :]
    place = lax.broadcasted_iota(jnp.int32, (8, 128), 0)
    for lane in range(0, chunk, 128):
        lanes = slice(lane, lane + 128)
        taps = [0.5 * taps_ref[t : t + 1, lanes].astype(F32) for t in range(9)]
        short = [tap.astype(BF16) for tap in taps]
        before = sum(taps[3 * a] * left[a : a + rows, lanes] for a in range(3))
        after = sum(taps[3 * a + 2] * right[a : a + rows, lanes] for a in range(3))
        total = jnp.zeros((8, 128), F32)

        def line(r):
            if r < 0:
                return rim[slot, pl.ds(pl.multiple_of(top, 8), 64), lanes].astype(BF16)
            if r == rows:
                return rim[slot, pl.ds(pl.multiple_of(bottom, 8), 64), lanes].astype(BF16)
            return upper_ref[r, :, lanes] if r < rows // 2 else lower_ref[r - rows // 2, :, lanes]

        window = [line(-1), line(0), None]
        for r in range(rows):
            window[2] = line(r + 1)
            one = [
                short[b] * window[0] + short[3 + b] * window[1] + short[6 + b] * window[2]
                for b in range(3)
            ]
            one = [line_sum.astype(F32) for line_sum in one]
            down = pltpu.roll(one[0], 1, 0)
            up = pltpu.roll(one[2], cols - 1, 0)
            first = jnp.where(place == 0, before[r : r + 1], down[0:8])
            last = jnp.where(place == 7, after[r : r + 1], up[cols - 8 :])
            whole = (
                one[1]
                + jnp.concatenate([first, down[8:]], 0)
                + jnp.concatenate([up[: cols - 8], last], 0)
            )
            act = gelu_twice(whole)
            act_ref[r, :, lanes] = act.astype(BF16)
            for s in range(0, cols, 8):
                total = total + act[s : s + 8]
            window = [window[1], window[2], None]
        sums[:, pl.ds(pl.multiple_of(step * chunk + lane, 128), 128)] = total
    rim_of(normed, w_ref, rim, 1 - slot)

    @pl.when(step == pl.num_programs(0) - 1)
    def _():
        squeeze_sums(sums, red_ref, part_ref)


def conv(upper, lower, over, pair, left, right, weight, taps, reduce, copies, chunk=256):
    rows, cols, width = upper.shape
    rows = 2 * rows
    channels = weight.shape[0]
    squeezed = reduce.shape[0]
    steps = width // chunk
    whole = lambda a: pl.BlockSpec(a.shape, lambda c: (0, 0))
    return pl.pallas_call(
        conv_kernel,
        grid=(steps,),
        in_specs=[
            pl.BlockSpec((rows // 2, cols, chunk), lambda c: (0, 0, c)),
            pl.BlockSpec((rows // 2, cols, chunk), lambda c: (0, 0, c)),
            whole(over),
            whole(pair),
            whole(left),
            whole(right),
            pl.BlockSpec((channels, chunk), lambda c: (0, 0)),
            pl.BlockSpec((channels, chunk), lambda c: (0, jnp.minimum(c + 1, steps - 1))),
            pl.BlockSpec((9, chunk), lambda c: (0, c)),
            whole(reduce),
        ],
        out_specs=[
            pl.BlockSpec((rows, cols, chunk), lambda c: (0, 0, c)),
            pl.BlockSpec((copies, squeezed), lambda c: (0, 0)),
        ],
        out_shape=[
            jax.ShapeDtypeStruct((rows, cols, width), BF16),
            jax.ShapeDtypeStruct((copies, squeezed), F32),
        ],
        scratch_shapes=[
            pltpu.VMEM((192, channels), BF16),
            pltpu.VMEM((2, 192, chunk), F32),
            pltpu.VMEM((24, chunk), F32),
            pltpu.VMEM((24, chunk), F32),
            pltpu.VMEM((8, width), F32),
        ],
        compiler_params=params(20),
        name="conv",
    )(upper, lower, over, pair, left, right, weight, weight, taps, reduce)


def gate_of(parts_ref, restore_ref, cell_count):
    average = jnp.sum(parts_ref[...], axis=0, keepdims=True) / cell_count
    squeezed = average * jax.nn.sigmoid(average)
    squeezed = jnp.broadcast_to(squeezed, (8, squeezed.shape[1]))
    return jax.nn.sigmoid(exact_dot(squeezed, restore_ref[...], ((1,), (0,))))


def mix(x, qkv_ref, out_ref, up_ref, down_ref):
    cells, channels = x.shape
    width = channels // HEADS
    normed = layer_norm(x).astype(BF16)
    projected = dot(normed, qkv_ref[...])
    queries = (projected[:, :channels] * (1.0 / math.sqrt(width))).astype(BF16)
    keys = projected[:, channels : 2 * channels].astype(BF16)
    values = projected[:, 2 * channels :].astype(BF16)
    lane = lax.broadcasted_iota(jnp.int32, (1, 128), 1)
    masks = [((lane >= h * width) & (lane < (h + 1) * width)).astype(BF16) for h in range(QUAD)]
    groups = []
    for g in range(0, cells, CELLS):
        mine = slice(g, g + CELLS)
        quads = []
        for c in range(0, channels, 128):
            lanes = slice(c, c + 128)
            q, k, v = queries[mine, lanes], keys[mine, lanes], values[mine, lanes]
            stacked = jnp.concatenate([q * m for m in masks], 0)
            scores = lax.dot_general(
                k, stacked, (((1,), (1,)), ((), ())), preferred_element_type=F32
            )
            weights = jnp.exp(scores - jnp.max(scores, axis=0, keepdims=True))
            shares = weights * (1.0 / jnp.sum(weights, axis=0, keepdims=True))
            blended = lax.dot_general(
                shares.astype(BF16), v, (((0,), (0,)), ((), ())), preferred_element_type=F32
            )
            picked = blended[3 * CELLS :]
            for h in (2, 1, 0):
                picked = jnp.where(
                    lane < (h + 1) * width, blended[h * CELLS : (h + 1) * CELLS], picked
                )
            quads.append(picked)
        groups.append(jnp.concatenate(quads, 1).astype(BF16))
    x = x + dot(jnp.concatenate(groups, 0), out_ref[...])
    normed = half_norm(x).astype(BF16)
    for c in range(0, up_ref.shape[1], 512):
        hidden = gelu_twice(dot(normed, up_ref[:, c : c + 512])).astype(BF16)
        x = x + dot(hidden, down_ref[c : c + 512, :])
    return x


def block_kernel(
    img_ref, act_ref, parts_ref, restore_ref, project_ref, qkv_ref, out_ref, up_ref, down_ref,
    res_ref, gate, *, cell_count,
):
    @pl.when(pl.program_id(0) == 0)
    def _():
        gate[...] = gate_of(parts_ref, restore_ref, cell_count)

    rows, cols, channels = img_ref.shape
    scaled = act_ref[...].reshape(rows * cols, act_ref.shape[2]).astype(F32) * gate[0:1, :]
    x = img_ref[...].reshape(rows * cols, channels).astype(F32)
    x = x + dot(scaled.astype(BF16), project_ref[...])
    wide = cols // WIN
    pieces = [
        x[r * cols + g * WIN : r * cols + (g + 1) * WIN] for g in range(wide) for r in range(rows)
    ]
    y = mix(jnp.concatenate(pieces, 0), qkv_ref, out_ref, up_ref, down_ref)
    pieces = [
        y[g * CELLS + r * WIN : g * CELLS + (r + 1) * WIN] for r in range(rows) for g in range(wide)
    ]
    res_ref[...] = jnp.concatenate(pieces, 0).astype(BF16).reshape(rows, cols, channels)


def block_part(image, act, parts, restore, project, qkv, out, up, down, cell_count, wide=64):
    rows, cols, channels = image.shape
    hidden = act.shape[2]
    across = cols // wide
    place = lambda i: (i // across, i % across, 0)
    whole = lambda a: pl.BlockSpec(a.shape, lambda i: (0, 0))
    weights = (restore, project, qkv, out, up, down)

    def kernel(*refs):
        block_kernel(*refs, cell_count=cell_count)

    return pl.pallas_call(
        kernel,
        grid=((rows // WIN) * across,),
        in_specs=[
            pl.BlockSpec((WIN, wide, channels), place),
            pl.BlockSpec((WIN, wide, hidden), place),
            whole(parts),
            *[whole(w) for w in weights],
        ],
        out_specs=pl.BlockSpec((WIN, wide, channels), place),
        out_shape=jax.ShapeDtypeStruct(image.shape, BF16),
        scratch_shapes=[pltpu.VMEM((8, hidden), F32)],
        compiler_params=params(40),
        name="block_part",
    )(image, act, parts, *weights)


def grid_kernel(x_ref, qkv_ref, out_ref, up_ref, down_ref, res_ref, before, after, *, groups):
    step = pl.program_id(0)
    members, held, channels = x_ref.shape

    @pl.when(step == 0)
    def _():
        put(before, x_ref[...].reshape(members * held, channels).astype(F32))

    x = jnp.concatenate(
        [take_strided(before, step * groups + g, members, held) for g in range(groups)], 0
    )
    y = mix(x, qkv_ref, out_ref, up_ref, down_ref)
    for g in range(groups):
        mine = y[g * CELLS : (g + 1) * CELLS]
        put_strided(after, mine, step * groups + g, members, held)

    @pl.when(step == pl.num_programs(0) - 1)
    def _():
        res_ref[...] = take(after).astype(BF16).reshape(members, held, channels)


def grid_part(x, qkv, out, up, down, groups=8):
    members, held, channels = x.shape
    weights = (qkv, out, up, down)

    def kernel(*refs):
        grid_kernel(*refs, groups=groups)

    return pl.pallas_call(
        kernel,
        grid=(held // groups,),
        in_specs=[
            pl.BlockSpec(x.shape, lambda i: (0, 0, 0)),
            *[pl.BlockSpec(w.shape, lambda i: (0, 0)) for w in weights],
        ],
        out_specs=pl.BlockSpec(x.shape, lambda i: (0, 0, 0)),
        out_shape=jax.ShapeDtypeStruct(x.shape, BF16),
        scratch_shapes=[
            panels(members * held, channels),
            panels(members * held, channels),
        ],
        compiler_params=params(40),
        name="grid_part",
    )(x, *weights)


def down_expand_kernel(x_ref, w_ref, out_ref, same_ref, cells):
    rows, cols, channels = x_ref.shape
    same_ref[...] = x_ref[...]
    put(cells, x_ref[...].reshape(rows * cols, channels).astype(F32))
    half = rows * cols // 2
    x = jnp.concatenate([take_strided(cells, parity, half, 2) for parity in range(2)], 0)
    normed = half_norm(x).astype(BF16)
    for c in range(0, w_ref.shape[1], 512):
        hidden = gelu_twice(dot(normed, w_ref[:, c : c + 512])).astype(BF16)
        for parity in range(2):
            out_ref[:, parity, :, c : c + 512] = hidden[parity * half : (parity + 1) * half].reshape(
                rows, cols // 2, 512
            )


def down_expand_part(x, weight, block=4):
    rows, cols, channels = x.shape
    hidden = weight.shape[1]
    return pl.pallas_call(
        down_expand_kernel,
        grid=(rows // block,),
        in_specs=[
            pl.BlockSpec((block, cols, channels), lambda i: (i, 0, 0)),
            pl.BlockSpec((channels, hidden), lambda i: (0, 0)),
        ],
        out_specs=[
            pl.BlockSpec((block, 2, cols // 2, hidden), lambda i: (i, 0, 0, 0)),
            pl.BlockSpec((block, cols, channels), lambda i: (i, 0, 0)),
        ],
        out_shape=[
            jax.ShapeDtypeStruct((rows, 2, cols // 2, hidden), BF16),
            jax.ShapeDtypeStruct(x.shape, BF16),
        ],
        scratch_shapes=[panels(block * cols, channels)],
        compiler_params=params(16),
        cost_estimate=cost(2 * rows * cols * channels * hidden, 2 * rows * cols * hidden),
        name="down_expand",
    )(x, weight)


def down_conv_kernel(
    hid_ref, upper_ref, left_ref, corner_ref, first_ref, w_ref, taps_ref, red_ref,
    act_ref, part_ref, cells, normed, rim, left, sums,
):
    step = pl.program_id(0)
    rows, _, cols, chunk = hid_ref.shape
    slot = step % 2

    @pl.when(step == 0)
    def _():
        row, col = lax.axis_index("row_pair") + lax.axis_index("core"), lax.axis_index("cols")
        has_upper, has_left = flag(row > 0), flag(col > 0)
        put(cells, half_norm(upper_ref[...].astype(F32)) * has_upper)
        normed[0:32, :] = take_strided(cells, 0, 32, 2).astype(BF16)
        normed[32:64, :] = take_strided(cells, 1, 32, 2).astype(BF16)
        normed[64:80, :] = (half_norm(left_ref[...].astype(F32)) * has_left).astype(BF16)
        corner = half_norm(corner_ref[...].astype(F32)) * (has_upper * has_left)
        normed[80:96, :] = jnp.broadcast_to(corner, (16, corner.shape[1])).astype(BF16)
        rim_of(normed, first_ref, rim, 0)

    left[0:1, :] = rim[slot, 80:81, :]
    left[1:17, :] = rim[slot, 64:80, :]
    place = lax.broadcasted_iota(jnp.int32, (8, 128), 0)
    for lane in range(0, chunk, 128):
        lanes = slice(lane, lane + 128)
        taps = [0.5 * taps_ref[t : t + 1, lanes].astype(F32) for t in range(9)]
        before = sum(taps[3 * a] * left[a : a + rows, lanes] for a in range(3))
        total = jnp.zeros((8, 128), F32)

        def line(r, parity):
            if r < 0:
                return rim[slot, 32 * parity : 32 * parity + 32, lanes]
            return hid_ref[r, parity, :, lanes].astype(F32)

        for p in range(rows // 2):
            even = [line(2 * p + a - 1, 0) for a in range(3)]
            odd = [line(2 * p + a - 1, 1) for a in range(3)]
            shifted = sum(taps[3 * a] * odd[a] for a in range(3))
            whole = sum(taps[3 * a + 1] * even[a] + taps[3 * a + 2] * odd[a] for a in range(3))
            shifted = pltpu.roll(shifted, 1, 0)
            first = jnp.where(place == 0, before[2 * p : 2 * p + 1], shifted[0:8])
            act = gelu_twice(whole + jnp.concatenate([first, shifted[8:]], 0))
            act_ref[p, :, lanes] = act.astype(BF16)
            for s in range(0, cols, 8):
                total = total + act[s : s + 8]
        sums[:, pl.ds(pl.multiple_of(step * chunk + lane, 128), 128)] = total
    rim_of(normed, w_ref, rim, 1 - slot)

    @pl.when(step == pl.num_programs(0) - 1)
    def _():
        squeeze_sums(sums, red_ref, part_ref)


def down_conv(hidden, upper, left, corner, weight, taps, reduce, copies, chunk=256):
    rows, _, cols, width = hidden.shape
    channels = weight.shape[0]
    squeezed = reduce.shape[0]
    steps = width // chunk
    whole = lambda a: pl.BlockSpec(a.shape, lambda c: (0, 0))
    return pl.pallas_call(
        down_conv_kernel,
        grid=(steps,),
        in_specs=[
            pl.BlockSpec((rows, 2, cols, chunk), lambda c: (0, 0, 0, c)),
            whole(upper),
            whole(left),
            whole(corner),
            pl.BlockSpec((channels, chunk), lambda c: (0, 0)),
            pl.BlockSpec((channels, chunk), lambda c: (0, jnp.minimum(c + 1, steps - 1))),
            pl.BlockSpec((9, chunk), lambda c: (0, c)),
            whole(reduce),
        ],
        out_specs=[
            pl.BlockSpec((rows // 2, cols, chunk), lambda c: (0, 0, c)),
            pl.BlockSpec((copies, squeezed), lambda c: (0, 0)),
        ],
        out_shape=[
            jax.ShapeDtypeStruct((rows // 2, cols, width), BF16),
            jax.ShapeDtypeStruct((copies, squeezed), F32),
        ],
        scratch_shapes=[
            panels(64, channels),
            pltpu.VMEM((96, channels), BF16),
            pltpu.VMEM((2, 96, chunk), F32),
            pltpu.VMEM((24, chunk), F32),
            pltpu.VMEM((8, width), F32),
        ],
        compiler_params=params(16),
        name="down_conv",
    )(hidden, upper, left, corner, weight, weight, taps, reduce)


def down_out_kernel(
    act_ref, x_ref, parts_ref, restore_ref, project_ref, short_ref, res_ref, cells, *, cell_count
):
    gate = gate_of(parts_ref, restore_ref, cell_count)
    rows, cols, channels = x_ref.shape
    half = cols // 2
    x = x_ref[...].astype(F32).reshape(rows // 2, 2, cols, channels)
    put(cells, (x[:, 0] + x[:, 1]).reshape(rows // 2 * cols, channels))
    count = rows // 2 * half
    pooled = (take_strided(cells, 0, count, 2) + take_strided(cells, 1, count, 2)) * 0.25
    scaled = act_ref[...].reshape(count, act_ref.shape[2]).astype(F32) * gate[0:1, :]
    y = dot(scaled.astype(BF16), project_ref[...]) + dot(pooled.astype(BF16), short_ref[...])
    res_ref[...] = y.astype(BF16).reshape(rows // 2, half, y.shape[1])


def down_out(act, x, parts, restore, project, short, cell_count):
    rows, cols, channels = x.shape
    outs = project.shape[1]

    def kernel(*refs):
        down_out_kernel(*refs, cell_count=cell_count)

    return pl.pallas_call(
        kernel,
        out_shape=jax.ShapeDtypeStruct((rows // 2, cols // 2, outs), BF16),
        scratch_shapes=[panels(rows // 2 * cols, channels)],
        compiler_params=params(24),
        name="down_out",
    )(act, x, parts, restore, project, short)


def shift(x, axes, by):
    size = lax.axis_size(axes)
    return lax.ppermute(x, axes, [(i, (i + by) % size) for i in range(size)])


def shift_both(x):
    rows, cols = lax.axis_size(ROWS), lax.axis_size("cols")
    pairs = [
        (r * cols + c, (r + 1) % rows * cols + (c + 1) % cols)
        for r in range(rows)
        for c in range(cols)
    ]
    return lax.ppermute(x, ALL, pairs)


def sum_parts(part):
    count, squeezed = part.shape
    part = part.reshape(count, 1, squeezed)
    arrived = lax.all_to_all(part, ALL, split_axis=0, concat_axis=0, tiled=True)
    return arrived.reshape(count, squeezed)


def row_rims(image, left, right):
    rows, cols, channels = image.shape
    size = lax.axis_size(ROWS)
    pad = jnp.zeros((14, channels), image.dtype)
    first = jnp.concatenate([image[0], left[:1], right[:1], pad], 0)
    last = jnp.concatenate([image[rows - 1], left[rows - 1 :], right[rows - 1 :], pad], 0)
    even = lax.axis_index("core") == 0
    away = jnp.where(even, first, last)
    near = jnp.where(even, last, first)
    pairs = [(r, (r - 1 if r % 2 == 0 else r + 1) % size) for r in range(size)]
    over = lax.ppermute(away, ROWS, pairs)
    pair = lax.ppermute(near, "core", [(0, 1), (1, 0)])
    return over, pair


def local(
    image,
    mb_expand,
    mb_taps,
    mb_reduce,
    mb_restore,
    mb_project,
    block_qkv,
    block_out,
    first_up,
    first_down,
    grid_qkv,
    grid_out,
    second_up,
    second_down,
    down_expand,
    down_taps,
    down_reduce,
    down_restore,
    down_project,
    down_shortcut,
):
    rows, cols, channels = image.shape
    sharers = lax.axis_size(CLASS)
    all_cells = rows * cols * lax.axis_size(ALL)

    left = shift(image[:, cols - 1], "cols", 1)
    right = shift(image[:, 0], "cols", -1)
    upper = expand(image, mb_expand, 0, rows // 2)
    left, right, upper = lax.optimization_barrier((left, right, upper))
    over, pair = row_rims(image, left, right)
    lower = expand(image, mb_expand, rows // 2, rows // 2)
    act, part = conv(
        upper, lower, over, pair, left, right, mb_expand, mb_taps, mb_reduce.T,
        lax.axis_size(ALL),
    )
    parts = sum_parts(part)
    mixed = block_part(
        image, act, parts, mb_restore, mb_project, block_qkv, block_out, first_up, first_down,
        all_cells,
    )
    held = rows * cols // sharers
    grouped = lax.all_to_all(
        mixed.reshape(sharers, held, channels), CLASS, split_axis=0, concat_axis=0, tiled=True
    )
    grouped = grid_part(grouped, grid_qkv, grid_out, second_up, second_down)
    section = lax.all_to_all(grouped, CLASS, split_axis=0, concat_axis=0, tiled=True)
    section = section.reshape(rows, cols, channels)

    upper = shift(section[rows - 1], ROWS, 1)
    left = shift(section[:, cols - 1], "cols", 1)
    corner = shift_both(section[rows - 1, cols - 1 :])
    hidden, section = down_expand_part(section, down_expand)
    act, part = down_conv(
        hidden, upper, left, corner, down_expand, down_taps, down_reduce.T, lax.axis_size(ALL)
    )
    parts = sum_parts(part)
    downsampled = down_out(
        act, section, parts, down_restore, down_project, down_shortcut, all_cells // 4
    )
    return (section, downsampled)


def solution(mesh):
    rows, cols = mesh.devices.shape
    fine = Mesh(np.asarray(mesh.devices).reshape(rows // 2, 2, cols), ALL)
    tile = P(ROWS, "cols", None)
    in_specs = (tile,) + (P(),) * 19
    return jax.shard_map(
        local, mesh=fine, in_specs=in_specs, out_specs=(tile, tile), check_vma=False
    )
```

```python
import functools
import math

import jax
import jax.numpy as jnp
import numpy as np
from jax import lax
from jax.experimental import pallas as pl
from jax.experimental.pallas import tpu as pltpu
from jax.sharding import Mesh
from jax.sharding import PartitionSpec as P

HEADS = 12
WIN = 8
CELLS = WIN * WIN
QUAD = 4

epsilon = 1e-05
F32 = jnp.float32
BF16 = jnp.bfloat16
ROWS = ("row_pair", "core")
ALL = ("row_pair", "core", "cols")
CLASS = ("row_pair", "cols")


def params(megabytes):
    return pltpu.CompilerParams(vmem_limit_bytes=megabytes << 20)


def resident(kernel, outs, args, scratch, megabytes, work, name, pinned=True, free=()):
    here = pl.BlockSpec(memory_space=pltpu.VMEM)
    args = [
        a if i in free else pltpu.with_memory_space_constraint(a, pltpu.VMEM)
        for i, a in enumerate(args)
    ]
    return pl.pallas_call(
        kernel,
        in_specs=[here] * len(args),
        out_specs=[here] * len(outs),
        out_shape=[(pltpu.VMEM if pinned else jax.ShapeDtypeStruct)(*out) for out in outs],
        scratch_shapes=scratch,
        compiler_params=params(megabytes),
        cost_estimate=pl.CostEstimate(flops=int(work), bytes_accessed=1 << 20, transcendentals=0),
        name=name,
    )(*args)


def gelu_twice(h):
    inner = h * (1.5957691216057308 + 0.285419265090401 * (h * h))
    return h + h * jnp.tanh(inner)


def layer_norm(x, scale=1.0):
    average = jnp.mean(x, axis=-1, keepdims=True)
    centred = x - average
    spread = jnp.mean(centred * centred, axis=-1, keepdims=True)
    return centred * (scale * lax.rsqrt(spread + epsilon))


def half_norm(x):
    return layer_norm(x, 0.5)


def dot(a, b):
    return jnp.dot(a, b, preferred_element_type=F32)


def exact_dot(a, b, dims):
    total = None
    for _ in range(3):
        term = a.astype(BF16)
        a = a - term.astype(F32)
        product = lax.dot_general(term, b, (dims, ((), ())), preferred_element_type=F32)
        total = product if total is None else total + product
    return total


def panels(rows, channels):
    return pltpu.VMEM((channels // 128, rows, 128), F32)


def put(ref, x):
    for c in range(ref.shape[0]):
        ref[c] = x[:, c * 128 : (c + 1) * 128]


def put_strided(ref, x, start, count, stride):
    for c in range(ref.shape[0]):
        ref[c, pl.ds(start, count, stride=stride), :] = x[:, c * 128 : (c + 1) * 128]


def take(ref):
    return jnp.concatenate([ref[c] for c in range(ref.shape[0])], 1)


def take_strided(ref, start, count, stride):
    return jnp.concatenate(
        [ref[c, pl.ds(start, count, stride=stride), :] for c in range(ref.shape[0])], 1
    )


def expand(image, weight, first, count):
    _, cols, channels = image.shape
    hidden = weight.shape[1]

    def kernel(x_hbm, w_hbm, out_ref, x_ref, w_ref, x_sem, w_sem):
        x_copy = pltpu.make_async_copy(x_hbm.at[first : first + count], x_ref, x_sem)
        w_copy = pltpu.make_async_copy(w_hbm, w_ref, w_sem)
        x_copy.start()
        w_copy.start()
        x_copy.wait()
        x = x_ref[...].reshape(count * cols, channels).astype(F32)
        normed = half_norm(x).astype(BF16)
        w_copy.wait()
        for c in range(0, hidden, 256):
            wide = gelu_twice(dot(normed, w_ref[:, c : c + 256])).astype(BF16)
            out_ref[:, :, c : c + 256] = wide.reshape(count, cols, 256)

    away = pl.BlockSpec(memory_space=pl.ANY)
    work = 4 * count * cols * channels * hidden
    return pl.pallas_call(
        kernel,
        in_specs=[away, away],
        out_specs=pl.BlockSpec(memory_space=pltpu.VMEM),
        out_shape=pltpu.VMEM((count, cols, hidden), BF16),
        scratch_shapes=[
            pltpu.VMEM((count, cols, channels), BF16),
            pltpu.VMEM(weight.shape, BF16),
            pltpu.SemaphoreType.DMA,
            pltpu.SemaphoreType.DMA,
        ],
        compiler_params=params(16),
        cost_estimate=pl.CostEstimate(flops=work, bytes_accessed=1 << 20, transcendentals=0),
        name="expand",
    )(*[pltpu.with_memory_space_constraint(a, pltpu.HBM) for a in (image, weight)])


def flag(held):
    return jnp.where(held, 1.0, 0.0).astype(F32)


def rim_of(normed, weight, rim, slot):
    rim[slot] = gelu_twice(dot(normed[...], weight)).astype(BF16).astype(F32)


def squeeze_sums(sums, red_ref, part_ref):
    parts = exact_dot(sums[...], red_ref[...], ((1,), (1,)))
    part_ref[...] = jnp.broadcast_to(jnp.sum(parts, axis=0, keepdims=True), part_ref.shape)


def lanes_at(start, size=128):
    return pl.ds(pl.multiple_of(start, 128), size)


def conv_kernel(
    upper_ref, lower_ref, over_ref, pair_ref, left_ref, right_ref, w_ref, taps_ref, red_ref,
    act_ref, part_ref, normed, rim, left, right, sums, *, chunk,
):
    core = lax.axis_index("core")
    rows, cols, width = act_ref.shape
    steps = width // chunk
    row, col = lax.axis_index("row_pair"), lax.axis_index("cols")
    has_over = flag(row + core > 0) * flag(row - (1 - core) < lax.axis_size("row_pair") - 1)
    has_left, has_right = flag(col > 0), flag(col < lax.axis_size("cols") - 1)
    cell = lax.broadcasted_iota(jnp.int32, (80, 1), 0)
    corners = jnp.where(cell == cols, has_left, jnp.where(cell == cols + 1, has_right, 1.0))
    for ref, start, held in (
        (over_ref, 0, corners * has_over),
        (pair_ref, 80, corners),
        (left_ref, 160, has_left),
        (right_ref, 176, has_right),
    ):
        size = ref.shape[0]
        normed[start : start + size, :] = (half_norm(ref[...].astype(F32)) * held).astype(BF16)
    rim_of(normed, w_ref[:, :chunk], rim, 0)
    top, bottom = core * 80, (1 - core) * 80
    place = lax.broadcasted_iota(jnp.int32, (8, 128), 0)

    def advance(step, carry):
        slot = step % 2
        for ref, start, corner in ((left, 160, 64), (right, 176, 65)):
            ref[0:1, :] = rim[slot, pl.ds(top + corner, 1), :]
            ref[1:17, :] = rim[slot, start : start + 16, :]
            ref[17:18, :] = rim[slot, pl.ds(bottom + corner, 1), :]
        for lane in range(0, chunk, 128):
            lanes = slice(lane, lane + 128)
            wide = lanes_at(step * chunk + lane)
            taps = [0.5 * taps_ref[t : t + 1, wide].astype(F32) for t in range(9)]
            short = [tap.astype(BF16) for tap in taps]
            before = sum(taps[3 * a] * left[a : a + rows, lanes] for a in range(3))
            after = sum(taps[3 * a + 2] * right[a : a + rows, lanes] for a in range(3))
            total = jnp.zeros((8, 128), F32)

            def line(r):
                if r < 0:
                    return rim[slot, pl.ds(pl.multiple_of(top, 8), 64), lanes].astype(BF16)
                if r == rows:
                    return rim[slot, pl.ds(pl.multiple_of(bottom, 8), 64), lanes].astype(BF16)
                return upper_ref[r, :, wide] if r < rows // 2 else lower_ref[r - rows // 2, :, wide]

            window = [line(-1), line(0), None]
            for r in range(rows):
                window[2] = line(r + 1)
                one = [
                    short[b] * window[0] + short[3 + b] * window[1] + short[6 + b] * window[2]
                    for b in range(3)
                ]
                one = [line_sum.astype(F32) for line_sum in one]
                down = pltpu.roll(one[0], 1, 0)
                up = pltpu.roll(one[2], cols - 1, 0)
                first = jnp.where(place == 0, before[r : r + 1], down[0:8])
                last = jnp.where(place == 7, after[r : r + 1], up[cols - 8 :])
                whole = (
                    one[1]
                    + jnp.concatenate([first, down[8:]], 0)
                    + jnp.concatenate([up[: cols - 8], last], 0)
                )
                act = gelu_twice(whole)
                act_ref[r, :, wide] = act.astype(BF16)
                for s in range(0, cols, 8):
                    total = total + act[s : s + 8]
                window = [window[1], window[2], None]
            sums[:, wide] = total
        later = jnp.minimum(step + 1, steps - 1) * chunk
        rim_of(normed, w_ref[:, lanes_at(later, chunk)], rim, 1 - slot)
        return carry

    lax.fori_loop(0, steps, advance, 0)
    squeeze_sums(sums, red_ref, part_ref)


def conv(upper, lower, over, pair, left, right, weight, taps, reduce, copies, chunk=256):
    half, cols, width = upper.shape
    channels = weight.shape[0]
    outs = [((2 * half, cols, width), BF16), ((copies, reduce.shape[0]), F32)]
    scratch = [
        pltpu.VMEM((192, channels), BF16),
        pltpu.VMEM((2, 192, chunk), F32),
        pltpu.VMEM((24, chunk), F32),
        pltpu.VMEM((24, chunk), F32),
        pltpu.VMEM((8, width), F32),
    ]
    args = (upper, lower, over, pair, left, right, weight, taps, reduce)
    kernel = functools.partial(conv_kernel, chunk=chunk)
    return resident(kernel, outs, args, scratch, 8, 8e9, "conv")


def gate_of(parts_ref, restore_ref, cell_count):
    average = jnp.sum(parts_ref[...], axis=0, keepdims=True) / cell_count
    squeezed = average * jax.nn.sigmoid(average)
    squeezed = jnp.broadcast_to(squeezed, (8, squeezed.shape[1]))
    return jax.nn.sigmoid(exact_dot(squeezed, restore_ref[...], ((1,), (0,))))


def mix(x, qkv_ref, out_ref, up_ref, down_ref):
    cells, channels = x.shape
    width = channels // HEADS
    normed = layer_norm(x).astype(BF16)
    projected = dot(normed, qkv_ref[...])
    queries = (projected[:, :channels] * (1.0 / math.sqrt(width))).astype(BF16)
    keys = projected[:, channels : 2 * channels].astype(BF16)
    values = projected[:, 2 * channels :].astype(BF16)
    lane = lax.broadcasted_iota(jnp.int32, (1, 128), 1)
    masks = [((lane >= h * width) & (lane < (h + 1) * width)).astype(BF16) for h in range(QUAD)]
    groups = []
    for g in range(0, cells, CELLS):
        mine = slice(g, g + CELLS)
        quads = []
        for c in range(0, channels, 128):
            lanes = slice(c, c + 128)
            q, k, v = queries[mine, lanes], keys[mine, lanes], values[mine, lanes]
            stacked = jnp.concatenate([q * m for m in masks], 0)
            scores = lax.dot_general(
                k, stacked, (((1,), (1,)), ((), ())), preferred_element_type=F32
            )
            weights = jnp.exp(scores - jnp.max(scores, axis=0, keepdims=True))
            shares = weights * (1.0 / jnp.sum(weights, axis=0, keepdims=True))
            blended = lax.dot_general(
                shares.astype(BF16), v, (((0,), (0,)), ((), ())), preferred_element_type=F32
            )
            picked = blended[3 * CELLS :]
            for h in (2, 1, 0):
                picked = jnp.where(
                    lane < (h + 1) * width, blended[h * CELLS : (h + 1) * CELLS], picked
                )
            quads.append(picked)
        groups.append(jnp.concatenate(quads, 1).astype(BF16))
    x = x + dot(jnp.concatenate(groups, 0), out_ref[...])
    normed = half_norm(x).astype(BF16)
    for c in range(0, up_ref.shape[1], 512):
        hidden = gelu_twice(dot(normed, up_ref[:, c : c + 512])).astype(BF16)
        x = x + dot(hidden, down_ref[c : c + 512, :])
    return x


def block_kernel(
    img_ref, act_ref, parts_ref, restore_ref, project_ref, qkv_ref, out_ref, up_ref, down_ref,
    res_ref, *, cell_count,
):
    rows, cols, channels = img_ref.shape
    cells = WIN * cols
    wide = cols // WIN
    gate = gate_of(parts_ref, restore_ref, cell_count)
    for strip in range(rows // WIN):
        mine = slice(strip * WIN, (strip + 1) * WIN)
        scaled = act_ref[mine].reshape(cells, act_ref.shape[2]).astype(F32) * gate[0:1, :]
        x = img_ref[mine].reshape(cells, channels).astype(F32)
        x = x + dot(scaled.astype(BF16), project_ref[...])
        pieces = [
            x[r * cols + g * WIN : r * cols + (g + 1) * WIN]
            for g in range(wide)
            for r in range(WIN)
        ]
        y = mix(jnp.concatenate(pieces, 0), qkv_ref, out_ref, up_ref, down_ref)
        pieces = [
            y[g * CELLS + r * WIN : g * CELLS + (r + 1) * WIN]
            for r in range(WIN)
            for g in range(wide)
        ]
        res_ref[strip * cells : (strip + 1) * cells, :] = jnp.concatenate(pieces, 0).astype(BF16)


def block_part(image, act, parts, restore, project, qkv, out, up, down, cell_count):
    rows, cols, channels = image.shape
    outs = [((rows * cols, channels), BF16)]
    args = (image, act, parts, restore, project, qkv, out, up, down)
    kernel = functools.partial(block_kernel, cell_count=cell_count)
    return resident(kernel, outs, args, [], 24, 12e9, "block_part")[0]


def grid_kernel(x_ref, qkv_ref, out_ref, up_ref, down_ref, res_ref, before, after, *, batch):
    groups = x_ref.shape[0] // CELLS
    put(before, x_ref[...].astype(F32))
    for start in range(0, groups, batch):
        x = [take_strided(before, start + g, CELLS, groups) for g in range(batch)]
        y = mix(jnp.concatenate(x, 0), qkv_ref, out_ref, up_ref, down_ref)
        for g in range(batch):
            put_strided(after, y[g * CELLS : (g + 1) * CELLS], start + g, CELLS, groups)
    res_ref[...] = take(after).astype(BF16)


def grid_part(x, qkv, out, up, down, batch=8):
    scratch = [panels(*x.shape), panels(*x.shape)]
    args = (x, qkv, out, up, down)
    kernel = functools.partial(grid_kernel, batch=batch)
    return resident(kernel, [(x.shape, BF16)], args, scratch, 24, 10e9, "grid_part")[0]


def down_expand_kernel(x_ref, w_ref, out_ref, pool_ref, cells, *, block):
    rows, cols, channels = x_ref.shape
    put(cells, x_ref[...].reshape(rows * cols, channels).astype(F32))
    half = block * cols // 2
    for start in range(0, rows, block):
        x = [take_strided(cells, start * cols + parity, half, 2) for parity in range(2)]
        pairs = (x[0] + x[1]).reshape(block // 2, 2, cols // 2, channels)
        pool = 0.25 * (pairs[:, 0] + pairs[:, 1])
        pool_ref[start // 2 : (start + block) // 2] = pool.astype(BF16)
        normed = half_norm(jnp.concatenate(x, 0)).astype(BF16)
        for c in range(0, w_ref.shape[1], 256):
            hidden = gelu_twice(dot(normed, w_ref[:, c : c + 256])).astype(BF16)
            for parity in range(2):
                mine = hidden[parity * half : (parity + 1) * half]
                out_ref[start : start + block, parity, :, c : c + 256] = mine.reshape(
                    block, cols // 2, 256
                )


def down_expand_part(x, weight, block=8):
    rows, cols, channels = x.shape
    hidden = weight.shape[1]
    outs = [((rows, 2, cols // 2, hidden), BF16), ((rows // 2, cols // 2, channels), BF16)]
    work = 4 * rows * cols * channels * hidden
    scratch = [panels(rows * cols, channels)]
    kernel = functools.partial(down_expand_kernel, block=block)
    return resident(kernel, outs, (x, weight), scratch, 8, work, "down_expand")


def down_conv_kernel(
    hid_ref, sec_ref, upper_ref, left_ref, corner_ref, w_ref, taps_ref,
    red_ref, act_ref, part_ref, section_ref, cells, normed, rim, left, sums, sem, *, chunk,
):
    rows, _, cols, width = hid_ref.shape
    steps = width // chunk
    copy = pltpu.make_async_copy(sec_ref, section_ref, sem)
    copy.start()
    row, col = lax.axis_index("row_pair") + lax.axis_index("core"), lax.axis_index("cols")
    has_upper, has_left = flag(row > 0), flag(col > 0)
    put(cells, half_norm(upper_ref[...].astype(F32)) * has_upper)
    normed[0:32, :] = take_strided(cells, 0, 32, 2).astype(BF16)
    normed[32:64, :] = take_strided(cells, 1, 32, 2).astype(BF16)
    normed[64:80, :] = (half_norm(left_ref[...].astype(F32)) * has_left).astype(BF16)
    corner = half_norm(corner_ref[...].astype(F32)) * (has_upper * has_left)
    normed[80:96, :] = jnp.broadcast_to(corner, (16, corner.shape[1])).astype(BF16)
    rim_of(normed, w_ref[:, :chunk], rim, 0)
    place = lax.broadcasted_iota(jnp.int32, (8, 128), 0)

    def advance(step, carry):
        slot = step % 2
        left[0:1, :] = rim[slot, 80:81, :]
        left[1:17, :] = rim[slot, 64:80, :]
        for lane in range(0, chunk, 128):
            lanes = slice(lane, lane + 128)
            wide = lanes_at(step * chunk + lane)
            taps = [0.5 * taps_ref[t : t + 1, wide].astype(F32) for t in range(9)]
            before = sum(taps[3 * a] * left[a : a + rows, lanes] for a in range(3))
            total = jnp.zeros((8, 128), F32)

            def line(r, parity):
                if r < 0:
                    return rim[slot, 32 * parity : 32 * parity + 32, lanes]
                return hid_ref[r, parity, :, wide].astype(F32)

            for p in range(rows // 2):
                even = [line(2 * p + a - 1, 0) for a in range(3)]
                odd = [line(2 * p + a - 1, 1) for a in range(3)]
                shifted = sum(taps[3 * a] * odd[a] for a in range(3))
                whole = sum(taps[3 * a + 1] * even[a] + taps[3 * a + 2] * odd[a] for a in range(3))
                shifted = pltpu.roll(shifted, 1, 0)
                first = jnp.where(place == 0, before[2 * p : 2 * p + 1], shifted[0:8])
                act = gelu_twice(whole + jnp.concatenate([first, shifted[8:]], 0))
                act_ref[p, :, wide] = act.astype(BF16)
                for s in range(0, cols, 8):
                    total = total + act[s : s + 8]
            sums[:, wide] = total
        later = jnp.minimum(step + 1, steps - 1) * chunk
        rim_of(normed, w_ref[:, lanes_at(later, chunk)], rim, 1 - slot)
        return carry

    lax.fori_loop(0, steps, advance, 0)
    squeeze_sums(sums, red_ref, part_ref)
    copy.wait()


def down_conv(hidden, section, upper, left, corner, weight, taps, reduce, copies, chunk=256):
    rows, _, cols, width = hidden.shape
    channels = weight.shape[0]
    here = pl.BlockSpec(memory_space=pltpu.VMEM)
    args = (hidden, section, upper, left, corner, weight, taps, reduce)
    return pl.pallas_call(
        functools.partial(down_conv_kernel, chunk=chunk),
        in_specs=[here] * len(args),
        out_specs=[here, here, pl.BlockSpec(memory_space=pl.ANY)],
        out_shape=[
            pltpu.VMEM((rows // 2, cols, width), BF16),
            pltpu.VMEM((copies, reduce.shape[0]), F32),
            jax.ShapeDtypeStruct((rows, 2 * cols, channels), BF16),
        ],
        scratch_shapes=[
            panels(64, channels),
            pltpu.VMEM((96, channels), BF16),
            pltpu.VMEM((2, 96, chunk), F32),
            pltpu.VMEM((24, chunk), F32),
            pltpu.VMEM((8, width), F32),
            pltpu.SemaphoreType.DMA,
        ],
        compiler_params=params(8),
        name="down_conv",
    )(*[pltpu.with_memory_space_constraint(a, pltpu.VMEM) for a in args])


def down_out(act, pooled, parts, restore, project, short, cell_count):
    rows, cols, hidden = act.shape
    outs = project.shape[1]
    count = rows * cols // 2

    def kernel(act_ref, pool_ref, parts_ref, restore_ref, project_ref, short_ref, res_ref):
        gate = gate_of(parts_ref, restore_ref, cell_count)
        for i in range(2):
            mine = slice(i * rows // 2, (i + 1) * rows // 2)
            scaled = act_ref[mine].reshape(count, hidden).astype(F32) * gate[0:1, :]
            pool = pool_ref[mine].reshape(count, pool_ref.shape[2])
            y = dot(scaled.astype(BF16), project_ref[...]) + dot(pool, short_ref[...])
            res_ref[mine] = y.astype(BF16).reshape(rows // 2, cols, outs)

    here = pl.BlockSpec(memory_space=pltpu.VMEM)
    args = (act, pooled, parts, restore, project, short)
    return pl.pallas_call(
        kernel,
        in_specs=[here] * len(args),
        out_specs=here,
        out_shape=jax.ShapeDtypeStruct((rows, cols, outs), BF16),
        compiler_params=params(8),
        name="down_out",
    )(*[pltpu.with_memory_space_constraint(a, pltpu.VMEM) for a in args])


def shift(x, axes, by):
    size = lax.axis_size(axes)
    return lax.ppermute(x, axes, [(i, (i + by) % size) for i in range(size)])


def shift_both(x):
    rows, cols = lax.axis_size(ROWS), lax.axis_size("cols")
    pairs = [
        (r * cols + c, (r + 1) % rows * cols + (c + 1) % cols)
        for r in range(rows)
        for c in range(cols)
    ]
    return lax.ppermute(x, ALL, pairs)


def exchange(x):
    cells, channels = x.shape
    sharers = lax.axis_size(CLASS)
    pieces = x.reshape(sharers, cells // sharers, channels)
    pieces = lax.all_to_all(pieces, CLASS, split_axis=0, concat_axis=0, tiled=True)
    return pieces.reshape(cells, channels)


def sum_parts(part):
    count, squeezed = part.shape
    part = part.reshape(count, 1, squeezed)
    arrived = lax.all_to_all(part, ALL, split_axis=0, concat_axis=0, tiled=True)
    return arrived.reshape(count, squeezed)


def row_rims(image, left, right):
    rows, cols, channels = image.shape
    size = lax.axis_size(ROWS)
    pad = jnp.zeros((14, channels), image.dtype)
    first = jnp.concatenate([image[0], left[:1], right[:1], pad], 0)
    last = jnp.concatenate([image[rows - 1], left[rows - 1 :], right[rows - 1 :], pad], 0)
    even = lax.axis_index("core") == 0
    away = jnp.where(even, first, last)
    near = jnp.where(even, last, first)
    pairs = [(r, (r - 1 if r % 2 == 0 else r + 1) % size) for r in range(size)]
    over = lax.ppermute(away, ROWS, pairs)
    pair = lax.ppermute(near, "core", [(0, 1), (1, 0)])
    return over, pair


def local(
    image,
    mb_expand,
    mb_taps,
    mb_reduce,
    mb_restore,
    mb_project,
    block_qkv,
    block_out,
    first_up,
    first_down,
    grid_qkv,
    grid_out,
    second_up,
    second_down,
    down_expand,
    down_taps,
    down_reduce,
    down_restore,
    down_project,
    down_shortcut,
):
    rows, cols, channels = image.shape
    all_cells = rows * cols * lax.axis_size(ALL)

    left = shift(image[:, cols - 1], "cols", 1)
    right = shift(image[:, 0], "cols", -1)
    upper = expand(image, mb_expand, 0, rows // 2)
    left, right, upper = lax.optimization_barrier((left, right, upper))
    over, pair = row_rims(image, left, right)
    lower = expand(image, mb_expand, rows // 2, rows // 2)
    act, part = conv(
        upper, lower, over, pair, left, right, mb_expand, mb_taps, mb_reduce.T,
        lax.axis_size(ALL),
    )
    parts = sum_parts(part)
    mixed = block_part(
        image, act, parts, mb_restore, mb_project, block_qkv, block_out, first_up, first_down,
        all_cells,
    )
    mixed = grid_part(exchange(mixed), grid_qkv, grid_out, second_up, second_down)
    section = exchange(mixed).reshape(rows, cols, channels)

    upper = shift(section[rows - 1], ROWS, 1)
    left = shift(section[:, cols - 1], "cols", 1)
    corner = shift_both(section[rows - 1, cols - 1 :])
    hidden, pooled = down_expand_part(section, down_expand)
    act, part, whole = down_conv(
        hidden, section, upper, left, corner, down_expand, down_taps, down_reduce.T,
        lax.axis_size(ALL),
    )
    parts = sum_parts(part)
    downsampled = down_out(
        act, pooled, parts, down_restore, down_project, down_shortcut, all_cells // 4
    )
    return (whole, downsampled)


def solution(mesh):
    rows, cols = mesh.devices.shape
    fine = Mesh(np.asarray(mesh.devices).reshape(rows // 2, 2, cols), ALL)
    tile = P(ROWS, "cols", None)
    in_specs = (tile,) + (P(),) * 19
    return jax.shard_map(
        local, mesh=fine, in_specs=in_specs, out_specs=(tile, tile), check_vma=False
    )
```

```python
import functools
import math

import jax
import jax.numpy as jnp
import numpy as np
from jax import lax
from jax.experimental import pallas as pl
from jax.experimental.pallas import tpu as pltpu
from jax.sharding import Mesh
from jax.sharding import PartitionSpec as P

HEADS = 12
WIN = 8
CELLS = WIN * WIN
QUAD = 4

epsilon = 1e-05
F32 = jnp.float32
BF16 = jnp.bfloat16
ROWS = ("row_pair", "core")
COLS = ("depth", "col_pair")
AXES = ("row_pair", "core", "depth", "col_pair")
ALL = ("core", "row_pair", "col_pair", "depth")
CLASS = ("row_pair", "col_pair", "depth")


def params(megabytes):
    return pltpu.CompilerParams(vmem_limit_bytes=megabytes << 20)


def resident(kernel, outs, args, scratch, megabytes, work, name):
    here = pl.BlockSpec(memory_space=pltpu.VMEM)
    args = [pltpu.with_memory_space_constraint(a, pltpu.VMEM) for a in args]
    return pl.pallas_call(
        kernel,
        in_specs=[here] * len(args),
        out_specs=[here] * len(outs),
        out_shape=[pltpu.VMEM(*out) for out in outs],
        scratch_shapes=scratch,
        compiler_params=params(megabytes),
        cost_estimate=pl.CostEstimate(flops=int(work), bytes_accessed=1 << 20, transcendentals=0),
        name=name,
    )(*args)


def gelu_twice(h):
    inner = h * (1.5957691216057308 + 0.285419265090401 * (h * h))
    return h + h * jnp.tanh(inner)


def layer_norm(x, scale=1.0):
    average = jnp.mean(x, axis=-1, keepdims=True)
    centred = x - average
    spread = jnp.mean(centred * centred, axis=-1, keepdims=True)
    return centred * (scale * lax.rsqrt(spread + epsilon))


def half_norm(x):
    return layer_norm(x, 0.5)


def dot(a, b):
    return jnp.dot(a, b, preferred_element_type=F32)


def exact_dot(a, b, dims):
    total = None
    for _ in range(3):
        term = a.astype(BF16)
        a = a - term.astype(F32)
        product = lax.dot_general(term, b, (dims, ((), ())), preferred_element_type=F32)
        total = product if total is None else total + product
    return total


def panels(rows, channels):
    return pltpu.VMEM((channels // 128, rows, 128), F32)


def put(ref, x):
    for c in range(ref.shape[0]):
        ref[c] = x[:, c * 128 : (c + 1) * 128]


def put_strided(ref, x, start, count, stride):
    for c in range(ref.shape[0]):
        ref[c, pl.ds(start, count, stride=stride), :] = x[:, c * 128 : (c + 1) * 128]


def take(ref):
    return jnp.concatenate([ref[c] for c in range(ref.shape[0])], 1)


def take_strided(ref, start, count, stride):
    return jnp.concatenate(
        [ref[c, pl.ds(start, count, stride=stride), :] for c in range(ref.shape[0])], 1
    )


def expand_kernel(x_ref, w_ref, out_ref, near_ref, first_ref, last_ref):
    step = pl.program_id(0)
    rows, cols, channels = x_ref.shape
    normed = half_norm(x_ref[...].reshape(rows * cols, channels).astype(F32)).astype(BF16)
    for c in range(0, w_ref.shape[1], 256):
        wide = gelu_twice(dot(normed, w_ref[:, c : c + 256])).astype(BF16)
        out_ref[:, :, c : c + 256] = wide.reshape(rows, cols, 256)

    @pl.when(step == 0)
    def _():
        near_ref[0:2] = out_ref[0:2]
        first_ref[...] = x_ref[0]

    @pl.when(step == pl.num_programs(0) - 1)
    def _():
        near_ref[2:4] = out_ref[rows - 2 : rows]
        last_ref[...] = x_ref[rows - 1]


def expand(image, weight, block=4):
    rows, cols, channels = image.shape
    hidden = weight.shape[1]
    still = lambda *shape: pl.BlockSpec(shape, lambda i: (0,) * len(shape))
    return pl.pallas_call(
        expand_kernel,
        grid=(rows // block,),
        in_specs=[
            pl.BlockSpec((block, cols, channels), lambda i: (i, 0, 0)),
            still(channels, hidden),
        ],
        out_specs=[
            pl.BlockSpec((block, cols, hidden), lambda i: (i, 0, 0)),
            still(4, cols, hidden),
            still(cols, channels),
            still(cols, channels),
        ],
        out_shape=[
            pltpu.HBM((rows, cols, hidden), BF16),
            jax.ShapeDtypeStruct((4, cols, hidden), BF16),
            jax.ShapeDtypeStruct((cols, channels), BF16),
            jax.ShapeDtypeStruct((cols, channels), BF16),
        ],
        compiler_params=params(16),
        cost_estimate=pl.CostEstimate(flops=int(4e9), bytes_accessed=1 << 20, transcendentals=0),
        name="expand",
    )(*[pltpu.with_memory_space_constraint(a, pltpu.HBM) for a in (image, weight)])


def flag(held):
    return jnp.where(held, 1.0, 0.0).astype(F32)


def rim_of(normed, weight, rim, slot):
    rim[slot] = gelu_twice(dot(normed[...], weight)).astype(BF16).astype(F32)


def squeeze_sums(sums, red_ref, part_ref):
    parts = exact_dot(sums[...], red_ref[...], ((1,), (1,)))
    part_ref[...] = jnp.broadcast_to(jnp.sum(parts, axis=0, keepdims=True), part_ref.shape)


def lanes_at(start, size=128):
    return pl.ds(pl.multiple_of(start, 128), size)


def conv_row(lines, short, before, after, place):
    cols = lines[0].shape[0]
    one = [
        (short[b] * lines[0] + short[3 + b] * lines[1] + short[6 + b] * lines[2]).astype(F32)
        for b in range(3)
    ]
    down = pltpu.roll(one[0], 1, 0)
    up = pltpu.roll(one[2], cols - 1, 0)
    first = jnp.where(place == 0, before, down[0:8])
    last = jnp.where(place == 7, after, up[cols - 8 :])
    whole = (
        one[1]
        + jnp.concatenate([first, down[8:]], 0)
        + jnp.concatenate([up[: cols - 8], last], 0)
    )
    act = gelu_twice(whole)
    return act, sum(act[s : s + 8] for s in range(0, cols, 8))


def half_taps(taps_ref, wide):
    taps = [0.5 * taps_ref[t : t + 1, wide].astype(F32) for t in range(9)]
    return taps, [tap.astype(BF16) for tap in taps]


def side_norms(normed, start, left_ref, right_ref):
    col = lax.axis_index(COLS)
    has_left, has_right = flag(col > 0), flag(col < lax.axis_size(COLS) - 1)
    for ref, at, held in ((left_ref, start, has_left), (right_ref, start + 16, has_right)):
        normed[at : at + 16, :] = (half_norm(ref[...].astype(F32)) * held).astype(BF16)
    return has_left, has_right


def inner_kernel(
    hid_ref, left_ref, right_ref, start_ref, w_ref, taps_ref, act_ref, sums_ref, normed, rim
):
    step = pl.program_id(0)
    rows, cols, chunk = hid_ref.shape
    slot = step % 2

    @pl.when(step == 0)
    def _():
        side_norms(normed, 0, left_ref, right_ref)
        rim_of(normed, start_ref[...], rim, 0)

    place = lax.broadcasted_iota(jnp.int32, (8, 128), 0)
    inner = rows - 2
    for lane in range(0, chunk, 128):
        lanes = slice(lane, lane + 128)
        taps, short = half_taps(taps_ref, lanes)
        before = sum(taps[3 * a] * rim[slot, a : a + inner, lanes] for a in range(3))
        after = sum(taps[3 * a + 2] * rim[slot, 16 + a : 16 + a + inner, lanes] for a in range(3))
        total = jnp.zeros((8, 128), F32)
        lines = [hid_ref[0, :, lanes], hid_ref[1, :, lanes], None]
        for r in range(1, rows - 1):
            lines[2] = hid_ref[r + 1, :, lanes]
            act, part = conv_row(lines, short, before[r - 1 : r], after[r - 1 : r], place)
            act_ref[r, :, lanes] = act.astype(BF16)
            total = total + part
            lines = [lines[1], lines[2], None]
        sums_ref[:, lanes] = total
    rim_of(normed, w_ref[...], rim, 1 - slot)


def conv_inner(hidden, left, right, weight, taps, chunk=256):
    rows, cols, width = hidden.shape
    channels = weight.shape[0]
    steps = width // chunk
    whole = lambda a: pl.BlockSpec(a.shape, lambda c: (0, 0))
    tall = pl.BlockSpec((rows, cols, chunk), lambda c: (0, 0, c))
    return pl.pallas_call(
        inner_kernel,
        grid=(steps,),
        in_specs=[
            tall,
            whole(left),
            whole(right),
            pl.BlockSpec((channels, chunk), lambda c: (0, 0)),
            pl.BlockSpec((channels, chunk), lambda c: (0, jnp.minimum(c + 1, steps - 1))),
            pl.BlockSpec((9, chunk), lambda c: (0, c)),
        ],
        out_specs=[tall, pl.BlockSpec((8, chunk), lambda c: (0, c))],
        out_shape=[jax.ShapeDtypeStruct(hidden.shape, BF16), jax.ShapeDtypeStruct((8, width), F32)],
        scratch_shapes=[pltpu.VMEM((32, channels), BF16), pltpu.VMEM((2, 32, chunk), F32)],
        compiler_params=params(16),
        cost_estimate=pl.CostEstimate(flops=int(7e9), bytes_accessed=1 << 20, transcendentals=0),
        name="conv_inner",
    )(
        pltpu.with_memory_space_constraint(hidden, pltpu.HBM), left, right, weight, weight, taps
    )


def outer_kernel(
    near_ref, over_ref, pair_ref, left_ref, right_ref, w_ref, taps_ref, red_ref, sums_ref,
    act_ref, part_ref, normed, rim, sums, *, chunk,
):
    _, cols, width = near_ref.shape
    steps = width // chunk
    row, core = lax.axis_index("row_pair"), lax.axis_index("core")
    has_over = flag(row + core > 0) * flag(row - (1 - core) < lax.axis_size("row_pair") - 1)
    has_left, has_right = side_norms(normed, 160, left_ref, right_ref)
    cell = lax.broadcasted_iota(jnp.int32, (80, 1), 0)
    corners = jnp.where(cell == cols, has_left, jnp.where(cell == cols + 1, has_right, 1.0))
    for ref, start, held in ((over_ref, 0, corners * has_over), (pair_ref, 80, corners)):
        normed[start : start + 80, :] = (half_norm(ref[...].astype(F32)) * held).astype(BF16)
    rim_of(normed, w_ref[:, :chunk], rim, 0)
    top, bottom = core * 80, (1 - core) * 80
    place = lax.broadcasted_iota(jnp.int32, (8, 128), 0)

    def advance(step, carry):
        slot = step % 2
        for lane in range(0, chunk, 128):
            lanes = slice(lane, lane + 128)
            wide = lanes_at(step * chunk + lane)
            taps, short = half_taps(taps_ref, wide)

            def cells(at, side):
                return rim[slot, pl.ds(pl.multiple_of(at, 8), 8), lanes][side : side + 1]

            def line(at):
                return rim[slot, pl.ds(pl.multiple_of(at, 8), 64), lanes].astype(BF16)

            total = sums_ref[:, wide]
            near = [near_ref[r, :, wide] for r in range(4)]
            edges = (
                ([line(top), near[0], near[1]], (top, 0), (160, 161)),
                ([near[2], near[3], line(bottom)], (bottom, 2), (174, 175)),
            )
            for i, (lines, (corner, turn), (one, two)) in enumerate(edges):
                beside = [[], []]
                for side in range(2):
                    beside[side].append(cells(corner + 64, side))
                    for at in (one, two):
                        beside[side].append(rim[slot, at + 16 * side : at + 16 * side + 1, lanes])
                before, after = [
                    sum(taps[3 * ((a + turn) % 3) + 2 * side] * beside[side][a] for a in range(3))
                    for side in range(2)
                ]
                act, part = conv_row(lines, short, before, after, place)
                act_ref[i, :, wide] = act.astype(BF16)
                total = total + part
            sums[:, wide] = total
        later = jnp.minimum(step + 1, steps - 1) * chunk
        rim_of(normed, w_ref[:, lanes_at(later, chunk)], rim, 1 - slot)
        return carry

    lax.fori_loop(0, steps, advance, 0)
    squeeze_sums(sums, red_ref, part_ref)


def conv_outer(near, over, pair, left, right, weight, taps, reduce, sums, copies, chunk=256):
    _, cols, width = near.shape
    channels = weight.shape[0]
    outs = [((2, cols, width), BF16), ((copies, reduce.shape[0]), F32)]
    scratch = [
        pltpu.VMEM((192, channels), BF16),
        pltpu.VMEM((2, 192, chunk), F32),
        pltpu.VMEM((8, width), F32),
    ]
    args = (near, over, pair, left, right, weight, taps, reduce, sums)
    kernel = functools.partial(outer_kernel, chunk=chunk)
    return resident(kernel, outs, args, scratch, 16, 2e9, "conv_outer")


def gate_of(parts_ref, restore_ref, cell_count):
    average = jnp.sum(parts_ref[...], axis=0, keepdims=True) / cell_count
    squeezed = average * jax.nn.sigmoid(average)
    squeezed = jnp.broadcast_to(squeezed, (8, squeezed.shape[1]))
    return jax.nn.sigmoid(exact_dot(squeezed, restore_ref[...], ((1,), (0,))))


def attend(x, qkv_ref, out_ref):
    cells, channels = x.shape
    width = channels // HEADS
    normed = layer_norm(x).astype(BF16)
    projected = dot(normed, qkv_ref[...])
    queries = (projected[:, :channels] * (1.0 / math.sqrt(width))).astype(BF16)
    keys = projected[:, channels : 2 * channels].astype(BF16)
    values = projected[:, 2 * channels :].astype(BF16)
    lane = lax.broadcasted_iota(jnp.int32, (1, 128), 1)
    masks = [((lane >= h * width) & (lane < (h + 1) * width)).astype(BF16) for h in range(QUAD)]
    groups = []
    for g in range(0, cells, CELLS):
        mine = slice(g, g + CELLS)
        quads = []
        for c in range(0, channels, 128):
            lanes = slice(c, c + 128)
            q, k, v = queries[mine, lanes], keys[mine, lanes], values[mine, lanes]
            stacked = jnp.concatenate([q * m for m in masks], 0)
            scores = lax.dot_general(
                k, stacked, (((1,), (1,)), ((), ())), preferred_element_type=F32
            )
            weights = jnp.exp(scores - jnp.max(scores, axis=0, keepdims=True))
            shares = weights * (1.0 / jnp.sum(weights, axis=0, keepdims=True))
            blended = lax.dot_general(
                shares.astype(BF16), v, (((0,), (0,)), ((), ())), preferred_element_type=F32
            )
            picked = blended[3 * CELLS :]
            for h in (2, 1, 0):
                picked = jnp.where(
                    lane < (h + 1) * width, blended[h * CELLS : (h + 1) * CELLS], picked
                )
            quads.append(picked)
        groups.append(jnp.concatenate(quads, 1).astype(BF16))
    return x + dot(jnp.concatenate(groups, 0), out_ref[...])


def feed(x, up_ref, down_ref):
    normed = half_norm(x).astype(BF16)
    hidden = [
        gelu_twice(dot(normed, up_ref[:, c : c + 256])).astype(BF16)
        for c in range(0, up_ref.shape[1], 256)
    ]
    return x + dot(jnp.concatenate(hidden, 1), down_ref[...])


def block_kernel(
    img_ref, act_ref, edge_ref, parts_ref, restore_ref, project_ref, qkv_ref, out_ref, up_ref,
    down_ref, res_ref, middle, *, cell_count,
):
    rows, cols, channels = img_ref.shape
    cells = WIN * cols
    wide = cols // WIN
    gate = gate_of(parts_ref, restore_ref, cell_count)
    acts = [
        jnp.concatenate([edge_ref[0:1], act_ref[1:WIN]], 0),
        jnp.concatenate([act_ref[WIN : rows - 1], edge_ref[1:2]], 0),
    ]
    for strip, act in enumerate(acts):
        mine = slice(strip * WIN, (strip + 1) * WIN)
        scaled = act.reshape(cells, act.shape[2]).astype(F32) * gate[0:1, :]
        x = img_ref[mine].reshape(cells, channels).astype(F32)
        x = x + dot(scaled.astype(BF16), project_ref[...])
        pieces = [
            x[r * cols + g * WIN : r * cols + (g + 1) * WIN]
            for g in range(wide)
            for r in range(WIN)
        ]
        y = attend(jnp.concatenate(pieces, 0), qkv_ref, out_ref)
        pieces = [
            y[g * CELLS + r * WIN : g * CELLS + (r + 1) * WIN]
            for r in range(WIN)
            for g in range(wide)
        ]
        middle[strip * cells : (strip + 1) * cells, :] = jnp.concatenate(pieces, 0)
    res_ref[...] = feed(middle[...], up_ref, down_ref).astype(BF16)


def block_part(image, act, edges, parts, restore, project, qkv, out, up, down, cell_count):
    rows, cols, channels = image.shape
    outs = [((rows * cols, channels), BF16)]
    args = (image, act, edges, parts, restore, project, qkv, out, up, down)
    scratch = [pltpu.VMEM((rows * cols, channels), F32)]
    kernel = functools.partial(block_kernel, cell_count=cell_count)
    return resident(kernel, outs, args, scratch, 24, 12e9, "block_part")[0]


def grid_kernel(x_ref, qkv_ref, out_ref, up_ref, down_ref, res_ref, cells, middle, *, batch):
    groups = x_ref.shape[0] // CELLS
    put(cells, x_ref[...].astype(F32))
    for start in range(0, groups, batch):
        x = [take_strided(cells, start + g, CELLS, groups) for g in range(batch)]
        y = attend(jnp.concatenate(x, 0), qkv_ref, out_ref)
        middle[start * CELLS : (start + batch) * CELLS, :] = y
    y = feed(middle[...], up_ref, down_ref)
    for g in range(groups):
        put_strided(cells, y[g * CELLS : (g + 1) * CELLS], g, CELLS, groups)
    res_ref[...] = take(cells).astype(BF16)


def grid_part(x, qkv, out, up, down, batch=8):
    scratch = [panels(*x.shape), pltpu.VMEM(x.shape, F32)]
    args = (x, qkv, out, up, down)
    kernel = functools.partial(grid_kernel, batch=batch)
    return resident(kernel, [(x.shape, BF16)], args, scratch, 24, 10e9, "grid_part")[0]


def down_expand_kernel(x_ref, w_ref, out_ref, pool_ref, cells, *, block):
    rows, cols, channels = x_ref.shape
    put(cells, x_ref[...].reshape(rows * cols, channels).astype(F32))
    half = block * cols // 2
    for start in range(0, rows, block):
        x = [take_strided(cells, start * cols + parity, half, 2) for parity in range(2)]
        pairs = (x[0] + x[1]).reshape(block // 2, 2, cols // 2, channels)
        pool = 0.25 * (pairs[:, 0] + pairs[:, 1])
        pool_ref[start // 2 : (start + block) // 2] = pool.astype(BF16)
        normed = half_norm(jnp.concatenate(x, 0)).astype(BF16)
        for c in range(0, w_ref.shape[1], 256):
            hidden = gelu_twice(dot(normed, w_ref[:, c : c + 256])).astype(BF16)
            for parity in range(2):
                mine = hidden[parity * half : (parity + 1) * half]
                out_ref[start : start + block, parity, :, c : c + 256] = mine.reshape(
                    block, cols // 2, 256
                )


def down_expand_part(x, weight, block=8):
    rows, cols, channels = x.shape
    hidden = weight.shape[1]
    outs = [((rows, 2, cols // 2, hidden), BF16), ((rows // 2, cols // 2, channels), BF16)]
    work = 4 * rows * cols * channels * hidden
    scratch = [panels(rows * cols, channels)]
    kernel = functools.partial(down_expand_kernel, block=block)
    return resident(kernel, outs, (x, weight), scratch, 8, work, "down_expand")


def down_conv_kernel(
    hid_ref, sec_ref, upper_ref, left_ref, corner_ref, w_ref, taps_ref,
    red_ref, act_ref, part_ref, section_ref, cells, normed, rim, left, sums, sem, *, chunk,
):
    rows, _, cols, width = hid_ref.shape
    steps = width // chunk
    copy = pltpu.make_async_copy(sec_ref, section_ref, sem)
    copy.start()
    row, col = lax.axis_index("row_pair") + lax.axis_index("core"), lax.axis_index(COLS)
    has_upper, has_left = flag(row > 0), flag(col > 0)
    put(cells, half_norm(upper_ref[...].astype(F32)) * has_upper)
    normed[0:32, :] = take_strided(cells, 0, 32, 2).astype(BF16)
    normed[32:64, :] = take_strided(cells, 1, 32, 2).astype(BF16)
    normed[64:80, :] = (half_norm(left_ref[...].astype(F32)) * has_left).astype(BF16)
    corner = half_norm(corner_ref[...].astype(F32)) * (has_upper * has_left)
    normed[80:96, :] = jnp.broadcast_to(corner, (16, corner.shape[1])).astype(BF16)
    rim_of(normed, w_ref[:, :chunk], rim, 0)
    place = lax.broadcasted_iota(jnp.int32, (8, 128), 0)

    def advance(step, carry):
        slot = step % 2
        left[0:1, :] = rim[slot, 80:81, :]
        left[1:17, :] = rim[slot, 64:80, :]
        for lane in range(0, chunk, 128):
            lanes = slice(lane, lane + 128)
            wide = lanes_at(step * chunk + lane)
            taps = [0.5 * taps_ref[t : t + 1, wide].astype(F32) for t in range(9)]
            before = sum(taps[3 * a] * left[a : a + rows, lanes] for a in range(3))
            total = jnp.zeros((8, 128), F32)

            def line(r, parity):
                if r < 0:
                    return rim[slot, 32 * parity : 32 * parity + 32, lanes]
                return hid_ref[r, parity, :, wide].astype(F32)

            for p in range(rows // 2):
                even = [line(2 * p + a - 1, 0) for a in range(3)]
                odd = [line(2 * p + a - 1, 1) for a in range(3)]
                shifted = sum(taps[3 * a] * odd[a] for a in range(3))
                whole = sum(taps[3 * a + 1] * even[a] + taps[3 * a + 2] * odd[a] for a in range(3))
                shifted = pltpu.roll(shifted, 1, 0)
                first = jnp.where(place == 0, before[2 * p : 2 * p + 1], shifted[0:8])
                act = gelu_twice(whole + jnp.concatenate([first, shifted[8:]], 0))
                act_ref[p, :, wide] = act.astype(BF16)
                for s in range(0, cols, 8):
                    total = total + act[s : s + 8]
            sums[:, wide] = total
        later = jnp.minimum(step + 1, steps - 1) * chunk
        rim_of(normed, w_ref[:, lanes_at(later, chunk)], rim, 1 - slot)
        return carry

    lax.fori_loop(0, steps, advance, 0)
    squeeze_sums(sums, red_ref, part_ref)
    copy.wait()


def down_conv(hidden, section, upper, left, corner, weight, taps, reduce, copies, chunk=256):
    rows, _, cols, width = hidden.shape
    channels = weight.shape[0]
    here = pl.BlockSpec(memory_space=pltpu.VMEM)
    args = (hidden, section, upper, left, corner, weight, taps, reduce)
    return pl.pallas_call(
        functools.partial(down_conv_kernel, chunk=chunk),
        in_specs=[here] * len(args),
        out_specs=[here, here, pl.BlockSpec(memory_space=pl.ANY)],
        out_shape=[
            pltpu.VMEM((rows // 2, cols, width), BF16),
            pltpu.VMEM((copies, reduce.shape[0]), F32),
            jax.ShapeDtypeStruct((rows, 2 * cols, channels), BF16),
        ],
        scratch_shapes=[
            panels(64, channels),
            pltpu.VMEM((96, channels), BF16),
            pltpu.VMEM((2, 96, chunk), F32),
            pltpu.VMEM((24, chunk), F32),
            pltpu.VMEM((8, width), F32),
            pltpu.SemaphoreType.DMA,
        ],
        compiler_params=params(8),
        name="down_conv",
    )(*[pltpu.with_memory_space_constraint(a, pltpu.VMEM) for a in args])


def down_out(act, pooled, parts, restore, project, short, cell_count):
    rows, cols, hidden = act.shape
    outs = project.shape[1]
    count = rows * cols // 2

    def kernel(act_ref, pool_ref, parts_ref, restore_ref, project_ref, short_ref, res_ref):
        gate = gate_of(parts_ref, restore_ref, cell_count)
        for i in range(2):
            mine = slice(i * rows // 2, (i + 1) * rows // 2)
            scaled = act_ref[mine].reshape(count, hidden).astype(F32) * gate[0:1, :]
            pool = pool_ref[mine].reshape(count, pool_ref.shape[2])
            y = dot(scaled.astype(BF16), project_ref[...]) + dot(pool, short_ref[...])
            res_ref[mine] = y.astype(BF16).reshape(rows // 2, cols, outs)

    here = pl.BlockSpec(memory_space=pltpu.VMEM)
    args = (act, pooled, parts, restore, project, short)
    return pl.pallas_call(
        kernel,
        in_specs=[here] * len(args),
        out_specs=here,
        out_shape=jax.ShapeDtypeStruct((rows, cols, outs), BF16),
        compiler_params=params(8),
        name="down_out",
    )(*[pltpu.with_memory_space_constraint(a, pltpu.VMEM) for a in args])


def shift(x, axes, by):
    size = lax.axis_size(axes)
    return lax.ppermute(x, axes, [(i, (i + by) % size) for i in range(size)])


def shift_both(x):
    rows, cols = lax.axis_size(ROWS), lax.axis_size(COLS)
    pairs = [
        (r * cols + c, (r + 1) % rows * cols + (c + 1) % cols)
        for r in range(rows)
        for c in range(cols)
    ]
    return lax.ppermute(x, AXES, pairs)


def exchange(x):
    cells, channels = x.shape
    sharers = lax.axis_size(CLASS)
    pieces = x.reshape(sharers, cells // sharers, channels)
    pieces = lax.all_to_all(pieces, CLASS, split_axis=0, concat_axis=0, tiled=True)
    return pieces.reshape(cells, channels)


def sum_parts(part):
    count, squeezed = part.shape
    part = part.reshape(count, 1, squeezed)
    arrived = lax.all_to_all(part, ALL, split_axis=0, concat_axis=0, tiled=True)
    return arrived.reshape(count, squeezed)


def row_rims(first, last, left, right):
    size = lax.axis_size(ROWS)
    pad = jnp.zeros((14, first.shape[1]), first.dtype)
    first = jnp.concatenate([first, left[:1], right[:1], pad], 0)
    last = jnp.concatenate([last, left[-1:], right[-1:], pad], 0)
    even = lax.axis_index("core") == 0
    away = jnp.where(even, first, last)
    near = jnp.where(even, last, first)
    pairs = [(r, (r - 1 if r % 2 == 0 else r + 1) % size) for r in range(size)]
    over = lax.ppermute(away, ROWS, pairs)
    pair = lax.ppermute(near, "core", [(0, 1), (1, 0)])
    return over, pair


def local(
    image,
    mb_expand,
    mb_taps,
    mb_reduce,
    mb_restore,
    mb_project,
    block_qkv,
    block_out,
    first_up,
    first_down,
    grid_qkv,
    grid_out,
    second_up,
    second_down,
    down_expand,
    down_taps,
    down_reduce,
    down_restore,
    down_project,
    down_shortcut,
):
    rows, cols, channels = image.shape
    all_cells = rows * cols * lax.axis_size(ALL)

    left = shift(image[:, cols - 1], COLS, 1)
    right = shift(image[:, 0], COLS, -1)
    hidden, near, first, last = expand(image, mb_expand)
    over, pair = row_rims(first, last, left, right)
    act, sums = conv_inner(hidden, left, right, mb_expand, mb_taps)
    edges, part = conv_outer(
        near, over, pair, left, right, mb_expand, mb_taps, mb_reduce.T, sums, lax.axis_size(ALL)
    )
    parts = sum_parts(part)
    mixed = block_part(
        image, act, edges, parts, mb_restore, mb_project, block_qkv, block_out, first_up, first_down,
        all_cells,
    )
    mixed = grid_part(exchange(mixed), grid_qkv, grid_out, second_up, second_down)
    section = exchange(mixed).reshape(rows, cols, channels)

    upper = shift(section[rows - 1], ROWS, 1)
    left = shift(section[:, cols - 1], COLS, 1)
    corner = shift_both(section[rows - 1, cols - 1 :])
    hidden, pooled = down_expand_part(section, down_expand)
    act, part, whole = down_conv(
        hidden, section, upper, left, corner, down_expand, down_taps, down_reduce.T,
        lax.axis_size(ALL),
    )
    parts = sum_parts(part)
    downsampled = down_out(
        act, pooled, parts, down_restore, down_project, down_shortcut, all_cells // 4
    )
    return (whole, downsampled)


def solution(mesh):
    rows, cols = mesh.devices.shape
    fine = Mesh(np.asarray(mesh.devices).reshape(rows // 2, 2, cols // 2, 2), AXES)
    tile = P(ROWS, COLS, None)
    in_specs = (tile,) + (P(),) * 19
    return jax.shard_map(
        local, mesh=fine, in_specs=in_specs, out_specs=(tile, tile), check_vma=False
    )
```

```python
import functools
import math

import jax
import jax.numpy as jnp
import numpy as np
from jax import lax
from jax.experimental import pallas as pl
from jax.experimental.pallas import tpu as pltpu
from jax.sharding import Mesh
from jax.sharding import PartitionSpec as P

HEADS = 12
WIN = 8
CELLS = WIN * WIN
QUAD = 4

epsilon = 1e-05
F32 = jnp.float32
BF16 = jnp.bfloat16
ROWS = ("row_pair", "core")
COLS = ("depth", "col_pair")
AXES = ("row_pair", "core", "depth", "col_pair")
ALL = ("core", "row_pair", "col_pair", "depth")
CLASS = ("row_pair", "col_pair", "depth")


def params(megabytes):
    return pltpu.CompilerParams(vmem_limit_bytes=megabytes << 20)


def resident(kernel, outs, args, scratch, megabytes, work, name):
    here = pl.BlockSpec(memory_space=pltpu.VMEM)
    args = [pltpu.with_memory_space_constraint(a, pltpu.VMEM) for a in args]
    return pl.pallas_call(
        kernel,
        in_specs=[here] * len(args),
        out_specs=[here] * len(outs),
        out_shape=[pltpu.VMEM(*out) for out in outs],
        scratch_shapes=scratch,
        compiler_params=params(megabytes),
        cost_estimate=pl.CostEstimate(flops=int(work), bytes_accessed=1 << 20, transcendentals=0),
        name=name,
    )(*args)


def gelu_twice(h):
    inner = h * (1.5957691216057308 + 0.285419265090401 * (h * h))
    return h + h * jnp.tanh(inner)


def layer_norm(x, scale=1.0):
    average = jnp.mean(x, axis=-1, keepdims=True)
    centred = x - average
    spread = jnp.mean(centred * centred, axis=-1, keepdims=True)
    return centred * (scale * lax.rsqrt(spread + epsilon))


def half_norm(x):
    return layer_norm(x, 0.5)


def dot(a, b):
    return jnp.dot(a, b, preferred_element_type=F32)


def exact_dot(a, b, dims):
    total = None
    for _ in range(3):
        term = a.astype(BF16)
        a = a - term.astype(F32)
        product = lax.dot_general(term, b, (dims, ((), ())), preferred_element_type=F32)
        total = product if total is None else total + product
    return total


def panels(rows, channels):
    return pltpu.VMEM((channels // 128, rows, 128), F32)


def put(ref, x):
    for c in range(ref.shape[0]):
        ref[c] = x[:, c * 128 : (c + 1) * 128]


def put_strided(ref, x, start, count, stride):
    for c in range(ref.shape[0]):
        ref[c, pl.ds(start, count, stride=stride), :] = x[:, c * 128 : (c + 1) * 128]


def take(ref):
    return jnp.concatenate([ref[c] for c in range(ref.shape[0])], 1)


def take_strided(ref, start, count, stride):
    return jnp.concatenate(
        [ref[c, pl.ds(start, count, stride=stride), :] for c in range(ref.shape[0])], 1
    )


def expand_upper(image, weight):
    rows, cols, channels = image.shape
    half, hidden = rows // 2, weight.shape[1]

    def kernel(
        x_hbm, w_hbm, up_ref, near_ref, first_ref, last_ref, x_ref, w_ref, x_sem, w_sem, last_sem
    ):
        x_copy = pltpu.make_async_copy(x_hbm.at[0:half], x_ref, x_sem)
        w_copy = pltpu.make_async_copy(w_hbm, w_ref, w_sem)
        last_copy = pltpu.make_async_copy(x_hbm.at[rows - 1], last_ref, last_sem)
        x_copy.start()
        w_copy.start()
        last_copy.start()
        x_copy.wait()
        first_ref[...] = x_ref[0]
        normed = half_norm(x_ref[...].reshape(half * cols, channels).astype(F32)).astype(BF16)
        w_copy.wait()
        for c in range(0, hidden, 256):
            wide = gelu_twice(dot(normed, w_ref[:, c : c + 256])).astype(BF16)
            wide = wide.reshape(half, cols, 256)
            up_ref[:, :, c : c + 256] = wide
            near_ref[:, :, c : c + 256] = wide[0:2]
        last_copy.wait()

    away = pl.BlockSpec(memory_space=pl.ANY)
    here = pl.BlockSpec(memory_space=pltpu.VMEM)
    return pl.pallas_call(
        kernel,
        in_specs=[away, away],
        out_specs=[here] * 4,
        out_shape=[
            pltpu.VMEM((half, cols, hidden), BF16),
            pltpu.VMEM((2, cols, hidden), BF16),
            pltpu.VMEM((cols, channels), BF16),
            pltpu.VMEM((cols, channels), BF16),
        ],
        scratch_shapes=[
            pltpu.VMEM((half, cols, channels), BF16),
            pltpu.VMEM(weight.shape, BF16),
            pltpu.SemaphoreType.DMA,
            pltpu.SemaphoreType.DMA,
            pltpu.SemaphoreType.DMA,
        ],
        compiler_params=params(16),
        cost_estimate=pl.CostEstimate(flops=int(2e9), bytes_accessed=1 << 20, transcendentals=0),
        name="expand_upper",
    )(*[pltpu.with_memory_space_constraint(a, pltpu.HBM) for a in (image, weight)])


def flag(held):
    return jnp.where(held, 1.0, 0.0).astype(F32)


def rim_of(normed, weight, rim, slot):
    rim[slot] = gelu_twice(dot(normed[...], weight)).astype(BF16).astype(F32)


def squeeze_sums(sums, red_ref, part_ref):
    parts = exact_dot(sums[...], red_ref[...], ((1,), (1,)))
    part_ref[...] = jnp.broadcast_to(jnp.sum(parts, axis=0, keepdims=True), part_ref.shape)


def lanes_at(start, size=128):
    return pl.ds(pl.multiple_of(start, 128), size)


def conv_row(lines, short, before, after, place):
    cols = lines[0].shape[0]
    one = [
        (short[b] * lines[0] + short[3 + b] * lines[1] + short[6 + b] * lines[2]).astype(F32)
        for b in range(3)
    ]
    down = pltpu.roll(one[0], 1, 0)
    up = pltpu.roll(one[2], cols - 1, 0)
    first = jnp.where(place == 0, before, down[0:8])
    last = jnp.where(place == 7, after, up[cols - 8 :])
    whole = (
        one[1]
        + jnp.concatenate([first, down[8:]], 0)
        + jnp.concatenate([up[: cols - 8], last], 0)
    )
    act = gelu_twice(whole)
    return act, sum(act[s : s + 8] for s in range(0, cols, 8))


def half_taps(taps_ref, wide):
    taps = [0.5 * taps_ref[t : t + 1, wide].astype(F32) for t in range(9)]
    return taps, [tap.astype(BF16) for tap in taps]


def side_norms(normed, start, left_ref, right_ref):
    col = lax.axis_index(COLS)
    has_left, has_right = flag(col > 0), flag(col < lax.axis_size(COLS) - 1)
    for ref, at, held in ((left_ref, start, has_left), (right_ref, start + 16, has_right)):
        normed[at : at + 16, :] = (half_norm(ref[...].astype(F32)) * held).astype(BF16)
    return has_left, has_right


def inner_kernel(
    x_hbm, up_ref, left_ref, right_ref, w_ref, taps_ref, act_ref, sums_ref, near_ref,
    x_ref, x_normed, low, normed, rim, x_sem, *, chunk,
):
    rows, cols, width = act_ref.shape
    half = rows // 2
    steps = width // chunk
    copy = pltpu.make_async_copy(x_hbm.at[half:rows], x_ref, x_sem)
    copy.start()
    side_norms(normed, 0, left_ref, right_ref)
    rim_of(normed, w_ref[:, :chunk], rim, 0)
    copy.wait()
    x = x_ref[...].reshape(half * cols, x_ref.shape[2]).astype(F32)
    x_normed[...] = half_norm(x).astype(BF16)

    def expand_lower(step, slot):
        weight = w_ref[:, lanes_at(step * chunk, chunk)]
        wide = gelu_twice(dot(x_normed[...], weight)).astype(BF16).reshape(half, cols, chunk)
        low[slot] = wide
        near_ref[:, :, lanes_at(step * chunk, chunk)] = wide[half - 2 :]
        return weight

    expand_lower(0, 0)
    place = lax.broadcasted_iota(jnp.int32, (8, 128), 0)
    inner = rows - 2

    def advance(step, carry):
        slot = step % 2
        for lane in range(0, chunk, 128):
            lanes = slice(lane, lane + 128)
            wide = lanes_at(step * chunk + lane)
            taps, short = half_taps(taps_ref, wide)
            before = sum(taps[3 * a] * rim[slot, a : a + inner, lanes] for a in range(3))
            after = sum(taps[3 * a + 2] * rim[slot, 16 + a : 16 + a + inner, lanes] for a in range(3))
            total = jnp.zeros((8, 128), F32)

            def line(r):
                return up_ref[r, :, wide] if r < half else low[slot, r - half, :, lanes]

            lines = [line(0), line(1), None]
            for r in range(1, rows - 1):
                lines[2] = line(r + 1)
                act, part = conv_row(lines, short, before[r - 1 : r], after[r - 1 : r], place)
                act_ref[r, :, wide] = act.astype(BF16)
                total = total + part
                lines = [lines[1], lines[2], None]
            sums_ref[:, wide] = total
        weight = expand_lower(jnp.minimum(step + 1, steps - 1), 1 - slot)
        rim_of(normed, weight, rim, 1 - slot)
        return carry

    lax.fori_loop(0, steps, advance, 0)


def conv_inner(image, upper, left, right, weight, taps, chunk=256):
    rows, cols, channels = image.shape
    half, _, width = upper.shape
    here = pl.BlockSpec(memory_space=pltpu.VMEM)
    args = [
        pltpu.with_memory_space_constraint(a, pltpu.VMEM)
        for a in (upper, left, right, weight, taps)
    ]
    return pl.pallas_call(
        functools.partial(inner_kernel, chunk=chunk),
        in_specs=[pl.BlockSpec(memory_space=pl.ANY)] + [here] * len(args),
        out_specs=[here] * 3,
        out_shape=[
            pltpu.VMEM((rows, cols, width), BF16),
            pltpu.VMEM((8, width), F32),
            pltpu.VMEM((2, cols, width), BF16),
        ],
        scratch_shapes=[
            pltpu.VMEM((half, cols, channels), BF16),
            pltpu.VMEM((half * cols, channels), BF16),
            pltpu.VMEM((2, half, cols, chunk), BF16),
            pltpu.VMEM((32, channels), BF16),
            pltpu.VMEM((2, 32, chunk), F32),
            pltpu.SemaphoreType.DMA,
        ],
        compiler_params=params(16),
        cost_estimate=pl.CostEstimate(flops=int(8e9), bytes_accessed=1 << 20, transcendentals=0),
        name="conv_inner",
    )(pltpu.with_memory_space_constraint(image, pltpu.HBM), *args)


def outer_kernel(
    near0_ref, near1_ref, over_ref, pair_ref, left_ref, right_ref, w_ref, taps_ref, red_ref, sums_ref,
    act_ref, part_ref, normed, rim, sums, *, chunk,
):
    _, cols, width = near0_ref.shape
    steps = width // chunk
    row, core = lax.axis_index("row_pair"), lax.axis_index("core")
    has_over = flag(row + core > 0) * flag(row - (1 - core) < lax.axis_size("row_pair") - 1)
    has_left, has_right = side_norms(normed, 160, left_ref, right_ref)
    cell = lax.broadcasted_iota(jnp.int32, (80, 1), 0)
    corners = jnp.where(cell == cols, has_left, jnp.where(cell == cols + 1, has_right, 1.0))
    for ref, start, held in ((over_ref, 0, corners * has_over), (pair_ref, 80, corners)):
        normed[start : start + 80, :] = (half_norm(ref[...].astype(F32)) * held).astype(BF16)
    rim_of(normed, w_ref[:, :chunk], rim, 0)
    top, bottom = core * 80, (1 - core) * 80
    place = lax.broadcasted_iota(jnp.int32, (8, 128), 0)

    def advance(step, carry):
        slot = step % 2
        for lane in range(0, chunk, 128):
            lanes = slice(lane, lane + 128)
            wide = lanes_at(step * chunk + lane)
            taps, short = half_taps(taps_ref, wide)

            def cells(at, side):
                return rim[slot, pl.ds(pl.multiple_of(at, 8), 8), lanes][side : side + 1]

            def line(at):
                return rim[slot, pl.ds(pl.multiple_of(at, 8), 64), lanes].astype(BF16)

            total = sums_ref[:, wide]
            near = [ref[r, :, wide] for ref in (near0_ref, near1_ref) for r in range(2)]
            edges = (
                ([line(top), near[0], near[1]], (top, 0), (160, 161)),
                ([near[2], near[3], line(bottom)], (bottom, 2), (174, 175)),
            )
            for i, (lines, (corner, turn), (one, two)) in enumerate(edges):
                beside = [[], []]
                for side in range(2):
                    beside[side].append(cells(corner + 64, side))
                    for at in (one, two):
                        beside[side].append(rim[slot, at + 16 * side : at + 16 * side + 1, lanes])
                before, after = [
                    sum(taps[3 * ((a + turn) % 3) + 2 * side] * beside[side][a] for a in range(3))
                    for side in range(2)
                ]
                act, part = conv_row(lines, short, before, after, place)
                act_ref[i, :, wide] = act.astype(BF16)
                total = total + part
            sums[:, wide] = total
        later = jnp.minimum(step + 1, steps - 1) * chunk
        rim_of(normed, w_ref[:, lanes_at(later, chunk)], rim, 1 - slot)
        return carry

    lax.fori_loop(0, steps, advance, 0)
    squeeze_sums(sums, red_ref, part_ref)


def conv_outer(near, over, pair, left, right, weight, taps, reduce, sums, copies, chunk=256):
    _, cols, width = near[0].shape
    channels = weight.shape[0]
    outs = [((2, cols, width), BF16), ((copies, reduce.shape[0]), F32)]
    scratch = [
        pltpu.VMEM((192, channels), BF16),
        pltpu.VMEM((2, 192, chunk), F32),
        pltpu.VMEM((8, width), F32),
    ]
    args = (*near, over, pair, left, right, weight, taps, reduce, sums)
    kernel = functools.partial(outer_kernel, chunk=chunk)
    return resident(kernel, outs, args, scratch, 16, 2e9, "conv_outer")


def gate_of(parts_ref, restore_ref, cell_count):
    average = jnp.sum(parts_ref[...], axis=0, keepdims=True) / cell_count
    squeezed = average * jax.nn.sigmoid(average)
    squeezed = jnp.broadcast_to(squeezed, (8, squeezed.shape[1]))
    return jax.nn.sigmoid(exact_dot(squeezed, restore_ref[...], ((1,), (0,))))


def attend(x, qkv_ref, out_ref):
    cells, channels = x.shape
    width = channels // HEADS
    normed = layer_norm(x).astype(BF16)
    projected = dot(normed, qkv_ref[...])
    queries = (projected[:, :channels] * (1.0 / math.sqrt(width))).astype(BF16)
    keys = projected[:, channels : 2 * channels].astype(BF16)
    values = projected[:, 2 * channels :].astype(BF16)
    lane = lax.broadcasted_iota(jnp.int32, (1, 128), 1)
    masks = [((lane >= h * width) & (lane < (h + 1) * width)).astype(BF16) for h in range(QUAD)]
    groups = []
    for g in range(0, cells, CELLS):
        mine = slice(g, g + CELLS)
        quads = []
        for c in range(0, channels, 128):
            lanes = slice(c, c + 128)
            q, k, v = queries[mine, lanes], keys[mine, lanes], values[mine, lanes]
            stacked = jnp.concatenate([q * m for m in masks], 0)
            scores = lax.dot_general(
                k, stacked, (((1,), (1,)), ((), ())), preferred_element_type=F32
            )
            weights = jnp.exp(scores - jnp.max(scores, axis=0, keepdims=True))
            shares = weights * (1.0 / jnp.sum(weights, axis=0, keepdims=True))
            blended = lax.dot_general(
                shares.astype(BF16), v, (((0,), (0,)), ((), ())), preferred_element_type=F32
            )
            picked = blended[3 * CELLS :]
            for h in (2, 1, 0):
                picked = jnp.where(
                    lane < (h + 1) * width, blended[h * CELLS : (h + 1) * CELLS], picked
                )
            quads.append(picked)
        groups.append(jnp.concatenate(quads, 1).astype(BF16))
    return x + dot(jnp.concatenate(groups, 0), out_ref[...])


def feed(x, up_ref, down_ref):
    normed = half_norm(x).astype(BF16)
    hidden = [
        gelu_twice(dot(normed, up_ref[:, c : c + 256])).astype(BF16)
        for c in range(0, up_ref.shape[1], 256)
    ]
    return x + dot(jnp.concatenate(hidden, 1), down_ref[...])


def block_kernel(
    img_ref, act_ref, edge_ref, parts_ref, restore_ref, project_ref, qkv_ref, out_ref, up_ref,
    down_ref, res_ref, middle, *, cell_count,
):
    rows, cols, channels = img_ref.shape
    cells = WIN * cols
    wide = cols // WIN
    gate = gate_of(parts_ref, restore_ref, cell_count)
    acts = [
        jnp.concatenate([edge_ref[0:1], act_ref[1:WIN]], 0),
        jnp.concatenate([act_ref[WIN : rows - 1], edge_ref[1:2]], 0),
    ]
    for strip, act in enumerate(acts):
        mine = slice(strip * WIN, (strip + 1) * WIN)
        scaled = act.reshape(cells, act.shape[2]).astype(F32) * gate[0:1, :]
        x = img_ref[mine].reshape(cells, channels).astype(F32)
        x = x + dot(scaled.astype(BF16), project_ref[...])
        pieces = [
            x[r * cols + g * WIN : r * cols + (g + 1) * WIN]
            for g in range(wide)
            for r in range(WIN)
        ]
        y = attend(jnp.concatenate(pieces, 0), qkv_ref, out_ref)
        pieces = [
            y[g * CELLS + r * WIN : g * CELLS + (r + 1) * WIN]
            for r in range(WIN)
            for g in range(wide)
        ]
        middle[strip * cells : (strip + 1) * cells, :] = jnp.concatenate(pieces, 0)
    res_ref[...] = feed(middle[...], up_ref, down_ref).astype(BF16)


def block_part(image, act, edges, parts, restore, project, qkv, out, up, down, cell_count):
    rows, cols, channels = image.shape
    outs = [((rows * cols, channels), BF16)]
    args = (image, act, edges, parts, restore, project, qkv, out, up, down)
    scratch = [pltpu.VMEM((rows * cols, channels), F32)]
    kernel = functools.partial(block_kernel, cell_count=cell_count)
    return resident(kernel, outs, args, scratch, 24, 12e9, "block_part")[0]


def grid_kernel(x_ref, qkv_ref, out_ref, up_ref, down_ref, res_ref, cells, middle, *, batch):
    groups = x_ref.shape[0] // CELLS
    put(cells, x_ref[...].astype(F32))
    for start in range(0, groups, batch):
        x = [take_strided(cells, start + g, CELLS, groups) for g in range(batch)]
        y = attend(jnp.concatenate(x, 0), qkv_ref, out_ref)
        middle[start * CELLS : (start + batch) * CELLS, :] = y
    y = feed(middle[...], up_ref, down_ref)
    for g in range(groups):
        put_strided(cells, y[g * CELLS : (g + 1) * CELLS], g, CELLS, groups)
    res_ref[...] = take(cells).astype(BF16)


def grid_part(x, qkv, out, up, down, batch=8):
    scratch = [panels(*x.shape), pltpu.VMEM(x.shape, F32)]
    args = (x, qkv, out, up, down)
    kernel = functools.partial(grid_kernel, batch=batch)
    return resident(kernel, [(x.shape, BF16)], args, scratch, 24, 10e9, "grid_part")[0]


def down_expand_kernel(x_ref, w_ref, out_ref, pool_ref, cells, *, block):
    rows, cols, channels = x_ref.shape
    put(cells, x_ref[...].reshape(rows * cols, channels).astype(F32))
    half = block * cols // 2
    for start in range(0, rows, block):
        x = [take_strided(cells, start * cols + parity, half, 2) for parity in range(2)]
        pairs = (x[0] + x[1]).reshape(block // 2, 2, cols // 2, channels)
        pool = 0.25 * (pairs[:, 0] + pairs[:, 1])
        pool_ref[start // 2 : (start + block) // 2] = pool.astype(BF16)
        normed = half_norm(jnp.concatenate(x, 0)).astype(BF16)
        for c in range(0, w_ref.shape[1], 256):
            hidden = gelu_twice(dot(normed, w_ref[:, c : c + 256])).astype(BF16)
            for parity in range(2):
                mine = hidden[parity * half : (parity + 1) * half]
                out_ref[start : start + block, parity, :, c : c + 256] = mine.reshape(
                    block, cols // 2, 256
                )


def down_expand_part(x, weight, block=8):
    rows, cols, channels = x.shape
    hidden = weight.shape[1]
    outs = [((rows, 2, cols // 2, hidden), BF16), ((rows // 2, cols // 2, channels), BF16)]
    work = 4 * rows * cols * channels * hidden
    scratch = [panels(rows * cols, channels)]
    kernel = functools.partial(down_expand_kernel, block=block)
    return resident(kernel, outs, (x, weight), scratch, 8, work, "down_expand")


def down_conv_kernel(
    hid_ref, sec_ref, upper_ref, left_ref, corner_ref, w_ref, taps_ref,
    red_ref, act_ref, part_ref, section_ref, cells, normed, rim, left, sums, sem, *, chunk,
):
    rows, _, cols, width = hid_ref.shape
    steps = width // chunk
    copy = pltpu.make_async_copy(sec_ref, section_ref, sem)
    copy.start()
    row, col = lax.axis_index("row_pair") + lax.axis_index("core"), lax.axis_index(COLS)
    has_upper, has_left = flag(row > 0), flag(col > 0)
    put(cells, half_norm(upper_ref[...].astype(F32)) * has_upper)
    normed[0:32, :] = take_strided(cells, 0, 32, 2).astype(BF16)
    normed[32:64, :] = take_strided(cells, 1, 32, 2).astype(BF16)
    normed[64:80, :] = (half_norm(left_ref[...].astype(F32)) * has_left).astype(BF16)
    corner = half_norm(corner_ref[...].astype(F32)) * (has_upper * has_left)
    normed[80:96, :] = jnp.broadcast_to(corner, (16, corner.shape[1])).astype(BF16)
    rim_of(normed, w_ref[:, :chunk], rim, 0)
    place = lax.broadcasted_iota(jnp.int32, (8, 128), 0)

    def advance(step, carry):
        slot = step % 2
        left[0:1, :] = rim[slot, 80:81, :]
        left[1:17, :] = rim[slot, 64:80, :]
        for lane in range(0, chunk, 128):
            lanes = slice(lane, lane + 128)
            wide = lanes_at(step * chunk + lane)
            taps = [0.5 * taps_ref[t : t + 1, wide].astype(F32) for t in range(9)]
            before = sum(taps[3 * a] * left[a : a + rows, lanes] for a in range(3))
            total = jnp.zeros((8, 128), F32)

            def line(r, parity):
                if r < 0:
                    return rim[slot, 32 * parity : 32 * parity + 32, lanes]
                return hid_ref[r, parity, :, wide].astype(F32)

            for p in range(rows // 2):
                even = [line(2 * p + a - 1, 0) for a in range(3)]
                odd = [line(2 * p + a - 1, 1) for a in range(3)]
                shifted = sum(taps[3 * a] * odd[a] for a in range(3))
                whole = sum(taps[3 * a + 1] * even[a] + taps[3 * a + 2] * odd[a] for a in range(3))
                shifted = pltpu.roll(shifted, 1, 0)
                first = jnp.where(place == 0, before[2 * p : 2 * p + 1], shifted[0:8])
                act = gelu_twice(whole + jnp.concatenate([first, shifted[8:]], 0))
                act_ref[p, :, wide] = act.astype(BF16)
                for s in range(0, cols, 8):
                    total = total + act[s : s + 8]
            sums[:, wide] = total
        later = jnp.minimum(step + 1, steps - 1) * chunk
        rim_of(normed, w_ref[:, lanes_at(later, chunk)], rim, 1 - slot)
        return carry

    lax.fori_loop(0, steps, advance, 0)
    squeeze_sums(sums, red_ref, part_ref)
    copy.wait()


def down_conv(hidden, section, upper, left, corner, weight, taps, reduce, copies, chunk=256):
    rows, _, cols, width = hidden.shape
    channels = weight.shape[0]
    here = pl.BlockSpec(memory_space=pltpu.VMEM)
    args = (hidden, section, upper, left, corner, weight, taps, reduce)
    return pl.pallas_call(
        functools.partial(down_conv_kernel, chunk=chunk),
        in_specs=[here] * len(args),
        out_specs=[here, here, pl.BlockSpec(memory_space=pl.ANY)],
        out_shape=[
            pltpu.VMEM((rows // 2, cols, width), BF16),
            pltpu.VMEM((copies, reduce.shape[0]), F32),
            jax.ShapeDtypeStruct((rows, 2 * cols, channels), BF16),
        ],
        scratch_shapes=[
            panels(64, channels),
            pltpu.VMEM((96, channels), BF16),
            pltpu.VMEM((2, 96, chunk), F32),
            pltpu.VMEM((24, chunk), F32),
            pltpu.VMEM((8, width), F32),
            pltpu.SemaphoreType.DMA,
        ],
        compiler_params=params(8),
        name="down_conv",
    )(*[pltpu.with_memory_space_constraint(a, pltpu.VMEM) for a in args])


def down_out(act, pooled, parts, restore, project, short, cell_count):
    rows, cols, hidden = act.shape
    outs = project.shape[1]
    count = rows * cols // 2

    def kernel(act_ref, pool_ref, parts_ref, restore_ref, project_ref, short_ref, res_ref):
        gate = gate_of(parts_ref, restore_ref, cell_count)
        for i in range(2):
            mine = slice(i * rows // 2, (i + 1) * rows // 2)
            scaled = act_ref[mine].reshape(count, hidden).astype(F32) * gate[0:1, :]
            pool = pool_ref[mine].reshape(count, pool_ref.shape[2])
            y = dot(scaled.astype(BF16), project_ref[...]) + dot(pool, short_ref[...])
            res_ref[mine] = y.astype(BF16).reshape(rows // 2, cols, outs)

    here = pl.BlockSpec(memory_space=pltpu.VMEM)
    args = (act, pooled, parts, restore, project, short)
    return pl.pallas_call(
        kernel,
        in_specs=[here] * len(args),
        out_specs=here,
        out_shape=jax.ShapeDtypeStruct((rows, cols, outs), BF16),
        compiler_params=params(8),
        name="down_out",
    )(*[pltpu.with_memory_space_constraint(a, pltpu.VMEM) for a in args])


def shift(x, axes, by):
    size = lax.axis_size(axes)
    return lax.ppermute(x, axes, [(i, (i + by) % size) for i in range(size)])


def shift_both(x):
    rows, cols = lax.axis_size(ROWS), lax.axis_size(COLS)
    pairs = [
        (r * cols + c, (r + 1) % rows * cols + (c + 1) % cols)
        for r in range(rows)
        for c in range(cols)
    ]
    return lax.ppermute(x, AXES, pairs)


def exchange(x):
    cells, channels = x.shape
    sharers = lax.axis_size(CLASS)
    pieces = x.reshape(sharers, cells // sharers, channels)
    pieces = lax.all_to_all(pieces, CLASS, split_axis=0, concat_axis=0, tiled=True)
    return pieces.reshape(cells, channels)


def sum_parts(part):
    count, squeezed = part.shape
    part = part.reshape(count, 1, squeezed)
    arrived = lax.all_to_all(part, ALL, split_axis=0, concat_axis=0, tiled=True)
    return arrived.reshape(count, squeezed)


def row_rims(first, last, left, right):
    size = lax.axis_size(ROWS)
    pad = jnp.zeros((14, first.shape[1]), first.dtype)
    first = jnp.concatenate([first, left[:1], right[:1], pad], 0)
    last = jnp.concatenate([last, left[-1:], right[-1:], pad], 0)
    even = lax.axis_index("core") == 0
    away = jnp.where(even, first, last)
    near = jnp.where(even, last, first)
    pairs = [(r, (r - 1 if r % 2 == 0 else r + 1) % size) for r in range(size)]
    over = lax.ppermute(away, ROWS, pairs)
    pair = lax.ppermute(near, "core", [(0, 1), (1, 0)])
    return over, pair


def local(
    image,
    mb_expand,
    mb_taps,
    mb_reduce,
    mb_restore,
    mb_project,
    block_qkv,
    block_out,
    first_up,
    first_down,
    grid_qkv,
    grid_out,
    second_up,
    second_down,
    down_expand,
    down_taps,
    down_reduce,
    down_restore,
    down_project,
    down_shortcut,
):
    rows, cols, channels = image.shape
    all_cells = rows * cols * lax.axis_size(ALL)

    left = shift(image[:, cols - 1], COLS, 1)
    right = shift(image[:, 0], COLS, -1)
    upper, near_top, first, last = expand_upper(image, mb_expand)
    over, pair = row_rims(first, last, left, right)
    act, sums, near_end = conv_inner(image, upper, left, right, mb_expand, mb_taps)
    edges, part = conv_outer(
        (near_top, near_end), over, pair, left, right, mb_expand, mb_taps, mb_reduce.T, sums,
        lax.axis_size(ALL),
    )
    parts = sum_parts(part)
    mixed = block_part(
        image, act, edges, parts, mb_restore, mb_project, block_qkv, block_out, first_up, first_down,
        all_cells,
    )
    mixed = grid_part(exchange(mixed), grid_qkv, grid_out, second_up, second_down)
    section = exchange(mixed).reshape(rows, cols, channels)

    upper = shift(section[rows - 1], ROWS, 1)
    left = shift(section[:, cols - 1], COLS, 1)
    corner = shift_both(section[rows - 1, cols - 1 :])
    hidden, pooled = down_expand_part(section, down_expand)
    act, part, whole = down_conv(
        hidden, section, upper, left, corner, down_expand, down_taps, down_reduce.T,
        lax.axis_size(ALL),
    )
    parts = sum_parts(part)
    downsampled = down_out(
        act, pooled, parts, down_restore, down_project, down_shortcut, all_cells // 4
    )
    return (whole, downsampled)


def solution(mesh):
    rows, cols = mesh.devices.shape
    fine = Mesh(np.asarray(mesh.devices).reshape(rows // 2, 2, cols // 2, 2), AXES)
    tile = P(ROWS, COLS, None)
    in_specs = (tile,) + (P(),) * 19
    return jax.shard_map(
        local, mesh=fine, in_specs=in_specs, out_specs=(tile, tile), check_vma=False
    )
```

```python
import functools
import math

import jax
import jax.numpy as jnp
import numpy as np
from jax import lax
from jax.experimental import pallas as pl
from jax.experimental.pallas import tpu as pltpu
from jax.sharding import Mesh
from jax.sharding import PartitionSpec as P

HEADS = 12
WIN = 8
CELLS = WIN * WIN
QUAD = 4

epsilon = 1e-05
F32 = jnp.float32
BF16 = jnp.bfloat16
ROWS = ("row_pair", "core")
COLS = ("depth", "col_pair")
AXES = ("row_pair", "core", "depth", "col_pair")
ALL = ("core", "row_pair", "col_pair", "depth")
CLASS = ("row_pair", "col_pair", "depth")


def params(megabytes):
    return pltpu.CompilerParams(vmem_limit_bytes=megabytes << 20)


def resident(kernel, outs, args, scratch, megabytes, work, name):
    here = pl.BlockSpec(memory_space=pltpu.VMEM)
    args = [pltpu.with_memory_space_constraint(a, pltpu.VMEM) for a in args]
    return pl.pallas_call(
        kernel,
        in_specs=[here] * len(args),
        out_specs=[here] * len(outs),
        out_shape=[pltpu.VMEM(*out) for out in outs],
        scratch_shapes=scratch,
        compiler_params=params(megabytes),
        cost_estimate=pl.CostEstimate(flops=int(work), bytes_accessed=1 << 20, transcendentals=0),
        name=name,
    )(*args)


def gelu_twice(h):
    inner = h * (1.5957691216057308 + 0.285419265090401 * (h * h))
    return h + h * jnp.tanh(inner)


def layer_norm(x, scale=1.0):
    average = jnp.mean(x, axis=-1, keepdims=True)
    centred = x - average
    spread = jnp.mean(centred * centred, axis=-1, keepdims=True)
    return centred * (scale * lax.rsqrt(spread + epsilon))


def half_norm(x):
    return layer_norm(x, 0.5)


def dot(a, b):
    return jnp.dot(a, b, preferred_element_type=F32)


def exact_dot(a, b, dims):
    total = None
    for _ in range(3):
        term = a.astype(BF16)
        a = a - term.astype(F32)
        product = lax.dot_general(term, b, (dims, ((), ())), preferred_element_type=F32)
        total = product if total is None else total + product
    return total


def panels(rows, channels):
    return pltpu.VMEM((channels // 128, rows, 128), F32)


def put(ref, x):
    for c in range(ref.shape[0]):
        ref[c] = x[:, c * 128 : (c + 1) * 128]


def put_strided(ref, x, start, count, stride):
    for c in range(ref.shape[0]):
        ref[c, pl.ds(start, count, stride=stride), :] = x[:, c * 128 : (c + 1) * 128]


def take(ref):
    return jnp.concatenate([ref[c] for c in range(ref.shape[0])], 1)


def take_strided(ref, start, count, stride):
    return jnp.concatenate(
        [ref[c, pl.ds(start, count, stride=stride), :] for c in range(ref.shape[0])], 1
    )


def expand_upper(image, weight, chunk=256):
    rows, cols, channels = image.shape
    half, hidden = rows // 2, weight.shape[1]

    def kernel(
        x_hbm, w_hbm, up_ref, near_ref, first_ref, last_ref, normed_ref, start_ref,
        x_ref, w_ref, x_sems, w_sem,
    ):
        parts = [slice(0, half), slice(half, rows)]
        x_copies = [
            pltpu.make_async_copy(x_hbm.at[part], x_ref.at[part], x_sems.at[i])
            for i, part in enumerate(parts)
        ]
        w_copy = pltpu.make_async_copy(w_hbm, w_ref, w_sem)
        x_copies[0].start()
        w_copy.start()
        x_copies[1].start()

        def norm(part):
            x = x_ref[part].reshape(half * cols, channels).astype(F32)
            return half_norm(x).astype(BF16)

        def wide(normed, c):
            hidden = gelu_twice(dot(normed, w_ref[:, c : c + chunk])).astype(BF16)
            return hidden.reshape(half, cols, chunk)

        x_copies[0].wait()
        first_ref[...] = x_ref[0]
        normed = norm(parts[0])
        w_copy.wait()
        for c in range(0, hidden, chunk):
            upper = wide(normed, c)
            up_ref[:, :, c : c + chunk] = upper
            near_ref[:, :, c : c + chunk] = upper[0:2]
        x_copies[1].wait()
        last_ref[...] = x_ref[rows - 1]
        normed = norm(parts[1])
        normed_ref[...] = normed
        start_ref[...] = wide(normed, 0)

    away = pl.BlockSpec(memory_space=pl.ANY)
    here = pl.BlockSpec(memory_space=pltpu.VMEM)
    return pl.pallas_call(
        kernel,
        in_specs=[away, away],
        out_specs=[here] * 6,
        out_shape=[
            pltpu.VMEM((half, cols, hidden), BF16),
            pltpu.VMEM((2, cols, hidden), BF16),
            pltpu.VMEM((cols, channels), BF16),
            pltpu.VMEM((cols, channels), BF16),
            pltpu.VMEM((half * cols, channels), BF16),
            pltpu.VMEM((half, cols, chunk), BF16),
        ],
        scratch_shapes=[
            pltpu.VMEM(image.shape, BF16),
            pltpu.VMEM(weight.shape, BF16),
            pltpu.SemaphoreType.DMA((2,)),
            pltpu.SemaphoreType.DMA,
        ],
        compiler_params=params(16),
        cost_estimate=pl.CostEstimate(flops=int(2e9), bytes_accessed=1 << 20, transcendentals=0),
        name="expand_upper",
    )(*[pltpu.with_memory_space_constraint(a, pltpu.HBM) for a in (image, weight)])


def flag(held):
    return jnp.where(held, 1.0, 0.0).astype(F32)


def rim_of(normed, weight, rim, slot):
    rim[slot] = gelu_twice(dot(normed[...], weight)).astype(BF16).astype(F32)


def squeeze_sums(sums, red_ref, part_ref):
    parts = exact_dot(sums[...], red_ref[...], ((1,), (1,)))
    part_ref[...] = jnp.broadcast_to(jnp.sum(parts, axis=0, keepdims=True), part_ref.shape)


def lanes_at(start, size=128):
    return pl.ds(pl.multiple_of(start, 128), size)


def conv_row(lines, short, before, after, place):
    cols = lines[0].shape[0]
    one = [
        (short[b] * lines[0] + short[3 + b] * lines[1] + short[6 + b] * lines[2]).astype(F32)
        for b in range(3)
    ]
    down = pltpu.roll(one[0], 1, 0)
    up = pltpu.roll(one[2], cols - 1, 0)
    first = jnp.where(place == 0, before, down[0:8])
    last = jnp.where(place == 7, after, up[cols - 8 :])
    whole = (
        one[1]
        + jnp.concatenate([first, down[8:]], 0)
        + jnp.concatenate([up[: cols - 8], last], 0)
    )
    act = gelu_twice(whole)
    return act, sum(act[s : s + 8] for s in range(0, cols, 8))


def half_taps(taps_ref, wide):
    taps = [0.5 * taps_ref[t : t + 1, wide].astype(F32) for t in range(9)]
    return taps, [tap.astype(BF16) for tap in taps]


def side_norms(normed, start, left_ref, right_ref):
    col = lax.axis_index(COLS)
    has_left, has_right = flag(col > 0), flag(col < lax.axis_size(COLS) - 1)
    for ref, at, held in ((left_ref, start, has_left), (right_ref, start + 16, has_right)):
        normed[at : at + 16, :] = (half_norm(ref[...].astype(F32)) * held).astype(BF16)
    return has_left, has_right


def inner_kernel(
    up_ref, x_ref, start_ref, left_ref, right_ref, w_ref, taps_ref, act_ref, sums_ref, near_ref,
    low, normed, rim, *, chunk,
):
    rows, cols, width = act_ref.shape
    half = rows // 2
    steps = width // chunk
    side_norms(normed, 0, left_ref, right_ref)
    rim_of(normed, w_ref[:, :chunk], rim, 0)
    low[0] = start_ref[...]
    near_ref[:, :, :chunk] = start_ref[half - 2 : half]

    def expand_lower(step, slot):
        weight = w_ref[:, lanes_at(step * chunk, chunk)]
        wide = gelu_twice(dot(x_ref[...], weight)).astype(BF16).reshape(half, cols, chunk)
        low[slot] = wide
        near_ref[:, :, lanes_at(step * chunk, chunk)] = wide[half - 2 :]
        return weight

    place = lax.broadcasted_iota(jnp.int32, (8, 128), 0)
    inner = rows - 2

    def advance(step, carry):
        slot = step % 2
        for lane in range(0, chunk, 128):
            lanes = slice(lane, lane + 128)
            wide = lanes_at(step * chunk + lane)
            taps, short = half_taps(taps_ref, wide)
            before = sum(taps[3 * a] * rim[slot, a : a + inner, lanes] for a in range(3))
            after = sum(taps[3 * a + 2] * rim[slot, 16 + a : 16 + a + inner, lanes] for a in range(3))
            total = jnp.zeros((8, 128), F32)

            def line(r):
                return up_ref[r, :, wide] if r < half else low[slot, r - half, :, lanes]

            lines = [line(0), line(1), None]
            for r in range(1, rows - 1):
                lines[2] = line(r + 1)
                act, part = conv_row(lines, short, before[r - 1 : r], after[r - 1 : r], place)
                act_ref[r, :, wide] = act.astype(BF16)
                total = total + part
                lines = [lines[1], lines[2], None]
            sums_ref[:, wide] = total
        weight = expand_lower(jnp.minimum(step + 1, steps - 1), 1 - slot)
        rim_of(normed, weight, rim, 1 - slot)
        return carry

    lax.fori_loop(0, steps, advance, 0)


def conv_inner(upper, normed, start, left, right, weight, taps):
    half, cols, width = upper.shape
    channels, chunk = weight.shape[0], start.shape[2]
    outs = [((2 * half, cols, width), BF16), ((8, width), F32), ((2, cols, width), BF16)]
    scratch = [
        pltpu.VMEM((2, half, cols, chunk), BF16),
        pltpu.VMEM((32, channels), BF16),
        pltpu.VMEM((2, 32, chunk), F32),
    ]
    args = (upper, normed, start, left, right, weight, taps)
    kernel = functools.partial(inner_kernel, chunk=chunk)
    return resident(kernel, outs, args, scratch, 16, 8e9, "conv_inner")


def outer_kernel(
    near0_ref, near1_ref, over_ref, pair_ref, left_ref, right_ref, w_ref, taps_ref, red_ref, sums_ref,
    act_ref, part_ref, normed, rim, sums, *, chunk,
):
    _, cols, width = near0_ref.shape
    steps = width // chunk
    row, core = lax.axis_index("row_pair"), lax.axis_index("core")
    has_over = flag(row + core > 0) * flag(row - (1 - core) < lax.axis_size("row_pair") - 1)
    has_left, has_right = side_norms(normed, 160, left_ref, right_ref)
    cell = lax.broadcasted_iota(jnp.int32, (80, 1), 0)
    corners = jnp.where(cell == cols, has_left, jnp.where(cell == cols + 1, has_right, 1.0))
    for ref, start, held in ((over_ref, 0, corners * has_over), (pair_ref, 80, corners)):
        normed[start : start + 80, :] = (half_norm(ref[...].astype(F32)) * held).astype(BF16)
    rim_of(normed, w_ref[:, :chunk], rim, 0)
    top, bottom = core * 80, (1 - core) * 80
    place = lax.broadcasted_iota(jnp.int32, (8, 128), 0)

    def advance(step, carry):
        slot = step % 2
        for lane in range(0, chunk, 128):
            lanes = slice(lane, lane + 128)
            wide = lanes_at(step * chunk + lane)
            taps, short = half_taps(taps_ref, wide)

            def cells(at, side):
                return rim[slot, pl.ds(pl.multiple_of(at, 8), 8), lanes][side : side + 1]

            def line(at):
                return rim[slot, pl.ds(pl.multiple_of(at, 8), 64), lanes].astype(BF16)

            total = sums_ref[:, wide]
            near = [ref[r, :, wide] for ref in (near0_ref, near1_ref) for r in range(2)]
            edges = (
                ([line(top), near[0], near[1]], (top, 0), (160, 161)),
                ([near[2], near[3], line(bottom)], (bottom, 2), (174, 175)),
            )
            for i, (lines, (corner, turn), (one, two)) in enumerate(edges):
                beside = [[], []]
                for side in range(2):
                    beside[side].append(cells(corner + 64, side))
                    for at in (one, two):
                        beside[side].append(rim[slot, at + 16 * side : at + 16 * side + 1, lanes])
                before, after = [
                    sum(taps[3 * ((a + turn) % 3) + 2 * side] * beside[side][a] for a in range(3))
                    for side in range(2)
                ]
                act, part = conv_row(lines, short, before, after, place)
                act_ref[i, :, wide] = act.astype(BF16)
                total = total + part
            sums[:, wide] = total
        later = jnp.minimum(step + 1, steps - 1) * chunk
        rim_of(normed, w_ref[:, lanes_at(later, chunk)], rim, 1 - slot)
        return carry

    lax.fori_loop(0, steps, advance, 0)
    squeeze_sums(sums, red_ref, part_ref)


def conv_outer(near, over, pair, left, right, weight, taps, reduce, sums, copies, chunk=768):
    _, cols, width = near[0].shape
    channels = weight.shape[0]
    outs = [((2, cols, width), BF16), ((copies, reduce.shape[0]), F32)]
    scratch = [
        pltpu.VMEM((192, channels), BF16),
        pltpu.VMEM((2, 192, chunk), F32),
        pltpu.VMEM((8, width), F32),
    ]
    args = (*near, over, pair, left, right, weight, taps, reduce, sums)
    kernel = functools.partial(outer_kernel, chunk=chunk)
    return resident(kernel, outs, args, scratch, 16, 2e9, "conv_outer")


def gate_of(parts_ref, restore_ref, cell_count):
    average = jnp.sum(parts_ref[...], axis=0, keepdims=True) / cell_count
    squeezed = average * jax.nn.sigmoid(average)
    squeezed = jnp.broadcast_to(squeezed, (8, squeezed.shape[1]))
    return jax.nn.sigmoid(exact_dot(squeezed, restore_ref[...], ((1,), (0,))))


def attend(x, qkv_ref, out_ref):
    cells, channels = x.shape
    width = channels // HEADS
    normed = layer_norm(x).astype(BF16)
    projected = dot(normed, qkv_ref[...])
    queries = (projected[:, :channels] * (1.0 / math.sqrt(width))).astype(BF16)
    keys = projected[:, channels : 2 * channels].astype(BF16)
    values = projected[:, 2 * channels :].astype(BF16)
    lane = lax.broadcasted_iota(jnp.int32, (1, 128), 1)
    masks = [((lane >= h * width) & (lane < (h + 1) * width)).astype(BF16) for h in range(QUAD)]
    groups = []
    for g in range(0, cells, CELLS):
        mine = slice(g, g + CELLS)
        quads = []
        for c in range(0, channels, 128):
            lanes = slice(c, c + 128)
            q, k, v = queries[mine, lanes], keys[mine, lanes], values[mine, lanes]
            stacked = jnp.concatenate([q * m for m in masks], 0)
            scores = lax.dot_general(
                k, stacked, (((1,), (1,)), ((), ())), preferred_element_type=F32
            )
            weights = jnp.exp(scores - jnp.max(scores, axis=0, keepdims=True))
            shares = weights * (1.0 / jnp.sum(weights, axis=0, keepdims=True))
            blended = lax.dot_general(
                shares.astype(BF16), v, (((0,), (0,)), ((), ())), preferred_element_type=F32
            )
            picked = blended[3 * CELLS :]
            for h in (2, 1, 0):
                picked = jnp.where(
                    lane < (h + 1) * width, blended[h * CELLS : (h + 1) * CELLS], picked
                )
            quads.append(picked)
        groups.append(jnp.concatenate(quads, 1).astype(BF16))
    return x + dot(jnp.concatenate(groups, 0), out_ref[...])


def feed(x, up_ref, down_ref):
    normed = half_norm(x).astype(BF16)
    hidden = [
        gelu_twice(dot(normed, up_ref[:, c : c + 256])).astype(BF16)
        for c in range(0, up_ref.shape[1], 256)
    ]
    return x + dot(jnp.concatenate(hidden, 1), down_ref[...])


def block_kernel(
    img_ref, act_ref, edge_ref, parts_ref, restore_ref, project_ref, qkv_ref, out_ref, up_ref,
    down_ref, res_ref, middle, *, cell_count,
):
    rows, cols, channels = img_ref.shape
    cells = WIN * cols
    wide = cols // WIN
    gate = gate_of(parts_ref, restore_ref, cell_count)
    acts = [
        jnp.concatenate([edge_ref[0:1], act_ref[1:WIN]], 0),
        jnp.concatenate([act_ref[WIN : rows - 1], edge_ref[1:2]], 0),
    ]
    for strip, act in enumerate(acts):
        mine = slice(strip * WIN, (strip + 1) * WIN)
        scaled = act.reshape(cells, act.shape[2]).astype(F32) * gate[0:1, :]
        x = img_ref[mine].reshape(cells, channels).astype(F32)
        x = x + dot(scaled.astype(BF16), project_ref[...])
        pieces = [
            x[r * cols + g * WIN : r * cols + (g + 1) * WIN]
            for g in range(wide)
            for r in range(WIN)
        ]
        y = attend(jnp.concatenate(pieces, 0), qkv_ref, out_ref)
        pieces = [
            y[g * CELLS + r * WIN : g * CELLS + (r + 1) * WIN]
            for r in range(WIN)
            for g in range(wide)
        ]
        middle[strip * cells : (strip + 1) * cells, :] = jnp.concatenate(pieces, 0)
    res_ref[...] = feed(middle[...], up_ref, down_ref).astype(BF16)


def block_part(image, act, edges, parts, restore, project, qkv, out, up, down, cell_count):
    rows, cols, channels = image.shape
    outs = [((rows * cols, channels), BF16)]
    args = (image, act, edges, parts, restore, project, qkv, out, up, down)
    scratch = [pltpu.VMEM((rows * cols, channels), F32)]
    kernel = functools.partial(block_kernel, cell_count=cell_count)
    return resident(kernel, outs, args, scratch, 24, 12e9, "block_part")[0]


def grid_kernel(x_ref, qkv_ref, out_ref, up_ref, down_ref, res_ref, cells, middle, *, batch):
    groups = x_ref.shape[0] // CELLS
    put(cells, x_ref[...].astype(F32))
    for start in range(0, groups, batch):
        x = [take_strided(cells, start + g, CELLS, groups) for g in range(batch)]
        y = attend(jnp.concatenate(x, 0), qkv_ref, out_ref)
        middle[start * CELLS : (start + batch) * CELLS, :] = y
    y = feed(middle[...], up_ref, down_ref)
    for g in range(groups):
        put_strided(cells, y[g * CELLS : (g + 1) * CELLS], g, CELLS, groups)
    res_ref[...] = take(cells).astype(BF16)


def grid_part(x, qkv, out, up, down, batch=8):
    scratch = [panels(*x.shape), pltpu.VMEM(x.shape, F32)]
    args = (x, qkv, out, up, down)
    kernel = functools.partial(grid_kernel, batch=batch)
    return resident(kernel, [(x.shape, BF16)], args, scratch, 24, 10e9, "grid_part")[0]


def down_expand_kernel(x_ref, w_ref, out_ref, pool_ref, cells, *, block):
    rows, cols, channels = x_ref.shape
    put(cells, x_ref[...].reshape(rows * cols, channels).astype(F32))
    half = block * cols // 2
    for start in range(0, rows, block):
        x = [take_strided(cells, start * cols + parity, half, 2) for parity in range(2)]
        pairs = (x[0] + x[1]).reshape(block // 2, 2, cols // 2, channels)
        pool = 0.25 * (pairs[:, 0] + pairs[:, 1])
        pool_ref[start // 2 : (start + block) // 2] = pool.astype(BF16)
        normed = half_norm(jnp.concatenate(x, 0)).astype(BF16)
        for c in range(0, w_ref.shape[1], 256):
            hidden = gelu_twice(dot(normed, w_ref[:, c : c + 256])).astype(BF16)
            for parity in range(2):
                mine = hidden[parity * half : (parity + 1) * half]
                out_ref[start : start + block, parity, :, c : c + 256] = mine.reshape(
                    block, cols // 2, 256
                )


def down_expand_part(x, weight, block=8):
    rows, cols, channels = x.shape
    hidden = weight.shape[1]
    outs = [((rows, 2, cols // 2, hidden), BF16), ((rows // 2, cols // 2, channels), BF16)]
    work = 4 * rows * cols * channels * hidden
    scratch = [panels(rows * cols, channels)]
    kernel = functools.partial(down_expand_kernel, block=block)
    return resident(kernel, outs, (x, weight), scratch, 8, work, "down_expand")


def down_conv_kernel(
    hid_ref, sec_ref, upper_ref, left_ref, corner_ref, w_ref, taps_ref,
    red_ref, act_ref, part_ref, section_ref, cells, normed, rim, left, sums, sem, *, chunk,
):
    rows, _, cols, width = hid_ref.shape
    steps = width // chunk
    copy = pltpu.make_async_copy(sec_ref, section_ref, sem)
    copy.start()
    row, col = lax.axis_index("row_pair") + lax.axis_index("core"), lax.axis_index(COLS)
    has_upper, has_left = flag(row > 0), flag(col > 0)
    put(cells, half_norm(upper_ref[...].astype(F32)) * has_upper)
    normed[0:32, :] = take_strided(cells, 0, 32, 2).astype(BF16)
    normed[32:64, :] = take_strided(cells, 1, 32, 2).astype(BF16)
    normed[64:80, :] = (half_norm(left_ref[...].astype(F32)) * has_left).astype(BF16)
    corner = half_norm(corner_ref[...].astype(F32)) * (has_upper * has_left)
    normed[80:96, :] = jnp.broadcast_to(corner, (16, corner.shape[1])).astype(BF16)
    rim_of(normed, w_ref[:, :chunk], rim, 0)
    place = lax.broadcasted_iota(jnp.int32, (8, 128), 0)

    def advance(step, carry):
        slot = step % 2
        left[0:1, :] = rim[slot, 80:81, :]
        left[1:17, :] = rim[slot, 64:80, :]
        for lane in range(0, chunk, 128):
            lanes = slice(lane, lane + 128)
            wide = lanes_at(step * chunk + lane)
            taps = [0.5 * taps_ref[t : t + 1, wide].astype(F32) for t in range(9)]
            before = sum(taps[3 * a] * left[a : a + rows, lanes] for a in range(3))
            total = jnp.zeros((8, 128), F32)

            def line(r, parity):
                if r < 0:
                    return rim[slot, 32 * parity : 32 * parity + 32, lanes]
                return hid_ref[r, parity, :, wide].astype(F32)

            for p in range(rows // 2):
                even = [line(2 * p + a - 1, 0) for a in range(3)]
                odd = [line(2 * p + a - 1, 1) for a in range(3)]
                shifted = sum(taps[3 * a] * odd[a] for a in range(3))
                whole = sum(taps[3 * a + 1] * even[a] + taps[3 * a + 2] * odd[a] for a in range(3))
                shifted = pltpu.roll(shifted, 1, 0)
                first = jnp.where(place == 0, before[2 * p : 2 * p + 1], shifted[0:8])
                act = gelu_twice(whole + jnp.concatenate([first, shifted[8:]], 0))
                act_ref[p, :, wide] = act.astype(BF16)
                for s in range(0, cols, 8):
                    total = total + act[s : s + 8]
            sums[:, wide] = total
        later = jnp.minimum(step + 1, steps - 1) * chunk
        rim_of(normed, w_ref[:, lanes_at(later, chunk)], rim, 1 - slot)
        return carry

    lax.fori_loop(0, steps, advance, 0)
    squeeze_sums(sums, red_ref, part_ref)
    copy.wait()


def down_conv(hidden, section, upper, left, corner, weight, taps, reduce, copies, chunk=768):
    rows, _, cols, width = hidden.shape
    channels = weight.shape[0]
    here = pl.BlockSpec(memory_space=pltpu.VMEM)
    args = (hidden, section, upper, left, corner, weight, taps, reduce)
    return pl.pallas_call(
        functools.partial(down_conv_kernel, chunk=chunk),
        in_specs=[here] * len(args),
        out_specs=[here, here, pl.BlockSpec(memory_space=pl.ANY)],
        out_shape=[
            pltpu.VMEM((rows // 2, cols, width), BF16),
            pltpu.VMEM((copies, reduce.shape[0]), F32),
            jax.ShapeDtypeStruct((rows, 2 * cols, channels), BF16),
        ],
        scratch_shapes=[
            panels(64, channels),
            pltpu.VMEM((96, channels), BF16),
            pltpu.VMEM((2, 96, chunk), F32),
            pltpu.VMEM((24, chunk), F32),
            pltpu.VMEM((8, width), F32),
            pltpu.SemaphoreType.DMA,
        ],
        compiler_params=params(8),
        name="down_conv",
    )(*[pltpu.with_memory_space_constraint(a, pltpu.VMEM) for a in args])


def down_out(act, pooled, parts, restore, project, short, cell_count):
    rows, cols, hidden = act.shape
    outs = project.shape[1]
    count = rows * cols // 2

    def kernel(act_ref, pool_ref, parts_ref, restore_ref, project_ref, short_ref, res_ref):
        gate = gate_of(parts_ref, restore_ref, cell_count)
        for i in range(2):
            mine = slice(i * rows // 2, (i + 1) * rows // 2)
            scaled = act_ref[mine].reshape(count, hidden).astype(F32) * gate[0:1, :]
            pool = pool_ref[mine].reshape(count, pool_ref.shape[2])
            y = dot(scaled.astype(BF16), project_ref[...]) + dot(pool, short_ref[...])
            res_ref[mine] = y.astype(BF16).reshape(rows // 2, cols, outs)

    here = pl.BlockSpec(memory_space=pltpu.VMEM)
    args = (act, pooled, parts, restore, project, short)
    return pl.pallas_call(
        kernel,
        in_specs=[here] * len(args),
        out_specs=here,
        out_shape=jax.ShapeDtypeStruct((rows, cols, outs), BF16),
        compiler_params=params(8),
        name="down_out",
    )(*[pltpu.with_memory_space_constraint(a, pltpu.VMEM) for a in args])


def shift(x, axes, by):
    size = lax.axis_size(axes)
    return lax.ppermute(x, axes, [(i, (i + by) % size) for i in range(size)])


def shift_both(x):
    rows, cols = lax.axis_size(ROWS), lax.axis_size(COLS)
    pairs = [
        (r * cols + c, (r + 1) % rows * cols + (c + 1) % cols)
        for r in range(rows)
        for c in range(cols)
    ]
    return lax.ppermute(x, AXES, pairs)


def exchange(x):
    cells, channels = x.shape
    sharers = lax.axis_size(CLASS)
    pieces = x.reshape(sharers, cells // sharers, channels)
    pieces = lax.all_to_all(pieces, CLASS, split_axis=0, concat_axis=0, tiled=True)
    return pieces.reshape(cells, channels)


def sum_parts(part):
    count, squeezed = part.shape
    part = part.reshape(count, 1, squeezed)
    arrived = lax.all_to_all(part, ALL, split_axis=0, concat_axis=0, tiled=True)
    return arrived.reshape(count, squeezed)


def rims_kernel(first_ref, last_ref, left_ref, right_ref, away_ref, near_ref):
    cols = first_ref.shape[0]
    even = (lax.axis_index("core") == 0).astype(jnp.int32)
    cell = lax.broadcasted_iota(jnp.int32, (16, 1), 0)
    left, right = left_ref[...].astype(F32), right_ref[...].astype(F32)

    def corners(r):
        tail = jnp.where(cell == 1, right[r : r + 1], 0.0)
        return jnp.where(cell == 0, left[r : r + 1], tail)

    first = jnp.concatenate([first_ref[...].astype(F32), corners(0)], 0)
    last = jnp.concatenate([last_ref[...].astype(F32), corners(15)], 0)
    turned = jnp.zeros((cols + 16, 1), jnp.int32) + even
    away_ref[...] = jnp.where(turned == 1, first, last).astype(BF16)
    near_ref[...] = jnp.where(turned == 1, last, first).astype(BF16)


def row_rims(first, last, left, right):
    size = lax.axis_size(ROWS)
    cols, channels = first.shape
    outs = [((cols + 16, channels), BF16)] * 2
    away, near = resident(rims_kernel, outs, (first, last, left, right), [], 4, 1e6, "rims")
    pairs = [(r, (r - 1 if r % 2 == 0 else r + 1) % size) for r in range(size)]
    over = lax.ppermute(away, ROWS, pairs)
    pair = lax.ppermute(near, "core", [(0, 1), (1, 0)])
    return over, pair


def local(
    image,
    mb_expand,
    mb_taps,
    mb_reduce,
    mb_restore,
    mb_project,
    block_qkv,
    block_out,
    first_up,
    first_down,
    grid_qkv,
    grid_out,
    second_up,
    second_down,
    down_expand,
    down_taps,
    down_reduce,
    down_restore,
    down_project,
    down_shortcut,
):
    rows, cols, channels = image.shape
    all_cells = rows * cols * lax.axis_size(ALL)

    left = shift(image[:, cols - 1], COLS, 1)
    right = shift(image[:, 0], COLS, -1)
    upper, near_top, first, last, normed, start = expand_upper(image, mb_expand)
    over, pair = row_rims(first, last, left, right)
    act, sums, near_end = conv_inner(upper, normed, start, left, right, mb_expand, mb_taps)
    edges, part = conv_outer(
        (near_top, near_end), over, pair, left, right, mb_expand, mb_taps, mb_reduce.T, sums,
        lax.axis_size(ALL),
    )
    parts = sum_parts(part)
    mixed = block_part(
        image, act, edges, parts, mb_restore, mb_project, block_qkv, block_out, first_up, first_down,
        all_cells,
    )
    mixed = grid_part(exchange(mixed), grid_qkv, grid_out, second_up, second_down)
    section = exchange(mixed).reshape(rows, cols, channels)

    upper = shift(section[rows - 1], ROWS, 1)
    left = shift(section[:, cols - 1], COLS, 1)
    corner = shift_both(section[rows - 1, cols - 1 :])
    hidden, pooled = down_expand_part(section, down_expand)
    act, part, whole = down_conv(
        hidden, section, upper, left, corner, down_expand, down_taps, down_reduce.T,
        lax.axis_size(ALL),
    )
    parts = sum_parts(part)
    downsampled = down_out(
        act, pooled, parts, down_restore, down_project, down_shortcut, all_cells // 4
    )
    return (whole, downsampled)


def solution(mesh):
    rows, cols = mesh.devices.shape
    fine = Mesh(np.asarray(mesh.devices).reshape(rows // 2, 2, cols // 2, 2), AXES)
    tile = P(ROWS, COLS, None)
    in_specs = (tile,) + (P(),) * 19
    return jax.shard_map(
        local, mesh=fine, in_specs=in_specs, out_specs=(tile, tile), check_vma=False
    )
```

```python
import functools
import math

import jax
import jax.numpy as jnp
import numpy as np
from jax import lax
from jax.experimental import pallas as pl
from jax.experimental.pallas import tpu as pltpu
from jax.sharding import Mesh
from jax.sharding import PartitionSpec as P

HEADS = 12
WIN = 8
CELLS = WIN * WIN
QUAD = 4

epsilon = 1e-05
F32 = jnp.float32
BF16 = jnp.bfloat16
ROWS = ("row_pair", "core")
COLS = ("depth", "col_pair")
AXES = ("row_pair", "core", "depth", "col_pair")
ALL = ("core", "row_pair", "col_pair", "depth")
CLASS = ("row_pair", "col_pair", "depth")


def params(megabytes):
    return pltpu.CompilerParams(vmem_limit_bytes=megabytes << 20)


def resident(kernel, outs, args, scratch, megabytes, work, name):
    here = pl.BlockSpec(memory_space=pltpu.VMEM)
    args = [pltpu.with_memory_space_constraint(a, pltpu.VMEM) for a in args]
    return pl.pallas_call(
        kernel,
        in_specs=[here] * len(args),
        out_specs=[here] * len(outs),
        out_shape=[pltpu.VMEM(*out) for out in outs],
        scratch_shapes=scratch,
        compiler_params=params(megabytes),
        cost_estimate=pl.CostEstimate(flops=int(work), bytes_accessed=1 << 20, transcendentals=0),
        name=name,
    )(*args)


def gelu_twice(h):
    inner = h * (1.5957691216057308 + 0.285419265090401 * (h * h))
    return h + h * jnp.tanh(inner)


def layer_norm(x, scale=1.0):
    average = jnp.mean(x, axis=-1, keepdims=True)
    centred = x - average
    spread = jnp.mean(centred * centred, axis=-1, keepdims=True)
    return centred * (scale * lax.rsqrt(spread + epsilon))


def half_norm(x):
    return layer_norm(x, 0.5)


def dot(a, b):
    return jnp.dot(a, b, preferred_element_type=F32)


def exact_dot(a, b, dims):
    total = None
    for _ in range(3):
        term = a.astype(BF16)
        a = a - term.astype(F32)
        product = lax.dot_general(term, b, (dims, ((), ())), preferred_element_type=F32)
        total = product if total is None else total + product
    return total


def panels(rows, channels):
    return pltpu.VMEM((channels // 128, rows, 128), F32)


def put(ref, x):
    for c in range(ref.shape[0]):
        ref[c] = x[:, c * 128 : (c + 1) * 128]


def put_strided(ref, x, start, count, stride):
    for c in range(ref.shape[0]):
        ref[c, pl.ds(start, count, stride=stride), :] = x[:, c * 128 : (c + 1) * 128]


def take(ref):
    return jnp.concatenate([ref[c] for c in range(ref.shape[0])], 1)


def take_strided(ref, start, count, stride):
    return jnp.concatenate(
        [ref[c, pl.ds(start, count, stride=stride), :] for c in range(ref.shape[0])], 1
    )


def expand_upper(image, weight, chunk=256):
    rows, cols, channels = image.shape
    half, hidden = rows // 2, weight.shape[1]

    def kernel(
        x_hbm, w_hbm, up_ref, near_ref, first_ref, last_ref, normed_ref, start_ref,
        x_ref, w_ref, x_sems, w_sem,
    ):
        parts = [slice(0, half), slice(half, rows)]
        x_copies = [
            pltpu.make_async_copy(x_hbm.at[part], x_ref.at[part], x_sems.at[i])
            for i, part in enumerate(parts)
        ]
        w_copy = pltpu.make_async_copy(w_hbm, w_ref, w_sem)
        x_copies[0].start()
        w_copy.start()
        x_copies[1].start()

        def norm(part):
            x = x_ref[part].reshape(half * cols, channels).astype(F32)
            return half_norm(x).astype(BF16)

        def wide(normed, c):
            hidden = gelu_twice(dot(normed, w_ref[:, c : c + chunk])).astype(BF16)
            return hidden.reshape(half, cols, chunk)

        x_copies[0].wait()
        first_ref[...] = x_ref[0]
        normed = norm(parts[0])
        w_copy.wait()
        for c in range(0, hidden, chunk):
            upper = wide(normed, c)
            up_ref[:, :, c : c + chunk] = upper
            near_ref[:, :, c : c + chunk] = upper[0:2]
        x_copies[1].wait()
        last_ref[...] = x_ref[rows - 1]
        normed = norm(parts[1])
        normed_ref[...] = normed
        start_ref[...] = wide(normed, 0)

    away = pl.BlockSpec(memory_space=pl.ANY)
    here = pl.BlockSpec(memory_space=pltpu.VMEM)
    return pl.pallas_call(
        kernel,
        in_specs=[away, away],
        out_specs=[here] * 6,
        out_shape=[
            pltpu.VMEM((half, cols, hidden), BF16),
            pltpu.VMEM((2, cols, hidden), BF16),
            pltpu.VMEM((cols, channels), BF16),
            pltpu.VMEM((cols, channels), BF16),
            pltpu.VMEM((half * cols, channels), BF16),
            pltpu.VMEM((half, cols, chunk), BF16),
        ],
        scratch_shapes=[
            pltpu.VMEM(image.shape, BF16),
            pltpu.VMEM(weight.shape, BF16),
            pltpu.SemaphoreType.DMA((2,)),
            pltpu.SemaphoreType.DMA,
        ],
        compiler_params=params(16),
        cost_estimate=pl.CostEstimate(flops=int(2e9), bytes_accessed=1 << 20, transcendentals=0),
        name="expand_upper",
    )(*[pltpu.with_memory_space_constraint(a, pltpu.HBM) for a in (image, weight)])


def flag(held):
    return jnp.where(held, 1.0, 0.0).astype(F32)


def rim_of(normed, weight, rim, slot):
    rim[slot] = gelu_twice(dot(normed[...], weight)).astype(BF16).astype(F32)


def squeeze_sums(sums, red_ref, part_ref):
    parts = exact_dot(sums[...], red_ref[...], ((1,), (1,)))
    part_ref[...] = jnp.broadcast_to(jnp.sum(parts, axis=0, keepdims=True), part_ref.shape)


def lanes_at(start, size=128):
    return pl.ds(pl.multiple_of(start, 128), size)


def conv_row(lines, short, before, after, place):
    cols = lines[0].shape[0]
    one = [
        (short[b] * lines[0] + short[3 + b] * lines[1] + short[6 + b] * lines[2]).astype(F32)
        for b in range(3)
    ]
    down = pltpu.roll(one[0], 1, 0)
    up = pltpu.roll(one[2], cols - 1, 0)
    first = jnp.where(place == 0, before, down[0:8])
    last = jnp.where(place == 7, after, up[cols - 8 :])
    whole = (
        one[1]
        + jnp.concatenate([first, down[8:]], 0)
        + jnp.concatenate([up[: cols - 8], last], 0)
    )
    act = gelu_twice(whole)
    return act, sum(act[s : s + 8] for s in range(0, cols, 8))


def half_taps(taps_ref, wide):
    taps = [0.5 * taps_ref[t : t + 1, wide].astype(F32) for t in range(9)]
    return taps, [tap.astype(BF16) for tap in taps]


def side_norms(normed, start, left_ref, right_ref):
    col = lax.axis_index(COLS)
    has_left, has_right = flag(col > 0), flag(col < lax.axis_size(COLS) - 1)
    for ref, at, held in ((left_ref, start, has_left), (right_ref, start + 16, has_right)):
        normed[at : at + 16, :] = (half_norm(ref[...].astype(F32)) * held).astype(BF16)
    return has_left, has_right


def inner_kernel(
    up_ref, x_ref, start_ref, left_ref, right_ref, w_ref, taps_ref, act_ref, sums_ref, near_ref,
    low, normed, rim, *, chunk,
):
    rows, cols, width = act_ref.shape
    half = rows // 2
    steps = width // chunk
    side_norms(normed, 0, left_ref, right_ref)
    rim_of(normed, w_ref[:, :chunk], rim, 0)
    low[0] = start_ref[...]
    near_ref[:, :, :chunk] = start_ref[half - 2 : half]

    def expand_lower(step, slot):
        weight = w_ref[:, lanes_at(step * chunk, chunk)]
        wide = gelu_twice(dot(x_ref[...], weight)).astype(BF16).reshape(half, cols, chunk)
        low[slot] = wide
        near_ref[:, :, lanes_at(step * chunk, chunk)] = wide[half - 2 :]
        return weight

    place = lax.broadcasted_iota(jnp.int32, (8, 128), 0)
    inner = rows - 2

    def advance(step, carry):
        slot = step % 2
        for lane in range(0, chunk, 128):
            lanes = slice(lane, lane + 128)
            wide = lanes_at(step * chunk + lane)
            taps, short = half_taps(taps_ref, wide)
            before = sum(taps[3 * a] * rim[slot, a : a + inner, lanes] for a in range(3))
            after = sum(taps[3 * a + 2] * rim[slot, 16 + a : 16 + a + inner, lanes] for a in range(3))
            total = jnp.zeros((8, 128), F32)

            def line(r):
                return up_ref[r, :, wide] if r < half else low[slot, r - half, :, lanes]

            lines = [line(0), line(1), None]
            for r in range(1, rows - 1):
                lines[2] = line(r + 1)
                act, part = conv_row(lines, short, before[r - 1 : r], after[r - 1 : r], place)
                act_ref[r, :, wide] = act.astype(BF16)
                total = total + part
                lines = [lines[1], lines[2], None]
            sums_ref[:, wide] = total
        weight = expand_lower(jnp.minimum(step + 1, steps - 1), 1 - slot)
        rim_of(normed, weight, rim, 1 - slot)
        return carry

    lax.fori_loop(0, steps, advance, 0)


def conv_inner(upper, normed, start, left, right, weight, taps):
    half, cols, width = upper.shape
    channels, chunk = weight.shape[0], start.shape[2]
    outs = [((2 * half, cols, width), BF16), ((8, width), F32), ((2, cols, width), BF16)]
    scratch = [
        pltpu.VMEM((2, half, cols, chunk), BF16),
        pltpu.VMEM((32, channels), BF16),
        pltpu.VMEM((2, 32, chunk), F32),
    ]
    args = (upper, normed, start, left, right, weight, taps)
    kernel = functools.partial(inner_kernel, chunk=chunk)
    return resident(kernel, outs, args, scratch, 16, 8e9, "conv_inner")


def outer_kernel(
    near0_ref, near1_ref, over_ref, pair_ref, left_ref, right_ref, w_ref, taps_ref, red_ref, sums_ref,
    act_ref, part_ref, normed, rim, sums, *, chunk,
):
    _, cols, width = near0_ref.shape
    steps = width // chunk
    row, core = lax.axis_index("row_pair"), lax.axis_index("core")
    has_over = flag(row + core > 0) * flag(row - (1 - core) < lax.axis_size("row_pair") - 1)
    has_left, has_right = side_norms(normed, 160, left_ref, right_ref)
    cell = lax.broadcasted_iota(jnp.int32, (80, 1), 0)
    corners = jnp.where(cell == cols, has_left, jnp.where(cell == cols + 1, has_right, 1.0))
    for ref, start, held in ((over_ref, 0, corners * has_over), (pair_ref, 80, corners)):
        normed[start : start + 80, :] = (half_norm(ref[...].astype(F32)) * held).astype(BF16)
    rim_of(normed, w_ref[:, :chunk], rim, 0)
    top, bottom = core * 80, (1 - core) * 80
    place = lax.broadcasted_iota(jnp.int32, (8, 128), 0)

    def advance(step, carry):
        slot = step % 2
        for lane in range(0, chunk, 128):
            lanes = slice(lane, lane + 128)
            wide = lanes_at(step * chunk + lane)
            taps, short = half_taps(taps_ref, wide)

            def cells(at, side):
                return rim[slot, pl.ds(pl.multiple_of(at, 8), 8), lanes][side : side + 1]

            def line(at):
                return rim[slot, pl.ds(pl.multiple_of(at, 8), 64), lanes].astype(BF16)

            total = sums_ref[:, wide]
            near = [ref[r, :, wide] for ref in (near0_ref, near1_ref) for r in range(2)]
            edges = (
                ([line(top), near[0], near[1]], (top, 0), (160, 161)),
                ([near[2], near[3], line(bottom)], (bottom, 2), (174, 175)),
            )
            for i, (lines, (corner, turn), (one, two)) in enumerate(edges):
                beside = [[], []]
                for side in range(2):
                    beside[side].append(cells(corner + 64, side))
                    for at in (one, two):
                        beside[side].append(rim[slot, at + 16 * side : at + 16 * side + 1, lanes])
                before, after = [
                    sum(taps[3 * ((a + turn) % 3) + 2 * side] * beside[side][a] for a in range(3))
                    for side in range(2)
                ]
                act, part = conv_row(lines, short, before, after, place)
                act_ref[i, :, wide] = act.astype(BF16)
                total = total + part
            sums[:, wide] = total
        later = jnp.minimum(step + 1, steps - 1) * chunk
        rim_of(normed, w_ref[:, lanes_at(later, chunk)], rim, 1 - slot)
        return carry

    lax.fori_loop(0, steps, advance, 0)
    squeeze_sums(sums, red_ref, part_ref)


def conv_outer(near, over, pair, left, right, weight, taps, reduce, sums, copies, chunk=768):
    _, cols, width = near[0].shape
    channels = weight.shape[0]
    outs = [((2, cols, width), BF16), ((copies, reduce.shape[0]), F32)]
    scratch = [
        pltpu.VMEM((192, channels), BF16),
        pltpu.VMEM((2, 192, chunk), F32),
        pltpu.VMEM((8, width), F32),
    ]
    args = (*near, over, pair, left, right, weight, taps, reduce, sums)
    kernel = functools.partial(outer_kernel, chunk=chunk)
    return resident(kernel, outs, args, scratch, 16, 2e9, "conv_outer")


def gate_of(parts_ref, restore_ref, cell_count):
    average = jnp.sum(parts_ref[...], axis=0, keepdims=True) / cell_count
    squeezed = average * jax.nn.sigmoid(average)
    squeezed = jnp.broadcast_to(squeezed, (8, squeezed.shape[1]))
    return jax.nn.sigmoid(exact_dot(squeezed, restore_ref[...], ((1,), (0,))))


def attend(x, qkv_ref, out_ref):
    cells, channels = x.shape
    width = channels // HEADS
    normed = layer_norm(x).astype(BF16)
    projected = dot(normed, qkv_ref[...])
    queries = (projected[:, :channels] * (1.0 / math.sqrt(width))).astype(BF16)
    keys = projected[:, channels : 2 * channels].astype(BF16)
    values = projected[:, 2 * channels :].astype(BF16)
    lane = lax.broadcasted_iota(jnp.int32, (1, 128), 1)
    masks = [((lane >= h * width) & (lane < (h + 1) * width)).astype(BF16) for h in range(QUAD)]
    groups = []
    for g in range(0, cells, CELLS):
        mine = slice(g, g + CELLS)
        quads = []
        for c in range(0, channels, 128):
            lanes = slice(c, c + 128)
            q, k, v = queries[mine, lanes], keys[mine, lanes], values[mine, lanes]
            stacked = jnp.concatenate([q * m for m in masks], 0)
            scores = lax.dot_general(
                k, stacked, (((1,), (1,)), ((), ())), preferred_element_type=F32
            )
            weights = jnp.exp(scores - jnp.max(scores, axis=0, keepdims=True))
            shares = weights * (1.0 / jnp.sum(weights, axis=0, keepdims=True))
            blended = lax.dot_general(
                shares.astype(BF16), v, (((0,), (0,)), ((), ())), preferred_element_type=F32
            )
            picked = blended[3 * CELLS :]
            for h in (2, 1, 0):
                picked = jnp.where(
                    lane < (h + 1) * width, blended[h * CELLS : (h + 1) * CELLS], picked
                )
            quads.append(picked)
        groups.append(jnp.concatenate(quads, 1).astype(BF16))
    return x + dot(jnp.concatenate(groups, 0), out_ref[...])


def feed(x, up_ref, down_ref):
    normed = half_norm(x).astype(BF16)
    hidden = [
        gelu_twice(dot(normed, up_ref[:, c : c + 256])).astype(BF16)
        for c in range(0, up_ref.shape[1], 256)
    ]
    return x + dot(jnp.concatenate(hidden, 1), down_ref[...])


def block_kernel(
    img_ref, act_ref, edge_ref, parts_ref, restore_ref, project_ref, qkv_ref, out_ref, up_ref,
    down_ref, res_ref, middle, *, cell_count,
):
    rows, cols, channels = img_ref.shape
    cells = WIN * cols
    wide = cols // WIN
    gate = gate_of(parts_ref, restore_ref, cell_count)
    acts = [
        jnp.concatenate([edge_ref[0:1], act_ref[1:WIN]], 0),
        jnp.concatenate([act_ref[WIN : rows - 1], edge_ref[1:2]], 0),
    ]
    for strip, act in enumerate(acts):
        mine = slice(strip * WIN, (strip + 1) * WIN)
        scaled = act.reshape(cells, act.shape[2]).astype(F32) * gate[0:1, :]
        x = img_ref[mine].reshape(cells, channels).astype(F32)
        x = x + dot(scaled.astype(BF16), project_ref[...])
        pieces = [
            x[r * cols + g * WIN : r * cols + (g + 1) * WIN]
            for g in range(wide)
            for r in range(WIN)
        ]
        y = attend(jnp.concatenate(pieces, 0), qkv_ref, out_ref)
        pieces = [
            y[g * CELLS + r * WIN : g * CELLS + (r + 1) * WIN]
            for r in range(WIN)
            for g in range(wide)
        ]
        middle[strip * cells : (strip + 1) * cells, :] = jnp.concatenate(pieces, 0)
    res_ref[...] = feed(middle[...], up_ref, down_ref).astype(BF16)


def block_part(image, act, edges, parts, restore, project, qkv, out, up, down, cell_count):
    rows, cols, channels = image.shape
    outs = [((rows * cols, channels), BF16)]
    args = (image, act, edges, parts, restore, project, qkv, out, up, down)
    scratch = [pltpu.VMEM((rows * cols, channels), F32)]
    kernel = functools.partial(block_kernel, cell_count=cell_count)
    return resident(kernel, outs, args, scratch, 24, 12e9, "block_part")[0]


def grid_kernel(x_ref, qkv_ref, out_ref, up_ref, down_ref, res_ref, cells, middle, *, batch):
    groups = x_ref.shape[0] // CELLS
    put(cells, x_ref[...].astype(F32))
    for start in range(0, groups, batch):
        x = [take_strided(cells, start + g, CELLS, groups) for g in range(batch)]
        y = attend(jnp.concatenate(x, 0), qkv_ref, out_ref)
        middle[start * CELLS : (start + batch) * CELLS, :] = y
    y = feed(middle[...], up_ref, down_ref)
    for g in range(groups):
        put_strided(cells, y[g * CELLS : (g + 1) * CELLS], g, CELLS, groups)
    res_ref[...] = take(cells).astype(BF16)


def grid_part(x, qkv, out, up, down, batch=8):
    scratch = [panels(*x.shape), pltpu.VMEM(x.shape, F32)]
    args = (x, qkv, out, up, down)
    kernel = functools.partial(grid_kernel, batch=batch)
    return resident(kernel, [(x.shape, BF16)], args, scratch, 24, 10e9, "grid_part")[0]


def down_expand_kernel(x_ref, w_ref, out_ref, pool_ref, cells, *, block):
    rows, cols, channels = x_ref.shape
    put(cells, x_ref[...].reshape(rows * cols, channels).astype(F32))
    half = block * cols // 2
    for start in range(0, rows, block):
        x = [take_strided(cells, start * cols + parity, half, 2) for parity in range(2)]
        pairs = (x[0] + x[1]).reshape(block // 2, 2, cols // 2, channels)
        pool = 0.25 * (pairs[:, 0] + pairs[:, 1])
        pool_ref[start // 2 : (start + block) // 2] = pool.astype(BF16)
        normed = half_norm(jnp.concatenate(x, 0)).astype(BF16)
        for c in range(0, w_ref.shape[1], 256):
            hidden = gelu_twice(dot(normed, w_ref[:, c : c + 256])).astype(BF16)
            for parity in range(2):
                mine = hidden[parity * half : (parity + 1) * half]
                out_ref[start : start + block, parity, :, c : c + 256] = mine.reshape(
                    block, cols // 2, 256
                )


def down_expand_part(x, weight, block=8):
    rows, cols, channels = x.shape
    hidden = weight.shape[1]
    outs = [((rows, 2, cols // 2, hidden), BF16), ((rows // 2, cols // 2, channels), BF16)]
    work = 4 * rows * cols * channels * hidden
    scratch = [panels(rows * cols, channels)]
    kernel = functools.partial(down_expand_kernel, block=block)
    return resident(kernel, outs, (x, weight), scratch, 8, work, "down_expand")


def down_conv_kernel(
    hid_ref, sec_ref, upper_ref, left_ref, corner_ref, w_ref, taps_ref,
    red_ref, act_ref, part_ref, section_ref, cells, normed, rim, left, sums, sem, *, chunk,
):
    rows, _, cols, width = hid_ref.shape
    steps = width // chunk
    copy = pltpu.make_async_copy(sec_ref, section_ref, sem)
    copy.start()
    row, col = lax.axis_index("row_pair") + lax.axis_index("core"), lax.axis_index(COLS)
    has_upper, has_left = flag(row > 0), flag(col > 0)
    put(cells, half_norm(upper_ref[...].astype(F32)) * has_upper)
    normed[0:32, :] = take_strided(cells, 0, 32, 2).astype(BF16)
    normed[32:64, :] = take_strided(cells, 1, 32, 2).astype(BF16)
    normed[64:80, :] = (half_norm(left_ref[...].astype(F32)) * has_left).astype(BF16)
    corner = half_norm(corner_ref[corner_ref.shape[0] - 16 :].astype(F32)[15:16]) * (has_upper * has_left)
    normed[80:96, :] = jnp.broadcast_to(corner, (16, corner.shape[1])).astype(BF16)
    rim_of(normed, w_ref[:, :chunk], rim, 0)
    place = lax.broadcasted_iota(jnp.int32, (8, 128), 0)

    def advance(step, carry):
        slot = step % 2
        left[0:1, :] = rim[slot, 80:81, :]
        left[1:17, :] = rim[slot, 64:80, :]
        for lane in range(0, chunk, 128):
            lanes = slice(lane, lane + 128)
            wide = lanes_at(step * chunk + lane)
            taps = [0.5 * taps_ref[t : t + 1, wide].astype(F32) for t in range(9)]
            before = sum(taps[3 * a] * left[a : a + rows, lanes] for a in range(3))
            total = jnp.zeros((8, 128), F32)

            def line(r, parity):
                if r < 0:
                    return rim[slot, 32 * parity : 32 * parity + 32, lanes]
                return hid_ref[r, parity, :, wide].astype(F32)

            for p in range(rows // 2):
                even = [line(2 * p + a - 1, 0) for a in range(3)]
                odd = [line(2 * p + a - 1, 1) for a in range(3)]
                shifted = sum(taps[3 * a] * odd[a] for a in range(3))
                whole = sum(taps[3 * a + 1] * even[a] + taps[3 * a + 2] * odd[a] for a in range(3))
                shifted = pltpu.roll(shifted, 1, 0)
                first = jnp.where(place == 0, before[2 * p : 2 * p + 1], shifted[0:8])
                act = gelu_twice(whole + jnp.concatenate([first, shifted[8:]], 0))
                act_ref[p, :, wide] = act.astype(BF16)
                for s in range(0, cols, 8):
                    total = total + act[s : s + 8]
            sums[:, wide] = total
        later = jnp.minimum(step + 1, steps - 1) * chunk
        rim_of(normed, w_ref[:, lanes_at(later, chunk)], rim, 1 - slot)
        return carry

    lax.fori_loop(0, steps, advance, 0)
    squeeze_sums(sums, red_ref, part_ref)
    copy.wait()


def down_conv(hidden, section, upper, left, corner, weight, taps, reduce, copies, chunk=768):
    rows, _, cols, width = hidden.shape
    channels = weight.shape[0]
    here = pl.BlockSpec(memory_space=pltpu.VMEM)
    args = (hidden, section, upper, left, corner, weight, taps, reduce)
    return pl.pallas_call(
        functools.partial(down_conv_kernel, chunk=chunk),
        in_specs=[here] * len(args),
        out_specs=[here, here, pl.BlockSpec(memory_space=pl.ANY)],
        out_shape=[
            pltpu.VMEM((rows // 2, cols, width), BF16),
            pltpu.VMEM((copies, reduce.shape[0]), F32),
            jax.ShapeDtypeStruct((rows, 2 * cols, channels), BF16),
        ],
        scratch_shapes=[
            panels(64, channels),
            pltpu.VMEM((96, channels), BF16),
            pltpu.VMEM((2, 96, chunk), F32),
            pltpu.VMEM((24, chunk), F32),
            pltpu.VMEM((8, width), F32),
            pltpu.SemaphoreType.DMA,
        ],
        compiler_params=params(8),
        name="down_conv",
    )(*[pltpu.with_memory_space_constraint(a, pltpu.VMEM) for a in args])


def down_out(act, pooled, parts, restore, project, short, cell_count):
    rows, cols, hidden = act.shape
    outs = project.shape[1]
    count = rows * cols // 2

    def kernel(act_ref, pool_ref, parts_ref, restore_ref, project_ref, short_ref, res_ref):
        gate = gate_of(parts_ref, restore_ref, cell_count)
        for i in range(2):
            mine = slice(i * rows // 2, (i + 1) * rows // 2)
            scaled = act_ref[mine].reshape(count, hidden).astype(F32) * gate[0:1, :]
            pool = pool_ref[mine].reshape(count, pool_ref.shape[2])
            y = dot(scaled.astype(BF16), project_ref[...]) + dot(pool, short_ref[...])
            res_ref[mine] = y.astype(BF16).reshape(rows // 2, cols, outs)

    here = pl.BlockSpec(memory_space=pltpu.VMEM)
    args = (act, pooled, parts, restore, project, short)
    return pl.pallas_call(
        kernel,
        in_specs=[here] * len(args),
        out_specs=here,
        out_shape=jax.ShapeDtypeStruct((rows, cols, outs), BF16),
        compiler_params=params(8),
        name="down_out",
    )(*[pltpu.with_memory_space_constraint(a, pltpu.VMEM) for a in args])


def shift(x, axes, by):
    size = lax.axis_size(axes)
    return lax.ppermute(x, axes, [(i, (i + by) % size) for i in range(size)])


def shift_both(x):
    rows, cols = lax.axis_size(ROWS), lax.axis_size(COLS)
    pairs = [
        (r * cols + c, (r + 1) % rows * cols + (c + 1) % cols)
        for r in range(rows)
        for c in range(cols)
    ]
    return lax.ppermute(x, AXES, pairs)


def exchange(x):
    cells, channels = x.shape
    sharers = lax.axis_size(CLASS)
    pieces = x.reshape(sharers, cells // sharers, channels)
    pieces = lax.all_to_all(pieces, CLASS, split_axis=0, concat_axis=0, tiled=True)
    return pieces.reshape(cells, channels)


def sum_parts(part):
    count, squeezed = part.shape
    part = part.reshape(count, 1, squeezed)
    arrived = lax.all_to_all(part, ALL, split_axis=0, concat_axis=0, tiled=True)
    return arrived.reshape(count, squeezed)


def rims_kernel(first_ref, last_ref, left_ref, right_ref, away_ref, near_ref):
    cols = first_ref.shape[0]
    even = (lax.axis_index("core") == 0).astype(jnp.int32)
    cell = lax.broadcasted_iota(jnp.int32, (16, 1), 0)
    left, right = left_ref[...].astype(F32), right_ref[...].astype(F32)

    def corners(r):
        tail = jnp.where(cell == 1, right[r : r + 1], 0.0)
        return jnp.where(cell == 0, left[r : r + 1], tail)

    first = jnp.concatenate([first_ref[...].astype(F32), corners(0)], 0)
    last = jnp.concatenate([last_ref[...].astype(F32), corners(15)], 0)
    turned = jnp.zeros((cols + 16, 1), jnp.int32) + even
    away_ref[...] = jnp.where(turned == 1, first, last).astype(BF16)
    near_ref[...] = jnp.where(turned == 1, last, first).astype(BF16)


def row_rims(first, last, left, right):
    size = lax.axis_size(ROWS)
    cols, channels = first.shape
    outs = [((cols + 16, channels), BF16)] * 2
    away, near = resident(rims_kernel, outs, (first, last, left, right), [], 4, 1e6, "rims")
    pairs = [(r, (r - 1 if r % 2 == 0 else r + 1) % size) for r in range(size)]
    over = lax.ppermute(away, ROWS, pairs)
    pair = lax.ppermute(near, "core", [(0, 1), (1, 0)])
    return over, pair


def local(
    image,
    mb_expand,
    mb_taps,
    mb_reduce,
    mb_restore,
    mb_project,
    block_qkv,
    block_out,
    first_up,
    first_down,
    grid_qkv,
    grid_out,
    second_up,
    second_down,
    down_expand,
    down_taps,
    down_reduce,
    down_restore,
    down_project,
    down_shortcut,
):
    rows, cols, channels = image.shape
    all_cells = rows * cols * lax.axis_size(ALL)

    left = shift(image[:, cols - 1], COLS, 1)
    right = shift(image[:, 0], COLS, -1)
    upper, near_top, first, last, normed, start = expand_upper(image, mb_expand)
    over, pair = row_rims(first, last, left, right)
    act, sums, near_end = conv_inner(upper, normed, start, left, right, mb_expand, mb_taps)
    edges, part = conv_outer(
        (near_top, near_end), over, pair, left, right, mb_expand, mb_taps, mb_reduce.T, sums,
        lax.axis_size(ALL),
    )
    parts = sum_parts(part)
    mixed = block_part(
        image, act, edges, parts, mb_restore, mb_project, block_qkv, block_out, first_up, first_down,
        all_cells,
    )
    mixed = grid_part(exchange(mixed), grid_qkv, grid_out, second_up, second_down)
    section = exchange(mixed).reshape(rows, cols, channels)

    upper = shift(section[rows - 1], ROWS, 1)
    left = shift(section[:, cols - 1], COLS, 1)
    corner = shift_both(section[rows - 2 :].reshape(2 * cols, channels))
    hidden, pooled = down_expand_part(section, down_expand)
    act, part, whole = down_conv(
        hidden, section, upper, left, corner, down_expand, down_taps, down_reduce.T,
        lax.axis_size(ALL),
    )
    parts = sum_parts(part)
    downsampled = down_out(
        act, pooled, parts, down_restore, down_project, down_shortcut, all_cells // 4
    )
    return (whole, downsampled)


def solution(mesh):
    rows, cols = mesh.devices.shape
    fine = Mesh(np.asarray(mesh.devices).reshape(rows // 2, 2, cols // 2, 2), AXES)
    tile = P(ROWS, COLS, None)
    in_specs = (tile,) + (P(),) * 19
    return jax.shard_map(
        local, mesh=fine, in_specs=in_specs, out_specs=(tile, tile), check_vma=False
    )
```
